32 devices in a mesh: dp: 16 (over z, y, core), tensor: 2 (over x).
Axes of the slice: x: 2, y: 2, z: 4, core: 2. Of those that a mesh axis runs over, the one named last changes fastest.
Arguments:
- passages: bfloat16 [16384, 768], P('dp'), may hold values from -6 to 6
- corrupted: bfloat16 [16384, 768], P('dp'), may hold values from -6 to 6
- lengths: int32 [16, 8], P('dp'), may hold values from 0 to 512, as said below
- cotangent: bfloat16 [16384, 768], P('dp'), may hold values from -6 to 6
- encoder_query: bfloat16 [768, 768], P(None, 'tensor'), may hold values from -0.21875 to 0.21875
- encoder_key: bfloat16 [768, 768], P(None, 'tensor'), may hold values from -0.21875 to 0.21875
- encoder_value: bfloat16 [768, 768], P(None, 'tensor'), may hold values from -0.21875 to 0.21875
- encoder_project: bfloat16 [768, 768], P(None, 'tensor'), may hold values from -0.875 to 0.875
- encoder_query_bias: float32 [768], P('tensor'), may hold values from -3 to 3
- encoder_value_bias: float32 [768], P('tensor'), may hold values from -3 to 3
- encoder_project_bias: float32 [768], replicated, may hold values from -3 to 3
- encoder_first_gain: float32 [768], replicated, may hold values from 0.5 to 1.5
- encoder_first_shift: float32 [768], replicated, may hold values from -3 to 3
- encoder_inner: bfloat16 [768, 3072], P(None, 'tensor'), may hold values from -0.21875 to 0.21875
- encoder_inner_bias: float32 [3072], P('tensor'), may hold values from -3 to 3
- encoder_outer: bfloat16 [768, 3072], P(None, 'tensor'), may hold values from -0.109375 to 0.109375
- encoder_outer_bias: float32 [768], replicated, may hold values from -3 to 3
- encoder_second_gain: float32 [768], replicated, may hold values from 0.5 to 1.5
- encoder_second_shift: float32 [768], replicated, may hold values from -3 to 3
- decoder_query: bfloat16 [768, 768], P(None, 'tensor'), may hold values from -0.21875 to 0.21875
- decoder_key: bfloat16 [768, 768], P(None, 'tensor'), may hold values from -0.21875 to 0.21875
- decoder_value: bfloat16 [768, 768], P(None, 'tensor'), may hold values from -0.21875 to 0.21875
- decoder_project: bfloat16 [768, 768], P(None, 'tensor'), may hold values from -0.875 to 0.875
- decoder_query_bias: float32 [768], P('tensor'), may hold values from -3 to 3
- decoder_value_bias: float32 [768], P('tensor'), may hold values from -3 to 3
- decoder_project_bias: float32 [768], replicated, may hold values from -3 to 3
- decoder_first_gain: float32 [768], replicated, may hold values from 0.5 to 1.5
- decoder_first_shift: float32 [768], replicated, may hold values from -3 to 3
- decoder_inner: bfloat16 [768, 3072], P(None, 'tensor'), may hold values from -0.21875 to 0.21875
- decoder_inner_bias: float32 [3072], P('tensor'), may hold values from -3 to 3
- decoder_outer: bfloat16 [768, 3072], P(None, 'tensor'), may hold values from -0.109375 to 0.109375
- decoder_outer_bias: float32 [768], replicated, may hold values from -3 to 3
- decoder_second_gain: float32 [768], replicated, may hold values from 0.5 to 1.5
- decoder_second_shift: float32 [768], replicated, may hold values from -3 to 3
Outputs:
- decoded: bfloat16 [16384, 768], P('dp')
- delta_passages: float32 [16384, 768], P('dp')
- delta_corrupted: float32 [16384, 768], P('dp')
- delta_encoder_query: float32 [768, 768], P('dp', 'tensor')
- delta_encoder_key: float32 [768, 768], P('dp', 'tensor')
- delta_encoder_value: float32 [768, 768], P('dp', 'tensor')
- delta_encoder_project: float32 [768, 768], P('dp', 'tensor')
- delta_encoder_query_bias: float32 [768], P('tensor')
- delta_encoder_value_bias: float32 [768], P('tensor')
- delta_encoder_project_bias: float32 [768], replicated
- delta_encoder_first_gain: float32 [768], replicated
- delta_encoder_first_shift: float32 [768], replicated
- delta_encoder_inner: float32 [768, 3072], P('dp', 'tensor')
- delta_encoder_inner_bias: float32 [3072], P('tensor')
- delta_encoder_outer: float32 [768, 3072], P('dp', 'tensor')
- delta_encoder_outer_bias: float32 [768], replicated
- delta_encoder_second_gain: float32 [768], replicated
- delta_encoder_second_shift: float32 [768], replicated
- delta_decoder_query: float32 [768, 768], P('dp', 'tensor')
- delta_decoder_key: float32 [768, 768], P('dp', 'tensor')
- delta_decoder_value: float32 [768, 768], P('dp', 'tensor')
- delta_decoder_project: float32 [768, 768], P('dp', 'tensor')
- delta_decoder_query_bias: float32 [768], P('tensor')
- delta_decoder_value_bias: float32 [768], P('tensor')
- delta_decoder_project_bias: float32 [768], replicated
- delta_decoder_first_gain: float32 [768], replicated
- delta_decoder_first_shift: float32 [768], replicated
- delta_decoder_inner: float32 [768, 3072], P('dp', 'tensor')
- delta_decoder_inner_bias: float32 [3072], P('tensor')
- delta_decoder_outer: float32 [768, 3072], P('dp', 'tensor')
- delta_decoder_outer_bias: float32 [768], replicated
- delta_decoder_second_gain: float32 [768], replicated
- delta_decoder_second_shift: float32 [768], replicated
The draws below stay inside these ranges and needn't reach their ends.
Inputs may be any that keep to these rules, and one draw needn't show every extreme that they name: Row i holds, in order, the lengths of the passages packed one after another from slot 0 into the 1024 slots of index i; a row sums to at most 1024; zero marks an unused passage slot; some row holds a passage of 512 tokens.
All inputs are finite; a program needn't handle non-finite values.
Results may differ from the reference program's by a relative error of at most 0.04.
Values may be sent and summed in bfloat16 or wider, within the bound.
No kernel may reach another device: no remote copies, remote signals or barrier semaphores. Data moves between devices by JAX's collectives and lax.ppermute only.
A program may use at most 256 MiB of HBM per device.

```python
import jax
import jax.numpy as jnp
from jax import lax

D = 768
FF = 3072
HEAD_SIZE = 64
TOK_DEV = 1024
PASS = 8
LONGEST = 512
TOKENS = 16384
N_DP = 16
N_TENSOR = 2


def draw_lengths(key, part):
    key = jax.random.fold_in(key, 11)
    keys = jax.random.split(key, 6)
    short_top = TOK_DEV // PASS
    long_top = (TOK_DEV - LONGEST) // (PASS - 1)
    short_len = jax.random.randint(keys[0], (N_DP, PASS), short_top // 2, short_top + 1)
    rest_len = jax.random.randint(keys[1], (N_DP, PASS), long_top // 2, long_top + 1)
    live_count = jax.random.randint(keys[2], (N_DP, 1), PASS // 2 + 1, PASS + 1)
    long_slot = jax.random.randint(keys[3], (N_DP, 1), 0, PASS // 2 + 1)
    holder = jax.random.randint(keys[4], (), 0, N_DP)
    lucky = jax.random.randint(keys[5], (N_DP, 1), 0, 4) == 0
    indices = jnp.arange(N_DP, dtype=jnp.int32)[:, None]
    holds_long = lucky | (indices == holder)
    slots = jnp.arange(PASS, dtype=jnp.int32)[None, :]
    with_long = jnp.where(slots == long_slot, LONGEST, rest_len)
    chosen = jnp.where(holds_long, with_long, short_len)
    return jnp.where(slots < live_count, chosen, 0).astype(jnp.int32)


def block_levels(rng, extent, shards, smallest, high):
    loudness, own = 1.0, jax.random.fold_in(rng, 6)
    for dim, parts in shards:
        steps = jnp.exp(jax.random.uniform(jax.random.fold_in(own, dim), (parts,), jnp.float32, smallest / len(shards), high / len(shards)))
        loudness = loudness * jnp.repeat(steps, extent[dim] // parts).reshape([-1 if axis == dim else 1 for axis in range(len(extent))])
    return loudness


def scatter_about(key, dims, scale, limit, shards=(), kind=jnp.bfloat16):
    drawn = jax.random.normal(key, dims, jnp.float32) * scale
    if len(shards) > 0:
        drawn = block_levels(key, dims, shards, -0.22, 0.18) * drawn
    return jnp.clip(drawn, min=-limit, max=limit).astype(kind)


def setup_inputs(seed: int = 0) -> dict:
    seeds = jax.random.split(jax.random.key(seed), 35)
    return {
        "passages": scatter_about(seeds[0], (TOKENS, D), 1.0, 6.0, ((0, 16),)),
        "corrupted": scatter_about(seeds[1], (TOKENS, D), 1.0, 6.0, ((0, 16),)),
        "lengths": draw_lengths(jax.random.fold_in(seeds[34], 71), 0),
        "cotangent": scatter_about(seeds[3], (TOKENS, D), 1.0, 6.0, ((0, 16),)),
        "encoder_query": scatter_about(seeds[4], (D, D), D ** -0.5, 0.21875, ((1, 2),)),
        "encoder_key": scatter_about(seeds[5], (D, D), D ** -0.5, 0.21875, ((1, 2),)),
        "encoder_value": scatter_about(seeds[6], (D, D), D ** -0.5, 0.21875, ((1, 2),)),
        "encoder_project": scatter_about(seeds[7], (D, D), (D // 16) ** -0.5, 0.875, ((1, 2),)),
        "encoder_query_bias": scatter_about(seeds[8], (D,), 0.5, 3.0, ((0, 2),), jnp.float32),
        "encoder_value_bias": scatter_about(seeds[9], (D,), 0.5, 3.0, ((0, 2),), jnp.float32),
        "encoder_project_bias": scatter_about(seeds[10], (D,), 0.5, 3.0, (), jnp.float32),
        "encoder_first_gain": jnp.clip(1.0 + 0.1 * jax.random.normal(seeds[11], (D,), jnp.float32), 0.5, 1.5),
        "encoder_first_shift": scatter_about(seeds[12], (D,), 0.3, 3.0, (), jnp.float32),
        "encoder_inner": scatter_about(seeds[13], (D, FF), D ** -0.5, 0.21875, ((1, 2),)),
        "encoder_inner_bias": scatter_about(seeds[14], (FF,), 0.5, 3.0, ((0, 2),), jnp.float32),
        "encoder_outer": scatter_about(seeds[15], (D, FF), FF ** -0.5, 0.109375, ((1, 2),)),
        "encoder_outer_bias": scatter_about(seeds[16], (D,), 0.5, 3.0, (), jnp.float32),
        "encoder_second_gain": jnp.clip(1.0 + 0.1 * jax.random.normal(seeds[17], (D,), jnp.float32), 0.5, 1.5),
        "encoder_second_shift": scatter_about(seeds[18], (D,), 0.3, 3.0, (), jnp.float32),
        "decoder_query": scatter_about(seeds[19], (D, D), D ** -0.5, 0.21875, ((1, 2),)),
        "decoder_key": scatter_about(seeds[20], (D, D), D ** -0.5, 0.21875, ((1, 2),)),
        "decoder_value": scatter_about(seeds[21], (D, D), D ** -0.5, 0.21875, ((1, 2),)),
        "decoder_project": scatter_about(seeds[22], (D, D), (D // 16) ** -0.5, 0.875, ((1, 2),)),
        "decoder_query_bias": scatter_about(seeds[23], (D,), 0.5, 3.0, ((0, 2),), jnp.float32),
        "decoder_value_bias": scatter_about(seeds[24], (D,), 0.5, 3.0, ((0, 2),), jnp.float32),
        "decoder_project_bias": scatter_about(seeds[25], (D,), 0.5, 3.0, (), jnp.float32),
        "decoder_first_gain": jnp.clip(1.0 + 0.1 * jax.random.normal(seeds[26], (D,), jnp.float32), 0.5, 1.5),
        "decoder_first_shift": scatter_about(seeds[27], (D,), 0.3, 3.0, (), jnp.float32),
        "decoder_inner": scatter_about(seeds[28], (D, FF), D ** -0.5, 0.21875, ((1, 2),)),
        "decoder_inner_bias": scatter_about(seeds[29], (FF,), 0.5, 3.0, ((0, 2),), jnp.float32),
        "decoder_outer": scatter_about(seeds[30], (D, FF), FF ** -0.5, 0.109375, ((1, 2),)),
        "decoder_outer_bias": scatter_about(seeds[31], (D,), 0.5, 3.0, (), jnp.float32),
        "decoder_second_gain": jnp.clip(1.0 + 0.1 * jax.random.normal(seeds[32], (D,), jnp.float32), 0.5, 1.5),
        "decoder_second_shift": scatter_about(seeds[33], (D,), 0.3, 3.0, (), jnp.float32),
    }


@jax.custom_vjp
def low(v):
    return lax.optimization_barrier(v.astype(jnp.bfloat16)).astype(jnp.float32)

@jax.custom_vjp
def low_back(v):
    return v

def low_keep(v):
    return (low(v), None)

def low_pass(kept, grad):
    return (grad,)

def back_keep(v):
    return (v, None)

def back_low(kept, grad):
    return (low(grad),)
low.defvjp(low_keep, low_pass)
low_back.defvjp(back_keep, back_low)
HIGHEST = lax.Precision.HIGHEST
EPSILON = 1e-06

def product(left, right):
    return jnp.dot(left, right, precision=HIGHEST, preferred_element_type=jnp.float32)

def norm_rows(summed, scales, shifts):
    center = lax.optimization_barrier(jnp.mean(summed, axis=-1, keepdims=True))
    offset = summed - center
    spread = lax.optimization_barrier(jnp.mean(offset * offset, axis=-1, keepdims=True))
    return offset * lax.rsqrt(spread + EPSILON) * scales + shifts

def layout(lengths_row, rows):
    ends = jnp.cumsum(lengths_row).astype(jnp.int32)
    places = jnp.arange(rows, dtype=jnp.int32)
    passed = places[:, None] >= ends[None, :]
    segment = lax.optimization_barrier(jnp.sum(passed.astype(jnp.int32), axis=1)).astype(jnp.int32)
    start = lax.optimization_barrier(jnp.sum(jnp.where(passed, lengths_row[None, :], 0), axis=1)).astype(jnp.int32)
    valid = places < ends[-1]
    return (segment, start, valid)

def attend(query_rows, key_rows, value_rows, same):
    rows, width = query_rows.shape
    heads = width // HEAD_SIZE
    block = min(rows, 512)
    count = rows // block
    key_heads = key_rows.reshape(rows, heads, HEAD_SIZE)
    value_heads = value_rows.reshape(rows, heads, HEAD_SIZE)

    def one(pieces):
        query_part, mask_part = pieces
        query_heads = query_part.reshape(block, heads, HEAD_SIZE)
        score = jnp.einsum('qhd,khd->hqk', query_heads, key_heads, precision=HIGHEST)
        score = low_back(score) * 0.125
        score = jnp.where(mask_part[None], score, -1e+30)
        top = lax.optimization_barrier(jnp.max(score, axis=2, keepdims=True))
        expo = jnp.exp(score - top)
        weights = expo / lax.optimization_barrier(jnp.sum(expo, axis=2, keepdims=True))
        mixed = jnp.einsum('hqk,khd->qhd', low(weights), value_heads, precision=HIGHEST)
        return mixed.reshape(block, width)
    mixed = lax.map(jax.checkpoint(one), (query_rows.reshape(count, block, width), same.reshape(count, block, rows)))
    return mixed.reshape(rows, width)

def block_layer(layer_in, weights, same):
    query_weight, key_weight, value_weight, project_weight, query_bias, value_bias, project_bias, first_gain, first_shift, inner_weight, inner_bias, outer_weight, outer_bias, second_gain, second_shift = weights
    part = query_weight.shape[1] // N_TENSOR
    hidden_part = inner_weight.shape[1] // N_TENSOR
    attended = jnp.zeros_like(layer_in)
    for group in range(N_TENSOR):
        cols = slice(group * part, (group + 1) * part)
        shared = low(low_back(layer_in))
        query_rows = low(low_back(product(shared, query_weight[:, cols]) + query_bias[cols]))
        key_rows = low(low_back(product(shared, key_weight[:, cols])))
        value_rows = low(low_back(product(shared, value_weight[:, cols]) + value_bias[cols]))
        mixed = low(low_back(attend(query_rows, key_rows, value_rows, same)))
        attended = attended + low(product(mixed, project_weight[:, cols].T))
    attended = low_back(attended)
    first_rows = norm_rows(layer_in + attended + project_bias, first_gain, first_shift)
    fed = jnp.zeros_like(layer_in)
    for group in range(N_TENSOR):
        cols = slice(group * hidden_part, (group + 1) * hidden_part)
        shared = low(low_back(first_rows))
        hidden_pre = low_back(product(shared, inner_weight[:, cols]) + inner_bias[cols])
        hidden_act = low(jax.nn.gelu(hidden_pre, approximate=False))
        fed = fed + low(product(hidden_act, outer_weight[:, cols].T))
    fed = low_back(fed)
    return norm_rows(first_rows + fed + outer_bias, second_gain, second_shift)

def forward_one(passage_rows, corrupt_rows, encoder_weights, decoder_weights, lengths_row):
    rows = passage_rows.shape[0]
    segment, start, valid = layout(lengths_row, rows)
    same = segment[:, None] == segment[None, :]
    encoded = block_layer(passage_rows, encoder_weights, same)
    decoder_input = corrupt_rows + jnp.take(encoded, start, axis=0)
    decoded = block_layer(decoder_input, decoder_weights, same)
    return decoded * valid[:, None].astype(decoded.dtype)

def reference(passages, corrupted, lengths, cotangent, encoder_query, encoder_key, encoder_value, encoder_project, encoder_query_bias, encoder_value_bias, encoder_project_bias, encoder_first_gain, encoder_first_shift, encoder_inner, encoder_inner_bias, encoder_outer, encoder_outer_bias, encoder_second_gain, encoder_second_shift, decoder_query, decoder_key, decoder_value, decoder_project, decoder_query_bias, decoder_value_bias, decoder_project_bias, decoder_first_gain, decoder_first_shift, decoder_inner, decoder_inner_bias, decoder_outer, decoder_outer_bias, decoder_second_gain, decoder_second_shift):
    encoder_weights = tuple((w.astype(jnp.float32) for w in (encoder_query, encoder_key, encoder_value, encoder_project, encoder_query_bias, encoder_value_bias, encoder_project_bias, encoder_first_gain, encoder_first_shift, encoder_inner, encoder_inner_bias, encoder_outer, encoder_outer_bias, encoder_second_gain, encoder_second_shift)))
    decoder_weights = tuple((w.astype(jnp.float32) for w in (decoder_query, decoder_key, decoder_value, decoder_project, decoder_query_bias, decoder_value_bias, decoder_project_bias, decoder_first_gain, decoder_first_shift, decoder_inner, decoder_inner_bias, decoder_outer, decoder_outer_bias, decoder_second_gain, decoder_second_shift)))
    width = passages.shape[1]
    passage_blocks = passages.astype(jnp.float32).reshape(N_DP, TOK_DEV, width)
    corrupt_blocks = corrupted.astype(jnp.float32).reshape(N_DP, TOK_DEV, width)
    cotangent_blocks = cotangent.astype(jnp.float32).reshape(N_DP, TOK_DEV, width)

    def step(totals, pieces):
        passage_rows, corrupt_rows, cotangent_rows, lengths_row = pieces

        def run(passage_in, corrupt_in, encoder_in, decoder_in):
            return forward_one(passage_in, corrupt_in, encoder_in, decoder_in, lengths_row)
        result, pull = jax.vjp(run, passage_rows, corrupt_rows, encoder_weights, decoder_weights)
        passage_grad, corrupt_grad, encoder_grad, decoder_grad = pull(cotangent_rows)
        totals = jax.tree.map(jnp.add, totals, (encoder_grad, decoder_grad))
        return (totals, (result.astype(jnp.bfloat16), passage_grad, corrupt_grad))
    zeros = jax.tree.map(jnp.zeros_like, (encoder_weights, decoder_weights))
    totals, outputs = lax.scan(step, zeros, (passage_blocks, corrupt_blocks, cotangent_blocks, lengths))
    encoder_grads, decoder_grads = totals
    decoded = outputs[0].reshape(N_DP * TOK_DEV, width)
    passage_delta = outputs[1].reshape(N_DP * TOK_DEV, width)
    corrupt_delta = outputs[2].reshape(N_DP * TOK_DEV, width)
    return (decoded, passage_delta, corrupt_delta, encoder_grads[0], encoder_grads[1], encoder_grads[2], encoder_grads[3], encoder_grads[4], encoder_grads[5], encoder_grads[6], encoder_grads[7], encoder_grads[8], encoder_grads[9], encoder_grads[10], encoder_grads[11], encoder_grads[12], encoder_grads[13], encoder_grads[14], decoder_grads[0], decoder_grads[1], decoder_grads[2], decoder_grads[3], decoder_grads[4], decoder_grads[5], decoder_grads[6], decoder_grads[7], decoder_grads[8], decoder_grads[9], decoder_grads[10], decoder_grads[11], decoder_grads[12], decoder_grads[13], decoder_grads[14])
```

```python
import functools

import jax
import jax.numpy as jnp
from jax import lax
from jax.experimental import pallas as pl
from jax.experimental.pallas import tpu as pltpu
from jax.sharding import PartitionSpec as P

HEAD_SIZE = 64
EPSILON = 1e-06
NEGATIVE = -1e30
TILE = 128
AXES = ("dp", "tensor")
VMEM_LIMIT = 56 * 1024 * 1024
F32 = jnp.float32
LOW = jnp.bfloat16


def dot(left, right, contract):
    return lax.dot_general(left, right, ((contract[0:1], contract[1:2]), ((), ())), preferred_element_type=F32)


def window_sizes(tiles):
    sizes = [2, 3, 4, 6, tiles]
    return sorted({min(s, tiles) for s in sizes})


def for_window(first, last, tiles, body):
    need = last - first
    below = 0
    for size in window_sizes(tiles):
        @pl.when((need > below) & (need <= size))
        def _(size=size):
            body(size, jnp.minimum(first, tiles - size))
        below = size


def attend_kernel(tile_lo, tile_hi, bounds_ref, q_ref, k_ref, v_ref, o_ref, lse_ref):
    rows, width = q_ref.shape
    tiles = rows // TILE
    lane = lax.broadcasted_iota(jnp.int32, (1, TILE), 1)
    first_head = lane < HEAD_SIZE

    def step(j, carry):
        def body(size, begin):
            span = size * TILE
            here = pl.ds(pl.multiple_of(j * TILE, TILE), TILE)
            keys = pl.ds(pl.multiple_of(begin * TILE, TILE), span)
            place = begin * TILE + lax.broadcasted_iota(jnp.int32, (TILE, span), 1)
            inside = (place >= bounds_ref[here, 0:1]) & (place < bounds_ref[here, 1:2])
            for pair in range(width // TILE):
                cols = pl.ds(pair * TILE, TILE)
                queries = q_ref[here, cols] * jnp.asarray(0.125, LOW)
                pair_keys = k_ref[keys, cols]
                pair_values = v_ref[keys, cols]
                mixed = []
                for half in range(2):
                    mine = first_head if half == 0 else jnp.logical_not(first_head)
                    score = dot(jnp.where(mine, queries, jnp.zeros_like(queries)), pair_keys, (1, 1))
                    score = jnp.where(inside, score, NEGATIVE)
                    top = jnp.max(score, axis=1, keepdims=True)
                    expo = jnp.exp(score - top)
                    total = jnp.sum(expo, axis=1, keepdims=True)
                    mixed.append(dot(expo.astype(LOW), pair_values, (1, 0)) / total)
                    head = 2 * pair + half
                    lse_ref[here, head : head + 1] = top + jnp.log(total)
                o_ref[here, cols] = jnp.where(first_head, mixed[0], mixed[1]).astype(LOW)

        for_window(tile_lo[j], tile_hi[j], tiles, body)
        return carry

    lax.fori_loop(0, tiles, step, 0)


def attend(tile_lo, tile_hi, bounds, query, key, value):
    rows, width = query.shape
    heads = width // HEAD_SIZE
    smem = pl.BlockSpec(memory_space=pltpu.SMEM)
    vmem = pl.BlockSpec(memory_space=pltpu.VMEM)
    return pl.pallas_call(
        attend_kernel,
        out_shape=(jax.ShapeDtypeStruct((rows, width), LOW), jax.ShapeDtypeStruct((rows, heads), F32)),
        in_specs=[smem, smem] + [vmem] * 4,
        out_specs=(vmem, vmem),
        compiler_params=pltpu.CompilerParams(vmem_limit_bytes=VMEM_LIMIT),
        cost_estimate=pl.CostEstimate(flops=8 * rows * 512 * width, bytes_accessed=8 * rows * width, transcendentals=rows * 512 * heads),
        name="attend",
    )(tile_lo, tile_hi, bounds, query, key, value)


def attend_back_kernel(
    tile_lo, tile_hi, bounds_ref, lse_ref, q_ref, k_ref, v_ref, g_ref, dq_ref, dk_ref, dv_ref, kt_ref, dk_sum, dv_sum
):
    rows, width = q_ref.shape
    tiles = rows // TILE
    pairs = width // TILE
    lane = lax.broadcasted_iota(jnp.int32, (1, TILE), 1)
    first_head = lane < HEAD_SIZE
    dk_sum[...] = jnp.zeros_like(dk_sum)
    dv_sum[...] = jnp.zeros_like(dv_sum)

    def turn(j, carry):
        here = pl.ds(pl.multiple_of(j * TILE, TILE), TILE)
        for pair in range(pairs):
            cols = pl.ds(pair * TILE, TILE)
            kt_ref[cols, here] = jnp.transpose(k_ref[here, cols].astype(F32)).astype(LOW)
        return carry

    lax.fori_loop(0, tiles, turn, 0)

    def step(j, carry):
        def body(size, begin):
            span = size * TILE
            here = pl.ds(pl.multiple_of(j * TILE, TILE), TILE)
            keys = pl.ds(pl.multiple_of(begin * TILE, TILE), span)
            place = begin * TILE + lax.broadcasted_iota(jnp.int32, (span, TILE), 0)
            inside = (place >= bounds_ref[0:1, here]) & (place < bounds_ref[1:2, here])
            for pair in range(pairs):
                cols = pl.ds(pair * TILE, TILE)
                queries = q_ref[here, cols] * jnp.asarray(0.125, LOW)
                grads = g_ref[here, cols]
                pair_keys = k_ref[keys, cols]
                pair_values = v_ref[keys, cols]
                weights, score_grads, own_q, own_g = [], [], [], []
                for half in range(2):
                    head = 2 * pair + half
                    mine = first_head if half == 0 else jnp.logical_not(first_head)
                    head_q = jnp.where(mine, queries, jnp.zeros_like(queries))
                    head_g = jnp.where(mine, grads, jnp.zeros_like(grads))
                    score = dot(pair_keys, head_q, (1, 1))
                    weight = jnp.exp(jnp.where(inside, score, NEGATIVE) - lse_ref[head : head + 1, here])
                    weight_grad = dot(pair_values, head_g, (1, 1))
                    middle = jnp.sum(weight * weight_grad, axis=0, keepdims=True)
                    score_grad = (weight * (weight_grad - middle)).astype(LOW)
                    turned = kt_ref[pl.ds(head * HEAD_SIZE, HEAD_SIZE), keys]
                    dq_ref[pl.ds(head * HEAD_SIZE, HEAD_SIZE), here] = (
                        dot(turned, score_grad, (1, 0)) * 0.125
                    ).astype(LOW)
                    weights.append(weight.astype(LOW))
                    score_grads.append(score_grad)
                    own_q.append(head_q)
                    own_g.append(head_g)
                dk_sum[keys, cols] += dot(
                    jnp.concatenate(score_grads, axis=1), jnp.concatenate(own_q, axis=0), (1, 0)
                )
                dv_sum[keys, cols] += dot(jnp.concatenate(weights, axis=1), jnp.concatenate(own_g, axis=0), (1, 0))

        for_window(tile_lo[j], tile_hi[j], tiles, body)
        return carry

    lax.fori_loop(0, tiles, step, 0)
    dk_ref[...] = dk_sum[...].astype(LOW)
    dv_ref[...] = dv_sum[...].astype(LOW)


def attend_back(tile_lo, tile_hi, bounds_t, lse_t, query, key, value, grad):
    rows, width = query.shape
    heads = width // HEAD_SIZE
    smem = pl.BlockSpec(memory_space=pltpu.SMEM)
    vmem = pl.BlockSpec(memory_space=pltpu.VMEM)
    return pl.pallas_call(
        attend_back_kernel,
        out_shape=(
            jax.ShapeDtypeStruct((width, rows), LOW),
            jax.ShapeDtypeStruct((rows, width), LOW),
            jax.ShapeDtypeStruct((rows, width), LOW),
        ),
        in_specs=[smem, smem] + [vmem] * 6,
        out_specs=(vmem, vmem, vmem),
        scratch_shapes=[
            pltpu.VMEM((width, rows), LOW),
            pltpu.VMEM((rows, width), F32),
            pltpu.VMEM((rows, width), F32),
        ],
        compiler_params=pltpu.CompilerParams(vmem_limit_bytes=VMEM_LIMIT),
        cost_estimate=pl.CostEstimate(flops=20 * rows * 512 * width, bytes_accessed=14 * rows * width, transcendentals=rows * 512 * heads),
        name="attend_back",
    )(tile_lo, tile_hi, bounds_t, lse_t, query, key, value, grad)


def gelu_and_slope(pre):
    phi_sum = 0.5 + 0.5 * lax.erf(pre * 0.7071067811865476)
    density = jnp.exp(-0.5 * pre * pre) * 0.3989422804014327
    return pre * phi_sum, phi_sum + pre * density


def feed_kernel(y_ref, inner_ref, bias_ref, outer_ref, act_ref, slope_ref, out_ref, pre_ref, total_ref):
    rows = y_ref.shape[0]
    step = pl.program_id(0)
    pre_ref[...] = dot(y_ref[...], inner_ref[...], (1, 0))
    chunk = 64

    def part(i, carry):
        here = pl.ds(pl.multiple_of(i * chunk, chunk), chunk)
        act, slope = gelu_and_slope(pre_ref[here, :] + bias_ref[...])
        act_ref[here, :] = act.astype(LOW)
        slope_ref[here, :] = slope.astype(LOW)
        return carry

    lax.fori_loop(0, rows // chunk, part, 0)
    fed = dot(act_ref[...], outer_ref[...], (1, 1))

    @pl.when(step == 0)
    def _():
        total_ref[...] = fed

    @pl.when(step > 0)
    def _():
        total_ref[...] += fed

    @pl.when(step == pl.num_programs(0) - 1)
    def _():
        out_ref[...] = total_ref[...].astype(LOW)


def feed(y_low, inner, inner_bias, outer):
    rows, width = y_low.shape
    hidden = inner.shape[1]
    block = 256
    column = lambda height: pl.BlockSpec((height, block), lambda j: (0, j))
    whole = pl.BlockSpec((rows, width), lambda j: (0, 0))
    return pl.pallas_call(
        feed_kernel,
        grid=(hidden // block,),
        out_shape=(
            jax.ShapeDtypeStruct((rows, hidden), LOW),
            jax.ShapeDtypeStruct((rows, hidden), LOW),
            jax.ShapeDtypeStruct((rows, width), LOW),
        ),
        in_specs=[whole, column(width), column(1), column(width)],
        out_specs=(column(rows), column(rows), whole),
        scratch_shapes=[pltpu.VMEM((rows, block), F32), pltpu.VMEM((rows, width), F32)],
        compiler_params=pltpu.CompilerParams(vmem_limit_bytes=VMEM_LIMIT),
        cost_estimate=pl.CostEstimate(flops=4 * rows * width * hidden, bytes_accessed=14 * 1024 * 1024, transcendentals=2 * rows * hidden),
        name="feed",
    )(y_low, inner, inner_bias.reshape(1, hidden), outer)


def feed_back_kernel(g_ref, outer_ref, slope_ref, inner_ref, pre_grad_ref, bias_grad_ref, out_ref, total_ref):
    step = pl.program_id(0)
    grad = dot(g_ref[...], outer_ref[...], (1, 0)) * slope_ref[...].astype(F32)
    pre_grad = grad.astype(LOW)
    pre_grad_ref[...] = pre_grad
    bias_grad_ref[...] = jnp.sum(pre_grad.astype(F32), axis=0, keepdims=True)
    back = dot(pre_grad_ref[...], inner_ref[...], (1, 1))

    @pl.when(step == 0)
    def _():
        total_ref[...] = back

    @pl.when(step > 0)
    def _():
        total_ref[...] += back

    @pl.when(step == pl.num_programs(0) - 1)
    def _():
        out_ref[...] = total_ref[...].astype(LOW)


def feed_back(fed_low, outer, slope, inner):
    rows, width = fed_low.shape
    hidden = inner.shape[1]
    block = 256
    column = lambda height: pl.BlockSpec((height, block), lambda j: (0, j))
    whole = pl.BlockSpec((rows, width), lambda j: (0, 0))
    return pl.pallas_call(
        feed_back_kernel,
        grid=(hidden // block,),
        out_shape=(
            jax.ShapeDtypeStruct((rows, hidden), LOW),
            jax.ShapeDtypeStruct((1, hidden), F32),
            jax.ShapeDtypeStruct((rows, width), LOW),
        ),
        in_specs=[whole, column(width), column(rows), column(width)],
        out_specs=(column(rows), column(1), whole),
        scratch_shapes=[pltpu.VMEM((rows, width), F32)],
        compiler_params=pltpu.CompilerParams(vmem_limit_bytes=VMEM_LIMIT),
        cost_estimate=pl.CostEstimate(flops=4 * rows * width * hidden, bytes_accessed=14 * 1024 * 1024, transcendentals=0),
        name="feed_back",
    )(fed_low, outer, slope, inner)


def norm(summed):
    center = jnp.mean(summed, axis=-1, keepdims=True)
    offset = summed - center
    scale = lax.rsqrt(jnp.mean(offset * offset, axis=-1, keepdims=True) + EPSILON)
    return offset * scale, scale


def norm_back(grad, unit, scale, gain):
    scaled = grad * gain
    return scale * (
        scaled - jnp.mean(scaled, axis=-1, keepdims=True) - unit * jnp.mean(scaled * unit, axis=-1, keepdims=True)
    )


def column_sum(values):
    return jnp.sum(values, axis=0)


class Links:
    def __init__(self, mesh):
        self.dp = mesh.shape["dp"]
        self.parts = mesh.shape["tensor"]
        self.bits = (self.dp // 2).bit_length() - 1
        self.core = lax.axis_index("dp") & 1
        self.group = lax.axis_index("dp") >> 1
        self.chip = lax.axis_index("tensor")
        self.home = self.core == self.chip

    def move(self, value, target):
        pairs = []
        for i in range(self.dp):
            for t in range(self.parts):
                to_i, to_t = target(i, t)
                pairs.append((i * self.parts + t, to_i * self.parts + to_t))
        return lax.ppermute(value, AXES, pairs)

    def swap_core(self, value):
        return self.move(value, lambda i, t: (i ^ 1, t))

    def swap_tensor(self, value):
        return self.move(value, lambda i, t: (i, t ^ 1))

    def swap_group(self, value, bit):
        return self.move(value, lambda i, t: (i ^ (2 << bit), t))

    def turn(self, value):
        return self.move(value, lambda i, t: (i, t) if (i & 1) == t else (i ^ 1, t ^ 1))

    def of_chip(self, value):
        return jnp.where(self.home, value, self.swap_core(value))

    def pick(self, value, axis, bit):
        return lax.dynamic_slice_in_dim(value, bit, 1, axis)

    def scatter_half(self, grad, order):
        height, width = grad.shape
        view = grad.reshape((2,) * self.bits + (2, height // self.dp, width))
        for step in order:
            if step < 0:
                axis, mine = self.bits, self.chip
                sent = self.swap_tensor(self.pick(view, axis, 1 - mine).astype(LOW))
            else:
                axis, mine = self.bits - 1 - step, (self.group >> step) & 1
                sent = self.swap_group(self.pick(view, axis, 1 - mine).astype(LOW), step)
            view = self.pick(view, axis, mine).astype(F32) + sent.astype(F32)
        block = view.reshape(height // self.dp, width)
        return self.turn(block)

    def sum_all(self, value, over_core):
        for bit in range(self.bits):
            value = value + self.swap_group(value, bit)
        if over_core:
            return value + self.swap_core(value)
        return value + self.swap_tensor(value)

    def exchange(self, value, step):
        return self.swap_core(value) if step == 0 else self.swap_group(value, step - 1)

    def gather_rows(self, value):
        for step in range(self.bits + 1):
            value = jnp.concatenate([value, self.exchange(value, step)], axis=0)
        return value

    def gather_block(self, value):
        rows, model = value.shape
        deep = model // self.dp
        view = value.T.reshape((2,) * (self.bits + 1) + (deep, 1, rows))
        for step in range(self.bits + 1):
            mine = (lax.axis_index("dp") >> step) & 1
            axis = self.bits - step
            sent = self.exchange(self.pick(view, axis, 1 - mine), step)
            view = jnp.concatenate([self.pick(view, axis, mine), sent], axis=-2)
        return view.reshape(deep, self.dp, rows)


def split_low(values):
    first = values.astype(LOW)
    rest = values - first.astype(F32)
    second = rest.astype(LOW)
    third = (rest - second.astype(F32)).astype(LOW)
    return first, second, third


def layout(lengths_row, rows):
    ends = jnp.cumsum(lengths_row)
    places = jnp.arange(rows, dtype=jnp.int32)
    passed = places[:, None] >= ends[None, :]
    segment = jnp.sum(passed.astype(jnp.int32), axis=1)
    start = jnp.sum(jnp.where(passed, lengths_row[None, :], 0), axis=1)
    valid = places < ends[-1]
    return (segment, start, valid, ends)


def local(mesh, passages, corrupted, lengths, cotangent, *weights):
    (
        e_query, e_key, e_value, e_project, e_query_bias, e_value_bias, e_project_bias, e_first_gain, e_first_shift,
        e_inner, e_inner_bias, e_outer, e_outer_bias, e_second_gain, e_second_shift,
    ) = weights[:15]
    (
        d_query, d_key, d_value, d_project, d_query_bias, d_value_bias, d_project_bias, d_first_gain, d_first_shift,
        d_inner, d_inner_bias, d_outer, d_outer_bias, d_second_gain, d_second_shift,
    ) = weights[15:]
    links = Links(mesh)
    rows, model = passages.shape
    part = e_query.shape[1]
    hidden = e_inner.shape[1]
    heads = part // HEAD_SIZE
    slots = lengths.shape[1]
    kept = -(-(slots + 1) // 16) * 16

    d_query = links.turn(d_query)
    d_key = links.turn(d_key)
    d_value = links.turn(d_value)
    d_halves = links.turn(jnp.concatenate([d_query_bias, d_value_bias, d_inner_bias]))
    d_query_bias, d_value_bias, d_inner_bias = d_halves[:part], d_halves[part : 2 * part], d_halves[2 * part :]
    d_project = links.turn(d_project)
    d_inner = links.turn(d_inner)
    d_outer = links.turn(d_outer)

    lengths_own = lengths[0]
    segment, start, valid, ends = layout(lengths_own, rows)
    firsts = jnp.concatenate([ends - lengths_own, ends[-1:]])
    firsts = jnp.concatenate([firsts, jnp.broadcast_to(firsts[-1:], (kept - slots - 1,))])
    firsts = jnp.minimum(firsts, rows - 1)
    marks = jnp.arange(kept, dtype=jnp.int32)
    same = marks[:, None] == segment[None, :]

    picked = (jnp.arange(rows, dtype=jnp.int32)[None, :] == firsts[:, None]).astype(LOW)
    x_low = dot(picked, passages, (1, 0)).astype(LOW)
    x_rows = x_low.astype(F32)
    e_q = (dot(x_low, e_query, (1, 0)) + e_query_bias).astype(LOW)
    q_heads = e_q.reshape(kept, heads, HEAD_SIZE)
    key_heads = e_key.reshape(model, heads, HEAD_SIZE)
    value_heads = e_value.reshape(model, heads, HEAD_SIZE)
    bias_heads = e_value_bias.reshape(heads, HEAD_SIZE)
    q_keys = jnp.einsum("phd,mhd->hpm", q_heads, key_heads, preferred_element_type=F32).astype(LOW)
    score = jnp.einsum("hpm,sm->hps", q_keys, passages, preferred_element_type=F32) * 0.125
    score = jnp.where(same[None], score, NEGATIVE)
    expo = jnp.exp(score - jnp.max(score, axis=2, keepdims=True))
    e_weights = expo / jnp.sum(expo, axis=2, keepdims=True)
    e_weights_low = e_weights.astype(LOW)
    weight_sum = jnp.sum(e_weights_low.astype(F32), axis=2)
    weight_x = jnp.einsum("hps,sm->hpm", e_weights_low, passages, preferred_element_type=F32).astype(LOW)
    e_mixed = jnp.einsum("hpm,mhd->phd", weight_x, value_heads, preferred_element_type=F32)
    e_mixed = e_mixed + weight_sum.T[:, :, None] * bias_heads[None]
    e_mixed = e_mixed.reshape(kept, part).astype(LOW)
    share = dot(e_mixed, e_project, (1, 1)).astype(LOW)
    e_attended = share.astype(F32) + links.swap_tensor(share).astype(F32)
    e_unit1, e_scale1 = norm(x_rows + e_attended + e_project_bias)
    e_first = e_unit1 * e_first_gain + e_first_shift
    e_first_low = e_first.astype(LOW)
    e_pre = dot(e_first_low, e_inner, (1, 0)) + e_inner_bias
    e_act, e_slope = gelu_and_slope(e_pre)
    e_act = e_act.astype(LOW)
    share = dot(e_act, e_outer, (1, 1)).astype(LOW)
    e_fed = share.astype(F32) + links.swap_tensor(share).astype(F32)
    e_unit2, e_scale2 = norm(e_first + e_fed + e_outer_bias)
    encoded = e_unit2 * e_second_gain + e_second_shift

    weight_x_rows = weight_x.reshape(heads * kept, model)
    left_forward = links.gather_block(jnp.concatenate([x_low, e_first_low, weight_x_rows], axis=0))
    right_forward = links.gather_rows(jnp.concatenate([e_act, e_mixed, e_q], axis=1))

    lengths_row = links.of_chip(lengths)[0]
    encoded = links.of_chip(encoded)
    corrupt = links.of_chip(corrupted)
    cot = links.of_chip(cotangent)
    c_segment, c_start, c_valid, c_ends = layout(lengths_row, rows)
    valid_rows = c_valid.astype(F32)[:, None]
    member = (c_segment[:, None] == marks[None, :]).astype(LOW)
    c_finish = jnp.sum(
        jnp.where(c_segment[:, None] == jnp.arange(slots + 1)[None, :], jnp.concatenate([c_ends, jnp.full((1,), rows, c_ends.dtype)])[None, :], 0),
        axis=1,
    )
    bounds = jnp.stack([c_start, c_finish], axis=1).astype(jnp.int32)
    tile_lo = c_start[::TILE] // TILE
    tile_hi = -(-c_finish[TILE - 1 :: TILE] // TILE)

    d_in = corrupt.astype(F32) + sum(dot(member, piece, (1, 0)) for piece in split_low(encoded))
    d_low = d_in.astype(LOW)
    query = (dot(d_low, d_query, (1, 0)) + d_query_bias).astype(LOW)
    key = dot(d_low, d_key, (1, 0)).astype(LOW)
    value = (dot(d_low, d_value, (1, 0)) + d_value_bias).astype(LOW)
    mixed, lse = attend(tile_lo, tile_hi, bounds, query, key, value)
    share = dot(mixed, d_project, (1, 1)).astype(LOW)
    attended = share.astype(F32) + links.swap_core(share).astype(F32)
    unit1, scale1 = norm(d_in + attended + d_project_bias)
    first = unit1 * d_first_gain + d_first_shift
    first_low = first.astype(LOW)
    act, slope, share = feed(first_low, d_inner, d_inner_bias, d_outer)
    fed = share.astype(F32) + links.swap_core(share).astype(F32)
    unit2, scale2 = norm(first + fed + d_outer_bias)
    decoded = ((unit2 * d_second_gain + d_second_shift) * valid_rows).astype(LOW)
    decoded = links.turn(decoded)

    grad_out = cot.astype(F32) * valid_rows
    second_gain_grad = column_sum(grad_out * unit2)
    second_shift_grad = column_sum(grad_out)
    second_grad = norm_back(grad_out, unit2, scale2, d_second_gain)
    outer_bias_grad = column_sum(second_grad)
    fed_low = second_grad.astype(LOW)
    pre_grad, inner_bias_grad, share = feed_back(fed_low, d_outer, slope, d_inner)
    back = share.astype(F32) + links.swap_core(share).astype(F32)
    outer_grad = dot(fed_low, act, (0, 0)).astype(LOW)
    inner_grad = dot(first_low, pre_grad, (0, 0)).astype(LOW)
    first_rows_grad = second_grad + back
    first_gain_grad = column_sum(first_rows_grad * unit1)
    first_shift_grad = column_sum(first_rows_grad)
    first_grad = norm_back(first_rows_grad, unit1, scale1, d_first_gain)
    project_bias_grad = column_sum(first_grad)
    attended_low = first_grad.astype(LOW)
    project_grad = dot(attended_low, mixed, (0, 0)).astype(LOW)
    mixed_grad = dot(attended_low, d_project, (1, 0)).astype(LOW)
    query_t, key_low, value_low = attend_back(tile_lo, tile_hi, bounds.T, lse.T, query, key, value, mixed_grad)
    query_bias_grad = jnp.sum(query_t.astype(F32), axis=1)
    value_bias_grad = column_sum(value_low.astype(F32))
    share = dot(query_t, d_query, (0, 1)) + dot(key_low, d_key, (1, 1)) + dot(value_low, d_value, (1, 1))
    share = share.astype(LOW)
    d_in_grad = first_grad + (share.astype(F32) + links.swap_core(share).astype(F32))
    query_grad = dot(d_low, query_t, (0, 1)).astype(LOW)
    key_grad = dot(d_low, key_low, (0, 0)).astype(LOW)
    value_grad = dot(d_low, value_low, (0, 0)).astype(LOW)
    corrupted_grad = links.turn(d_in_grad.astype(LOW)).astype(F32)

    across = list(range(links.bits))
    tensor_first = [-1] + across
    group_first = across[:1] + [-1] + across[1:]
    group_early = across[1:2] + across[:1] + [-1] + across[2:]
    d_outer_grad = links.scatter_half(outer_grad, tensor_first)
    d_inner_grad = links.scatter_half(inner_grad, group_first)
    d_project_grad = links.scatter_half(project_grad, group_early)
    d_query_grad = links.scatter_half(query_grad, tensor_first)
    d_key_grad = links.scatter_half(key_grad, group_first)
    d_value_grad = links.scatter_half(value_grad, group_early)
    vectors = jnp.concatenate([
        query_bias_grad, value_bias_grad, inner_bias_grad[0], project_bias_grad, first_gain_grad, first_shift_grad,
        outer_bias_grad, second_gain_grad, second_shift_grad,
    ])
    vectors = links.sum_all(vectors, False)
    halves = links.of_chip(vectors[: 2 * part + hidden])
    d_vectors = [halves[:part], halves[part : 2 * part], halves[2 * part :]]
    d_vectors += [vectors[2 * part + hidden + i * model : 2 * part + hidden + (i + 1) * model] for i in range(6)]

    totals = sum(dot(member, piece, (0, 0)) for piece in split_low(d_in_grad))
    totals = links.turn(totals)
    e_second_gain_grad = column_sum(totals * e_unit2)
    e_second_shift_grad = column_sum(totals)
    e_second_grad = norm_back(totals, e_unit2, e_scale2, e_second_gain)
    e_outer_bias_grad = column_sum(e_second_grad)
    e_fed_low = e_second_grad.astype(LOW)
    e_pre_grad = (dot(e_fed_low, e_outer, (1, 0)) * e_slope).astype(LOW)
    e_inner_bias_grad = column_sum(e_pre_grad.astype(F32))
    share = dot(e_pre_grad, e_inner, (1, 1)).astype(LOW)
    e_first_rows_grad = e_second_grad + (share.astype(F32) + links.swap_tensor(share).astype(F32))
    e_first_gain_grad = column_sum(e_first_rows_grad * e_unit1)
    e_first_shift_grad = column_sum(e_first_rows_grad)
    e_first_grad = norm_back(e_first_rows_grad, e_unit1, e_scale1, e_first_gain)
    e_project_bias_grad = column_sum(e_first_grad)
    e_attended_low = e_first_grad.astype(LOW)
    e_mixed_grad = dot(e_attended_low, e_project, (1, 0)).astype(LOW)
    g_heads = e_mixed_grad.reshape(kept, heads, HEAD_SIZE)
    g_values = jnp.einsum("phd,mhd->hpm", g_heads, value_heads, preferred_element_type=F32).astype(LOW)
    g_bias = jnp.einsum("phd,hd->hp", g_heads.astype(F32), bias_heads)
    weight_grad = jnp.einsum("hpm,sm->hps", g_values, passages, preferred_element_type=F32) + g_bias[:, :, None]
    middle = jnp.sum(e_weights * weight_grad, axis=2, keepdims=True)
    score_grad = (e_weights * (weight_grad - middle)).astype(LOW)
    score_x = jnp.einsum("hps,sm->hpm", score_grad, passages, preferred_element_type=F32).astype(LOW)
    e_q_grad = (jnp.einsum("hpm,mhd->phd", score_x, key_heads, preferred_element_type=F32) * 0.125).astype(LOW)
    e_q_grad = e_q_grad.reshape(kept, part)
    e_query_bias_grad = column_sum(e_q_grad.astype(F32))
    e_value_bias_grad = jnp.einsum("hp,phd->hd", weight_sum, g_heads.astype(F32)).reshape(part)
    q_back = dot(e_q_grad, e_query, (1, 1)).astype(LOW)
    coefs = jnp.concatenate([score_grad, e_weights_low], axis=0)
    coefs = jnp.sum(jnp.where(same[None], coefs, jnp.zeros_like(coefs)).astype(F32), axis=1).astype(LOW)
    carried = jnp.concatenate([(q_keys * jnp.asarray(0.125, LOW)), g_values], axis=0).reshape(2 * heads * kept, model)

    def spread(values):
        values = jnp.where(same[None], values[:, None, :], jnp.zeros((), LOW))
        return values.reshape(2 * heads * kept, rows)

    coefs_far = spread(links.swap_tensor(coefs))
    carried_far = links.swap_tensor(carried)
    coefs = spread(coefs)
    q_back = q_back.astype(F32) + links.swap_tensor(q_back).astype(F32)
    picked_grad = e_first_grad + q_back
    place = (picked.astype(F32) * jnp.any(same, axis=1)[:, None]).astype(LOW)
    near = dot(coefs, carried, (0, 0))
    far = dot(coefs_far, carried_far, (0, 0))
    passages_grad = (near + far) + sum(dot(place, piece, (0, 0)) for piece in split_low(picked_grad))

    deep = model // links.dp
    score_rows = score_x.reshape(heads * kept, model)
    left_back = links.gather_block(jnp.concatenate([e_fed_low, e_attended_low, score_rows], axis=0))
    right_back = links.gather_rows(jnp.concatenate([e_pre_grad, e_q_grad, e_mixed_grad], axis=1))
    flat = lambda values: values.reshape(deep, -1)
    e_outer_grad = dot(flat(left_back[:, :, :kept]), right_forward[:, :hidden], (1, 0))
    e_inner_grad = dot(flat(left_forward[:, :, kept : 2 * kept]), right_back[:, :hidden], (1, 0))
    e_project_grad = dot(flat(left_back[:, :, kept : 2 * kept]), right_forward[:, hidden : hidden + part], (1, 0))
    e_query_grad = dot(flat(left_forward[:, :, :kept]), right_back[:, hidden : hidden + part], (1, 0))
    head_of = jnp.arange(part, dtype=jnp.int32) // HEAD_SIZE

    def by_head(values):
        values = values.reshape(links.dp, 1, kept, part)
        mine = jnp.arange(heads, dtype=jnp.int32)[None, :, None, None] == head_of[None, None, None, :]
        return jnp.where(mine, values, jnp.zeros((), LOW)).reshape(links.dp * heads * kept, part)

    e_key_grad = dot(flat(left_back[:, :, 2 * kept :]), by_head(right_forward[:, hidden + part :]), (1, 0)) * 0.125
    e_value_grad = dot(flat(left_forward[:, :, 2 * kept :]), by_head(right_back[:, hidden + part :]), (1, 0))
    vectors = jnp.concatenate([
        e_query_bias_grad, e_value_bias_grad, e_inner_bias_grad, e_project_bias_grad, e_first_gain_grad,
        e_first_shift_grad, e_outer_bias_grad, e_second_gain_grad, e_second_shift_grad,
    ])
    vectors = links.sum_all(vectors, True)
    e_vectors = [vectors[:part], vectors[part : 2 * part], vectors[2 * part : 2 * part + hidden]]
    e_vectors += [vectors[2 * part + hidden + i * model : 2 * part + hidden + (i + 1) * model] for i in range(6)]

    def ordered(matrices, small):
        query_g, key_g, value_g, project_g, inner_g, outer_g = matrices
        query_b, value_b, inner_b, project_b, gain1, shift1, outer_b, gain2, shift2 = small
        return (
            query_g, key_g, value_g, project_g, query_b, value_b, project_b, gain1, shift1,
            inner_g, inner_b, outer_g, outer_b, gain2, shift2,
        )

    return (
        (decoded, passages_grad, corrupted_grad)
        + ordered((e_query_grad, e_key_grad, e_value_grad, e_project_grad, e_inner_grad, e_outer_grad), e_vectors)
        + ordered((d_query_grad, d_key_grad, d_value_grad, d_project_grad, d_inner_grad, d_outer_grad), d_vectors)
    )


def solution(mesh):
    rows = P("dp", None)
    columns, half, whole = P(None, "tensor"), P("tensor"), P()
    block_in = (columns,) * 4 + (half, half, whole, whole, whole, columns, half, columns, whole, whole, whole)
    split = P("dp", "tensor")
    block_out = (split,) * 4 + (half, half, whole, whole, whole, split, half, split, whole, whole, whole)
    return jax.shard_map(
        functools.partial(local, mesh),
        mesh=mesh,
        in_specs=(rows,) * 4 + block_in * 2,
        out_specs=(rows,) * 3 + block_out * 2,
        check_vma=False,
    )
```

```python
import functools

import jax
import jax.numpy as jnp
from jax import lax
from jax.experimental import pallas as pl
from jax.experimental.pallas import tpu as pltpu
from jax.sharding import PartitionSpec as P

HEAD_SIZE = 64
EPSILON = 1e-06
NEGATIVE = -1e30
TILE = 128
AXES = ("dp", "tensor")
VMEM_LIMIT = 56 * 1024 * 1024
F32 = jnp.float32
LOW = jnp.bfloat16


def dot(left, right, contract):
    return lax.dot_general(left, right, ((contract[0:1], contract[1:2]), ((), ())), preferred_element_type=F32)


def call(kernel, name, outs, scalars, arrays, after=(), scratch=(), steps=None, axes=None):
    outs = [jax.ShapeDtypeStruct(shape, kind) for shape, kind in outs]
    count, real = len(scalars) + len(arrays), len(outs)
    passed = [entry for entry in after if hasattr(entry, "held")]
    after = [entry for entry in after if not hasattr(entry, "held")]
    views = [entry.held for entry in passed]
    skip = count + len(views) + len(after)

    def body(*refs):
        kernel(*refs[:count], *refs[skip : skip + real], *refs[skip + real + len(views) :])

    def spec(array):
        if steps is None:
            return pl.BlockSpec(memory_space=pltpu.VMEM)
        axis = axes(array.shape)
        block = [size // steps if d == axis else size for d, size in enumerate(array.shape)]
        return pl.BlockSpec(block, lambda i: tuple(i if d == axis else 0 for d in range(len(block))))

    anywhere = pl.BlockSpec(memory_space=pl.ANY)
    results = pl.pallas_call(
        body,
        out_shape=outs + [jax.ShapeDtypeStruct(view.shape, view.dtype) for view in views],
        grid=() if steps is None else (steps,),
        in_specs=[pl.BlockSpec(memory_space=pltpu.SMEM)] * len(scalars)
        + [spec(array) for array in arrays]
        + [anywhere] * (len(views) + len(after)),
        out_specs=[spec(out) for out in outs] + [anywhere] * len(views),
        scratch_shapes=list(scratch),
        input_output_aliases={count + i: real + i for i in range(len(views))},
        compiler_params=pltpu.CompilerParams(vmem_limit_bytes=VMEM_LIMIT),
        cost_estimate=pl.CostEstimate(flops=0, bytes_accessed=0, transcendentals=0),
        name=name,
    )(*scalars, *arrays, *views, *after)
    for entry, view in zip(passed, results[real:]):
        entry.held = view
    return results[:real]


def by_rows(rows):
    return lambda shape: 0 if shape[0] == rows else None


def first_step():
    return pl.program_id(0) == 0


def last_step():
    return pl.program_id(0) == pl.num_programs(0) - 1


def over_rows(rows, chunk, body):
    def step(i, carry):
        body(pl.ds(pl.multiple_of(i * chunk, chunk), chunk), i * chunk)
        return carry

    lax.fori_loop(0, rows // chunk, step, 0)


def ends_of(home, own, far):
    ends, end = [], 0
    for p in range(own.shape[1]):
        end = end + (own[0, p] if far is None else jnp.where(home[0] == 1, own[0, p], far[0, p]))
        ends.append(end)
    return ends


def segment_of(place, ends):
    return sum((place >= end).astype(jnp.int32) for end in ends)


def start_of(place, ends):
    start = jnp.zeros_like(place)
    for end in ends:
        start = jnp.where(place >= end, end, start)
    return start


def finish_of(place, ends, rows):
    finish = jnp.full_like(place, rows)
    for end in ends[::-1]:
        finish = jnp.where(place < end, end, finish)
    return finish


def iota(shape, axis):
    return lax.broadcasted_iota(jnp.int32, shape, axis)


def split_low(values):
    first = values.astype(LOW)
    rest = values - first.astype(F32)
    second = rest.astype(LOW)
    third = (rest - second.astype(F32)).astype(LOW)
    return [first, second, third]


def gelu_and_slope(pre):
    phi_sum = 0.5 + 0.5 * lax.erf(pre * 0.7071067811865476)
    density = jnp.exp(-0.5 * pre * pre) * 0.3989422804014327
    return pre * phi_sum, phi_sum + pre * density


def norm(summed):
    center = jnp.mean(summed, axis=-1, keepdims=True)
    offset = summed - center
    scale = lax.rsqrt(jnp.mean(offset * offset, axis=-1, keepdims=True) + EPSILON)
    return offset * scale, scale


def norm_back(grad, unit, scale, gain):
    scaled = grad * gain
    return scale * (
        scaled - jnp.mean(scaled, axis=-1, keepdims=True) - unit * jnp.mean(scaled * unit, axis=-1, keepdims=True)
    )


def column_sum(values):
    return jnp.sum(values, axis=0)


def eights(values):
    return jnp.sum(values.reshape(values.shape[0] // 8, 8, values.shape[1]), axis=0)


def encoder_attend(lengths, passages, query, key, value, project, query_bias, value_bias):
    rows, model = passages.shape
    part = query.shape[1]
    heads = part // HEAD_SIZE
    kept = -(-(lengths.shape[1] + 1) // 16) * 16

    def kernel(own, x_ref, q_w, k_w, v_w, p_w, q_b, v_b, xs_ref, q_ref, qk_ref, w_ref, wx_ref, o_ref, share_ref):
        ends = ends_of(None, own, None)
        firsts = [0] + ends
        row, place = iota((kept, rows), 0), iota((kept, rows), 1)
        first = jnp.zeros((kept, rows), jnp.int32)
        for p, at in enumerate(firsts):
            first = jnp.where(row == p, jnp.minimum(at, rows - 1), first)
        xs = dot((place == first).astype(LOW), x_ref[...], (1, 0)).astype(LOW)
        xs_ref[...] = xs
        same = row == segment_of(place, ends)
        queries = (dot(xs, q_w[...], (1, 0)) + q_b[...]).astype(LOW)
        q_ref[...] = queries
        head_of = iota((kept, part), 1) // HEAD_SIZE
        spread = jnp.concatenate(
            [jnp.where(head_of == h, queries, jnp.zeros_like(queries)) for h in range(heads)], axis=0
        )
        q_keys = dot(spread, k_w[...], (1, 1)).astype(LOW)
        qk_ref[...] = q_keys
        score = dot(q_keys, x_ref[...], (1, 1)) * 0.125
        score = jnp.where(same[None], score.reshape(heads, kept, rows), NEGATIVE)
        expo = jnp.exp(score - jnp.max(score, axis=2, keepdims=True))
        weights = (expo / jnp.sum(expo, axis=2, keepdims=True)).reshape(heads * kept, rows)
        w_ref[...] = weights
        low = weights.astype(LOW)
        weight_x = dot(low, x_ref[...], (1, 0)).astype(LOW)
        wx_ref[...] = weight_x
        mixed = dot(weight_x, v_w[...], (1, 0)) + jnp.sum(low.astype(F32), axis=1, keepdims=True) * v_b[...]
        mixed = sum(
            jnp.where(head_of == h, mixed[h * kept : (h + 1) * kept], 0.0) for h in range(heads)
        ).astype(LOW)
        o_ref[...] = mixed
        share_ref[...] = dot(mixed, p_w[...], (1, 1)).astype(LOW)

    return call(
        kernel,
        "encoder_attend",
        [
            ((kept, model), LOW), ((kept, part), LOW), ((heads * kept, model), LOW), ((heads * kept, rows), F32),
            ((heads * kept, model), LOW), ((kept, part), LOW), ((kept, model), LOW),
        ],
        [lengths],
        [passages, query, key, value, project, query_bias[None], value_bias[None]],
    )


def encoder_feed(xs, share, far, project_bias, gain, shift, inner, inner_bias, outer, after):
    kept, model = xs.shape
    hidden = inner.shape[1]

    def kernel(xs_ref, s_ref, f_ref, pb, g1, b1, in_w, in_b, out_w, unit_ref, scale_ref, y_ref, low_ref, act_ref, slope_ref, share_ref):
        attended = s_ref[...].astype(F32) + f_ref[...].astype(F32)
        unit, scale = norm(xs_ref[...].astype(F32) + attended + pb[...])
        unit_ref[...] = unit
        scale_ref[...] = scale
        first = unit * g1[...] + b1[...]
        y_ref[...] = first
        first_low = first.astype(LOW)
        low_ref[...] = first_low
        act, slope = gelu_and_slope(dot(first_low, in_w[...], (1, 0)) + in_b[...])
        act_ref[...] = act.astype(LOW)
        slope_ref[...] = slope
        share_ref[...] = dot(act.astype(LOW), out_w[...], (1, 1)).astype(LOW)

    return call(
        kernel,
        "encoder_feed",
        [
            ((kept, model), F32), ((kept, 1), F32), ((kept, model), F32), ((kept, model), LOW), ((kept, hidden), LOW),
            ((kept, hidden), F32), ((kept, model), LOW),
        ],
        [],
        [xs, share, far, project_bias[None], gain[None], shift[None], inner, inner_bias[None], outer],
        after,
    )


def encoder_end(first, share, far, outer_bias, gain, shift, after):
    kept, model = first.shape

    def kernel(y_ref, s_ref, f_ref, ob, g2, b2, unit_ref, scale_ref, out_ref):
        fed = s_ref[...].astype(F32) + f_ref[...].astype(F32)
        unit, scale = norm(y_ref[...] + fed + ob[...])
        unit_ref[...] = unit
        scale_ref[...] = scale
        out_ref[...] = unit * g2[...] + b2[...]

    return call(
        kernel,
        "encoder_end",
        [((kept, model), F32), ((kept, 1), F32), ((kept, model), F32)],
        [],
        [first, share, far, outer_bias[None], gain[None], shift[None]],
        after,
    )


def encoder_feed_back(totals, unit, scale, gain, outer, slope, inner, after):
    kept, model = totals.shape
    hidden = inner.shape[1]

    def kernel(t_ref, u_ref, r_ref, g2, out_w, slope_ref, in_w, grad_ref, low_ref, pre_ref, sums_ref, bias_ref, share_ref):
        totals, unit = t_ref[...], u_ref[...]
        grad = norm_back(totals, unit, r_ref[...], g2[...])
        grad_ref[...] = grad
        sums_ref[0:1, :] = jnp.sum(grad, axis=0, keepdims=True)
        sums_ref[1:2, :] = jnp.sum(totals * unit, axis=0, keepdims=True)
        sums_ref[2:3, :] = jnp.sum(totals, axis=0, keepdims=True)
        low = grad.astype(LOW)
        low_ref[...] = low
        pre = (dot(low, out_w[...], (1, 0)) * slope_ref[...]).astype(LOW)
        pre_ref[...] = pre
        bias_ref[...] = jnp.sum(pre.astype(F32), axis=0, keepdims=True)
        share_ref[...] = dot(pre, in_w[...], (1, 1)).astype(LOW)

    return call(
        kernel,
        "encoder_feed_back",
        [
            ((kept, model), F32), ((kept, model), LOW), ((kept, hidden), LOW), ((3, model), F32), ((1, hidden), F32),
            ((kept, model), LOW),
        ],
        [],
        [totals, unit, scale, gain[None], outer, slope, inner],
        after,
    )


def encoder_attend_back(lengths, second, share, far, unit, scale, gain, project, query, key, value, value_bias, passages, weights, q_keys, after):
    kept, model = second.shape
    rows = passages.shape[0]
    part = query.shape[1]
    heads = part // HEAD_SIZE

    def kernel(
        own, s_grad, s_ref, f_ref, u_ref, r_ref, g1, p_w, q_w, k_w, v_w, v_b, x_ref, w_ref, qk_ref,
        grad_ref, low_ref, sums_ref, mg_ref, sx_ref, dq_ref, dq_sum, dv_sum, coef_ref, carried_ref, back_ref,
    ):
        unit = u_ref[...]
        first_grad = s_grad[...] + (s_ref[...].astype(F32) + f_ref[...].astype(F32))
        grad = norm_back(first_grad, unit, r_ref[...], g1[...])
        grad_ref[...] = grad
        sums_ref[0:1, :] = jnp.sum(grad, axis=0, keepdims=True)
        sums_ref[1:2, :] = jnp.sum(first_grad * unit, axis=0, keepdims=True)
        sums_ref[2:3, :] = jnp.sum(first_grad, axis=0, keepdims=True)
        low = grad.astype(LOW)
        low_ref[...] = low
        mixed_grad = dot(low, p_w[...], (1, 0)).astype(LOW)
        mg_ref[...] = mixed_grad
        head_of = iota((kept, part), 1) // HEAD_SIZE
        spread = jnp.concatenate(
            [jnp.where(head_of == h, mixed_grad, jnp.zeros_like(mixed_grad)) for h in range(heads)], axis=0
        )
        g_values = dot(spread, v_w[...], (1, 1)).astype(LOW)
        weights = w_ref[...]
        weights_low = weights.astype(LOW)
        weight_grad = dot(g_values, x_ref[...], (1, 1)) + jnp.sum(spread.astype(F32) * v_b[...], axis=1, keepdims=True)
        middle = jnp.sum(weights * weight_grad, axis=1, keepdims=True)
        score_grad = (weights * (weight_grad - middle)).astype(LOW)
        score_x = dot(score_grad, x_ref[...], (1, 0)).astype(LOW)
        sx_ref[...] = score_x
        q_grad = dot(score_x, k_w[...], (1, 0)) * 0.125
        q_grad = sum(jnp.where(head_of == h, q_grad[h * kept : (h + 1) * kept], 0.0) for h in range(heads)).astype(LOW)
        dq_ref[...] = q_grad
        dq_sum[...] = jnp.sum(q_grad.astype(F32), axis=0, keepdims=True)
        weight_sum = jnp.sum(weights_low.astype(F32), axis=1, keepdims=True)
        dv_sum[...] = jnp.sum(spread.astype(F32) * weight_sum, axis=0, keepdims=True)
        back_ref[...] = dot(q_grad, q_w[...], (1, 1)).astype(LOW)
        ends = ends_of(None, own, None)
        same = iota((kept, rows), 0) == segment_of(iota((kept, rows), 1), ends)
        for kind, values in enumerate((score_grad, weights_low)):
            for h in range(heads):
                coefs = jnp.where(same, values[h * kept : (h + 1) * kept].astype(F32), 0.0)
                coef_ref[kind * heads + h : kind * heads + h + 1, :] = jnp.sum(coefs, axis=0, keepdims=True)
        carried_ref[0 : heads * kept, :] = qk_ref[...] * jnp.asarray(0.125, LOW)
        carried_ref[heads * kept :, :] = g_values

    return call(
        kernel,
        "encoder_attend_back",
        [
            ((kept, model), F32), ((kept, model), LOW), ((3, model), F32), ((kept, part), LOW),
            ((heads * kept, model), LOW), ((kept, part), LOW), ((1, part), F32), ((1, part), F32),
            ((2 * heads, rows), F32), ((2 * heads * kept, model), LOW), ((kept, model), LOW),
        ],
        [lengths],
        [
            second, share, far, unit, scale, gain[None], project, query, key, value, value_bias[None], passages,
            weights, q_keys,
        ],
        after,
    )


def passages_back(chip, lengths, coefs, coefs_far, carried, carried_far, back, back_far, picked_grad, after):
    kinds, rows = coefs.shape
    count, model = carried.shape
    kept = count // kinds

    def kernel(chip_ref, own, c_ref, cf_ref, v_ref, vf_ref, b_ref, bf_ref, g_ref, out_ref):
        low_chip = chip_ref[0] == 0
        ends = ends_of(None, own, None)
        row, place = iota((kept, rows), 0), iota((kept, rows), 1)
        same = row == segment_of(place, ends)

        def spread(values):
            return jnp.concatenate(
                [jnp.where(same, values[i : i + 1, :], 0.0).astype(LOW) for i in range(kinds)], axis=0
            )

        mine, other = c_ref[...].astype(F32), cf_ref[...].astype(F32)
        first = spread(jnp.where(low_chip, mine, other))
        second = spread(jnp.where(low_chip, other, mine))
        mine, other = v_ref[...].astype(F32), vf_ref[...].astype(F32)
        first = dot(first, jnp.where(low_chip, mine, other).astype(LOW), (0, 0))
        second = dot(second, jnp.where(low_chip, other, mine).astype(LOW), (0, 0))
        leads = (same & (place == start_of(place, ends))).astype(F32).astype(LOW)
        picked = g_ref[...] + (b_ref[...].astype(F32) + bf_ref[...].astype(F32))
        pieces = jnp.concatenate(split_low(picked), axis=0)
        out_ref[...] = (first + second) + dot(jnp.concatenate([leads] * 3, axis=0), pieces, (0, 0))

    return call(
        kernel,
        "passages_back",
        [((rows, model), F32)],
        [chip, lengths],
        [coefs, coefs_far, carried, carried_far, back, back_far, picked_grad],
        after,
    )[0]


def window_sizes(tiles):
    sizes = [2, 3, 4, 6, tiles]
    return sorted({min(s, tiles) for s in sizes})


def for_window(first, last, tiles, body):
    need = last - first
    below = 0
    for size in window_sizes(tiles):
        @pl.when((need > below) & (need <= size))
        def _(size=size):
            body(size, jnp.minimum(first, tiles - size))
        below = size


def tile_window(j, ends, rows):
    low = start_of(j * TILE, ends)
    high = finish_of(j * TILE + TILE - 1, ends, rows)
    return low // TILE, (high + TILE - 1) // TILE


def decoder_attend(home, own, far, corrupt, corrupt_far, encoded, encoded_far, query, key, value, query_bias, value_bias, project, after):
    rows, model = corrupt.shape
    part = query.shape[1]
    kept = encoded.shape[0]
    heads = part // HEAD_SIZE
    tiles = rows // TILE

    def kernel(
        home_ref, own_ref, far_ref, c_ref, cf_ref, e_ref, ef_ref, q_w, k_w, v_w, q_b, v_b, p_w,
        in_ref, low_ref, q_ref, k_ref, v_ref, o_ref, lse_ref, share_ref, table_ref,
    ):
        ends = ends_of(home_ref, own_ref, far_ref)
        at_home = home_ref[0] == 1
        table_ref[...] = jnp.concatenate(split_low(jnp.where(at_home, e_ref[...], ef_ref[...])), axis=0)

        def fill(here, begin):
            place = begin + iota((TILE, 3 * kept), 0)
            lane = iota((TILE, 3 * kept), 1)
            lane = jnp.where(lane >= 2 * kept, lane - 2 * kept, jnp.where(lane >= kept, lane - kept, lane))
            member = (segment_of(place, ends) == lane).astype(F32).astype(LOW)
            corrupt = jnp.where(at_home, c_ref[here, :].astype(F32), cf_ref[here, :].astype(F32))
            d_in = corrupt + dot(member, table_ref[...], (1, 0))
            in_ref[here, :] = d_in
            low_ref[here, :] = d_in.astype(LOW)

        over_rows(rows, TILE, fill)
        q_ref[...] = (dot(low_ref[...], q_w[...], (1, 0)) + q_b[...]).astype(LOW)
        k_ref[...] = dot(low_ref[...], k_w[...], (1, 0)).astype(LOW)
        v_ref[...] = (dot(low_ref[...], v_w[...], (1, 0)) + v_b[...]).astype(LOW)
        first_head = iota((1, TILE), 1) < HEAD_SIZE
        lane = iota((TILE, TILE), 1)

        def step(j, carry):
            def body(size, begin):
                span = size * TILE
                here = pl.ds(pl.multiple_of(j * TILE, TILE), TILE)
                keys = pl.ds(pl.multiple_of(begin * TILE, TILE), span)
                row = j * TILE + iota((TILE, 1), 0)
                place = begin * TILE + iota((TILE, span), 1)
                inside = (place >= start_of(row, ends)) & (place < finish_of(row, ends, rows))
                logs = jnp.zeros((TILE, TILE), F32)
                for pair in range(part // TILE):
                    cols = pl.ds(pair * TILE, TILE)
                    queries = q_ref[here, cols] * jnp.asarray(0.125, LOW)
                    pair_keys = k_ref[keys, cols]
                    pair_values = v_ref[keys, cols]
                    mixed = []
                    for half in range(2):
                        mine = first_head if half == 0 else jnp.logical_not(first_head)
                        score = dot(jnp.where(mine, queries, jnp.zeros_like(queries)), pair_keys, (1, 1))
                        score = jnp.where(inside, score, NEGATIVE)
                        top = jnp.max(score, axis=1, keepdims=True)
                        expo = jnp.exp(score - top)
                        total = jnp.sum(expo, axis=1, keepdims=True)
                        mixed.append(dot(expo.astype(LOW), pair_values, (1, 0)) / total)
                        logs = jnp.where(lane == 2 * pair + half, top + jnp.log(total), logs)
                    o_ref[here, cols] = jnp.where(first_head, mixed[0], mixed[1]).astype(LOW)
                lse_ref[:, here] = jnp.transpose(logs)[0:8, :]

            first, last = tile_window(j, ends, rows)
            for_window(first, last, tiles, body)
            return carry

        lax.fori_loop(0, tiles, step, 0)
        share_ref[...] = dot(o_ref[...], p_w[...], (1, 1)).astype(LOW)

    return call(
        kernel,
        "decoder_attend",
        [
            ((rows, model), F32), ((rows, model), LOW), ((rows, part), LOW), ((rows, part), LOW), ((rows, part), LOW),
            ((rows, part), LOW), ((8, rows), F32), ((rows, model), LOW),
        ],
        [home, own, far],
        [
            corrupt, corrupt_far, encoded, encoded_far, query, key, value, query_bias[None], value_bias[None], project,
        ],
        after,
        [pltpu.VMEM((3 * kept, model), LOW)],
    )


def decoder_norm(d_in, share, far, project_bias, gain, shift, after):
    rows, model = d_in.shape

    def kernel(x_ref, s_ref, f_ref, pb, g1, b1, unit_ref, scale_ref, low_ref):
        def part(here, begin):
            attended = s_ref[here, :].astype(F32) + f_ref[here, :].astype(F32)
            unit, scale = norm(x_ref[here, :] + attended + pb[...])
            unit_ref[here, :] = unit
            scale_ref[here, :] = scale
            low_ref[here, :] = (unit * g1[...] + b1[...]).astype(LOW)

        over_rows(unit_ref.shape[0], 64, part)

    return call(
        kernel,
        "decoder_norm",
        [((rows, model), F32), ((rows, 1), F32), ((rows, model), LOW)],
        [],
        [d_in, share, far, project_bias[None], gain[None], shift[None]],
        after,
        steps=rows // 256,
        axes=by_rows(rows),
    )


def decoder_hidden(first_low, inner, inner_bias, after):
    rows, model = first_low.shape
    hidden = inner.shape[1]
    block = 256

    def kernel(low_ref, in_w, in_b, act_ref, slope_ref, pre_ref):
        pre_ref[...] = dot(low_ref[...], in_w[...], (1, 0))

        def activate(here, begin):
            act, slope = gelu_and_slope(pre_ref[here, :] + in_b[...])
            act_ref[here, :] = act.astype(LOW)
            slope_ref[here, :] = slope.astype(LOW)

        over_rows(rows, 64, activate)

    return call(
        kernel,
        "decoder_hidden",
        [((rows, hidden), LOW), ((rows, hidden), LOW)],
        [],
        [first_low, inner, inner_bias[None]],
        after,
        [pltpu.VMEM((rows, block), F32)],
        steps=hidden // block,
        axes=lambda shape: 1 if shape[1] == hidden else None,
    )


def weight_grads(name, left, right, base):
    rows, model = left.shape
    width = right.shape[1]
    block = 384
    steps = width // block
    first = steps if base is None else 0

    def kernel(l_ref, r_ref, *refs):
        refs[-1][...] = dot(l_ref[...], r_ref[...], (0, 0)).astype(LOW)

    return pl.pallas_call(
        kernel,
        out_shape=jax.ShapeDtypeStruct((model, 2 * width), LOW),
        grid=(steps,),
        in_specs=[pl.BlockSpec((rows, model), lambda i: (0, 0)), pl.BlockSpec((rows, block), lambda i: (0, i))]
        + [pl.BlockSpec(memory_space=pl.ANY)] * (base is not None),
        out_specs=pl.BlockSpec((model, block), lambda i: (0, i + first)),
        input_output_aliases={} if base is None else {2: 0},
        compiler_params=pltpu.CompilerParams(vmem_limit_bytes=VMEM_LIMIT),
        cost_estimate=pl.CostEstimate(flops=0, bytes_accessed=0, transcendentals=0),
        name=name,
    )(left, right, *([] if base is None else [base]))


def decoder_norm_back(home, own, far_lengths, unit1, share, far, first_gain, first_shift, outer_bias, gain, shift, cot, cot_far, after):
    rows, model = unit1.shape
    steps = rows // 128

    def kernel(
        home_ref, own_ref, farl_ref, u_ref, s_ref, f_ref, g1, b1, ob, g2, b2, c_ref, cf_ref,
        out_ref, grad_ref, low_ref, sums_ref, acc_ref,
    ):
        ends = ends_of(home_ref, own_ref, farl_ref)
        at_home = home_ref[0] == 1
        height = u_ref.shape[0]

        @pl.when(first_step())
        def _():
            acc_ref[...] = jnp.zeros_like(acc_ref)

        def part(here, begin):
            fed = s_ref[here, :].astype(F32) + f_ref[here, :].astype(F32)
            first = u_ref[here, :] * g1[...] + b1[...]
            unit, scale = norm(first + fed + ob[...])
            valid = (pl.program_id(0) * height + begin + iota((64, 1), 0) < ends[-1]).astype(F32)
            out_ref[here, :] = ((unit * g2[...] + b2[...]) * valid).astype(LOW)
            cot = jnp.where(at_home, c_ref[here, :].astype(F32), cf_ref[here, :].astype(F32)) * valid
            grad = norm_back(cot, unit, scale, g2[...])
            grad_ref[here, :] = grad
            low_ref[here, :] = grad.astype(LOW)
            acc_ref[0:8, :] += eights(grad)
            acc_ref[8:16, :] += eights(cot * unit)
            acc_ref[16:24, :] += eights(cot)

        over_rows(height, 64, part)

        @pl.when(last_step())
        def _():
            for i in range(3):
                sums_ref[i : i + 1, :] = jnp.sum(acc_ref[8 * i : 8 * i + 8, :], axis=0, keepdims=True)

    return call(
        kernel,
        "decoder_norm_back",
        [((rows, model), LOW), ((rows, model), F32), ((rows, model), LOW), ((3, model), F32)],
        [home, own, far_lengths],
        [
            unit1, share, far, first_gain[None], first_shift[None], outer_bias[None], gain[None], shift[None], cot,
            cot_far,
        ],
        after,
        [pltpu.VMEM((24, model), F32)],
        steps=steps,
        axes=by_rows(rows),
    )


def decoder_feed_back(fed_low, outer, slope, inner, after):
    rows, model = fed_low.shape
    hidden = inner.shape[1]
    block = 256

    def kernel(low_ref, out_w, slope_ref, in_w, pre_ref, bias_ref, share_ref, wide_ref, bias_acc):
        for j in range(hidden // block):
            cols = slice(j * block, (j + 1) * block)
            wide_ref[...] = dot(low_ref[...], out_w[:, cols], (1, 0))
            bias_acc[...] = jnp.zeros_like(bias_acc)

            def slopes(here, begin):
                pre = (wide_ref[here, :] * slope_ref[here, cols].astype(F32)).astype(LOW)
                pre_ref[here, cols] = pre
                bias_acc[...] += eights(pre.astype(F32))

            over_rows(rows, 128, slopes)
            bias_ref[:, cols] = jnp.sum(bias_acc[...], axis=0, keepdims=True)
        share_ref[...] = dot(pre_ref[...], in_w[...], (1, 1)).astype(LOW)

    return call(
        kernel,
        "decoder_feed_back",
        [((rows, hidden), LOW), ((1, hidden), F32), ((rows, model), LOW)],
        [],
        [fed_low, outer, slope, inner],
        after,
        [pltpu.VMEM((rows, block), F32), pltpu.VMEM((8, block), F32)],
    )


def decoder_first_back(second, share, far, unit, scale, gain, after):
    rows, model = second.shape

    def kernel(s_grad, s_ref, f_ref, u_ref, r_ref, g1, grad_ref, low_ref, sums_ref, acc_ref):
        @pl.when(first_step())
        def _():
            acc_ref[...] = jnp.zeros_like(acc_ref)

        def part(here, begin):
            unit = u_ref[here, :]
            first_grad = s_grad[here, :] + (s_ref[here, :].astype(F32) + f_ref[here, :].astype(F32))
            grad = norm_back(first_grad, unit, r_ref[here, :], g1[...])
            grad_ref[here, :] = grad
            low_ref[here, :] = grad.astype(LOW)
            acc_ref[0:8, :] += eights(grad)
            acc_ref[8:16, :] += eights(first_grad * unit)
            acc_ref[16:24, :] += eights(first_grad)

        over_rows(u_ref.shape[0], 64, part)

        @pl.when(last_step())
        def _():
            for i in range(3):
                sums_ref[i : i + 1, :] = jnp.sum(acc_ref[8 * i : 8 * i + 8, :], axis=0, keepdims=True)

    return call(
        kernel,
        "decoder_first_back",
        [((rows, model), F32), ((rows, model), LOW), ((3, model), F32)],
        [],
        [second, share, far, unit, scale, gain[None]],
        after,
        [pltpu.VMEM((24, model), F32)],
        steps=rows // 128,
        axes=by_rows(rows),
    )


def decoder_attend_back(home, own, far_lengths, low, project, lse, query, key, value, query_w, key_w, value_w, after):
    rows, model = low.shape
    part = query.shape[1]
    tiles = rows // TILE

    def kernel(
        home_ref, own_ref, farl_ref, low_ref, p_w, lse_ref, q_ref, k_ref, v_ref, q_w, k_w, v_w,
        all_ref, share_ref, sums_ref, g_ref, kt_ref, dk_sum, dv_sum, acc_ref,
    ):
        ends = ends_of(home_ref, own_ref, farl_ref)
        g_ref[...] = dot(low_ref[...], p_w[...], (1, 0)).astype(LOW)
        first_head = iota((1, TILE), 1) < HEAD_SIZE
        dk_sum[...] = jnp.zeros_like(dk_sum)
        dv_sum[...] = jnp.zeros_like(dv_sum)
        acc_ref[...] = jnp.zeros_like(acc_ref)

        def turn(here, begin):
            for pair in range(part // TILE):
                cols = pl.ds(pair * TILE, TILE)
                kt_ref[cols, here] = jnp.transpose(k_ref[here, cols].astype(F32)).astype(LOW)

        over_rows(rows, TILE, turn)

        def step(j, carry):
            def body(size, begin):
                span = size * TILE
                here = pl.ds(pl.multiple_of(j * TILE, TILE), TILE)
                keys = pl.ds(pl.multiple_of(begin * TILE, TILE), span)
                column = j * TILE + iota((1, TILE), 1)
                place = begin * TILE + iota((span, TILE), 0)
                inside = (place >= start_of(column, ends)) & (place < finish_of(column, ends, rows))
                for pair in range(part // TILE):
                    cols = pl.ds(pair * TILE, TILE)
                    queries = q_ref[here, cols] * jnp.asarray(0.125, LOW)
                    grads = g_ref[here, cols]
                    pair_keys = k_ref[keys, cols]
                    pair_values = v_ref[keys, cols]
                    weights, score_grads, own_q, own_g, q_grads = [], [], [], [], []
                    for half in range(2):
                        head = 2 * pair + half
                        mine = first_head if half == 0 else jnp.logical_not(first_head)
                        head_q = jnp.where(mine, queries, jnp.zeros_like(queries))
                        head_g = jnp.where(mine, grads, jnp.zeros_like(grads))
                        score = dot(pair_keys, head_q, (1, 1))
                        weight = jnp.exp(jnp.where(inside, score, NEGATIVE) - lse_ref[head : head + 1, here])
                        weight_grad = dot(pair_values, head_g, (1, 1))
                        middle = jnp.sum(weight * weight_grad, axis=0, keepdims=True)
                        score_grad = (weight * (weight_grad - middle)).astype(LOW)
                        turned = kt_ref[pl.ds(head * HEAD_SIZE, HEAD_SIZE), keys]
                        q_grads.append(dot(turned, score_grad, (1, 0)) * 0.125)
                        weights.append(weight.astype(LOW))
                        score_grads.append(score_grad)
                        own_q.append(head_q)
                        own_g.append(head_g)
                    all_ref[here, cols] = jnp.transpose(jnp.concatenate(q_grads, axis=0)).astype(LOW)
                    dk_sum[keys, cols] += dot(
                        jnp.concatenate(score_grads, axis=1), jnp.concatenate(own_q, axis=0), (1, 0)
                    )
                    dv_sum[keys, cols] += dot(jnp.concatenate(weights, axis=1), jnp.concatenate(own_g, axis=0), (1, 0))

            first, last = tile_window(j, ends, rows)
            for_window(first, last, tiles, body)
            return carry

        lax.fori_loop(0, tiles, step, 0)

        def close(here, begin):
            all_ref[here, part : 2 * part] = dk_sum[here, :].astype(LOW)
            value_grad = dv_sum[here, :].astype(LOW)
            all_ref[here, 2 * part :] = value_grad
            acc_ref[:, 0:part] += eights(all_ref[here, 0:part].astype(F32))
            acc_ref[:, part:] += eights(value_grad.astype(F32))

        over_rows(rows, TILE, close)
        sums_ref[...] = jnp.sum(acc_ref[...], axis=0, keepdims=True)
        share = dot(all_ref[:, 0:part], q_w[...], (1, 1)) + dot(all_ref[:, part : 2 * part], k_w[...], (1, 1))
        share_ref[...] = (share + dot(all_ref[:, 2 * part :], v_w[...], (1, 1))).astype(LOW)

    return call(
        kernel,
        "decoder_attend_back",
        [((rows, 3 * part), LOW), ((rows, model), LOW), ((1, 2 * part), F32)],
        [home, own, far_lengths],
        [low, project, lse, query, key, value, query_w, key_w, value_w],
        after,
        [
            pltpu.VMEM((rows, part), LOW), pltpu.VMEM((part, rows), LOW), pltpu.VMEM((rows, part), F32),
            pltpu.VMEM((rows, part), F32), pltpu.VMEM((8, 2 * part), F32),
        ],
    )


def attend_weight_grads(d_low, grads, attended_low, mixed, after):
    rows, model = d_low.shape
    part = mixed.shape[1]

    def kernel(x_ref, g_ref, a_ref, o_ref, first_ref, last_ref):
        first_ref[...] = dot(x_ref[...], g_ref[:, 0 : 2 * part], (0, 0)).astype(LOW)
        last_ref[:, 0:part] = dot(x_ref[...], g_ref[:, 2 * part :], (0, 0)).astype(LOW)
        last_ref[:, part:] = dot(a_ref[...], o_ref[...], (0, 0)).astype(LOW)

    return call(
        kernel, "attend_weight_grads", [((model, 2 * part), LOW)] * 2, [], [d_low, grads, attended_low, mixed], after
    )


def pack_vectors(blocks, after):
    model = blocks[0][-1].shape[1]
    part = model // 2
    height = -(-9 * len(blocks) // 8) * 8

    def kernel(*refs):
        out = refs[-1]
        out[...] = jnp.zeros_like(out)
        for i in range(len(blocks)):
            query, value, inner, first, second = refs[5 * i : 5 * i + 5]
            row = 9 * i
            out[row : row + 1, 0:part] = query[...]
            out[row : row + 1, part:] = value[...]
            out[row + 1 : row + 2, :] = inner[:, 0:model]
            out[row + 2 : row + 3, :] = inner[:, model:]
            out[row + 3 : row + 6, :] = first[...]
            out[row + 6 : row + 9, :] = second[...]

    arrays = [array for block in blocks for array in block]
    return call(kernel, "pack_vectors", [((height, model), F32)], [], arrays, after)[0]


def decoder_end(home, own, far_lengths, grad, share, far, kept, after):
    rows, model = grad.shape
    chunk = 256

    def kernel(home_ref, own_ref, farl_ref, g_ref, s_ref, f_ref, low_ref, total_ref):
        ends = ends_of(home_ref, own_ref, farl_ref)

        @pl.when(first_step())
        def _():
            total_ref[...] = jnp.zeros_like(total_ref)

        d_in = g_ref[...] + (s_ref[...].astype(F32) + f_ref[...].astype(F32))
        low_ref[...] = d_in.astype(LOW)
        member = iota((kept, chunk), 0) == segment_of(pl.program_id(0) * chunk + iota((kept, chunk), 1), ends)
        member = member.astype(F32).astype(LOW)
        total_ref[...] += sum(dot(member, piece, (1, 0)) for piece in split_low(d_in))

    return call(
        kernel,
        "decoder_end",
        [((rows, model), LOW), ((kept, model), F32)],
        [home, own, far_lengths],
        [grad, share, far],
        after,
        steps=rows // chunk,
        axes=by_rows(rows),
    )


class Links:
    def __init__(self, mesh):
        self.dp = mesh.shape["dp"]
        self.parts = mesh.shape["tensor"]
        self.bits = (self.dp // 2).bit_length() - 1
        self.core = lax.axis_index("dp") & 1
        self.group = lax.axis_index("dp") >> 1
        self.chip = lax.axis_index("tensor")
        self.home = self.core == self.chip

    def move(self, value, target):
        pairs = []
        for i in range(self.dp):
            for t in range(self.parts):
                to_i, to_t = target(i, t)
                pairs.append((i * self.parts + t, to_i * self.parts + to_t))
        return lax.ppermute(value, AXES, pairs)

    def swap_core(self, value):
        return self.move(value, lambda i, t: (i ^ 1, t))

    def swap_tensor(self, value):
        return self.move(value, lambda i, t: (i, t ^ 1))

    def swap_group(self, value, bit):
        return self.move(value, lambda i, t: (i ^ (2 << bit), t))

    def turn(self, value):
        return self.move(value, lambda i, t: (i, t) if (i & 1) == t else (i ^ 1, t ^ 1))

    def of_chip(self, value):
        return jnp.where(self.home, value, self.swap_core(value))

    def pick(self, value, axis, bit):
        return lax.dynamic_slice_in_dim(value, bit, 1, axis)

    def last_halving(self, value):
        view = value.reshape(2, -1, value.shape[1])
        sent = self.swap_tensor(self.pick(view, 0, 1 - self.chip))
        return self.turn((self.pick(view, 0, self.chip).astype(F32) + sent.astype(F32))[0])

    def copies(self, value, lanes):
        rows = value.shape[0]
        value = value.reshape(rows, -1, lanes).transpose(1, 0, 2).reshape(-1, lanes)
        return jnp.broadcast_to(value[None], (self.dp,) + value.shape)

    def rows_of(self, value, rows):
        lanes = value.shape[2]
        return value.reshape(self.dp, -1, rows, lanes).transpose(0, 2, 1, 3).reshape(self.dp, rows, -1)

    def gather_rows(self, value):
        copies = self.copies(value, 128)
        return self.rows_of(lax.all_to_all(copies, "dp", 0, 0, tiled=True), value.shape[0])

    def scatter_groups(self, value):
        cores = [[2 * g + c for g in range(self.dp // 2)] for c in range(2)]
        return lax.psum_scatter(value, "dp", scatter_dimension=0, axis_index_groups=cores, tiled=True)


class Held:
    def __init__(self, view):
        self.held = view


class Total:
    def __init__(self, links, value):
        self.links, self.held, self.done = links, value, 0

    def step(self):
        self.held = self.held + self.links.swap_group(self.held, self.done)
        self.done += 1

    def finish(self):
        while self.done < self.links.bits:
            self.step()
        return self.held


class Halving:
    def __init__(self, links, grad, order):
        self.links, self.order = links, list(order)
        self.shape = (grad.shape[0] // links.dp, grad.shape[1])
        view = grad.reshape((2,) * links.bits + (2,) + self.shape)
        self.parts = [(view, {})]

    @property
    def held(self):
        return self.parts[-1][0]

    @held.setter
    def held(self, value):
        self.parts[-1] = (value, self.parts[-1][1])

    def cut(self, place, axis=None, bit=None):
        total = 0
        for view, own in self.parts:
            at = {**place, **own} if axis is None else {**place, **own, axis: bit}
            starts = [at.get(d, 0) if view.shape[d] > 1 else 0 for d in range(view.ndim)]
            sizes = [1 if d in at else view.shape[d] for d in range(view.ndim)]
            total = total + lax.dynamic_slice(view, starts, sizes).astype(F32)
        return total

    def step(self):
        links, step = self.links, self.order.pop(0)
        if step < 0:
            axis, mine, swap = links.bits, links.chip, links.swap_tensor
        else:
            axis, mine = links.bits - 1 - step, (links.group >> step) & 1
            swap = lambda value: links.swap_group(value, step)
        sent = swap(self.cut({}, axis, 1 - mine).astype(LOW))
        self.parts = [(view, {**own, axis: mine}) for view, own in self.parts] + [(sent, {})]

    def left(self):
        return self.cut({}).reshape(-1, self.shape[1])

    def finish(self):
        while self.order:
            self.step()
        return self.links.turn(self.left())


def local(mesh, passages, corrupted, lengths, cotangent, *weights):
    (
        e_query, e_key, e_value, e_project, e_query_bias, e_value_bias, e_project_bias, e_first_gain, e_first_shift,
        e_inner, e_inner_bias, e_outer, e_outer_bias, e_second_gain, e_second_shift,
    ) = weights[:15]
    (
        d_query, d_key, d_value, d_project, d_query_bias, d_value_bias, d_project_bias, d_first_gain, d_first_shift,
        d_inner, d_inner_bias, d_outer, d_outer_bias, d_second_gain, d_second_shift,
    ) = weights[15:]
    links = Links(mesh)
    rows, model = passages.shape
    part = e_query.shape[1]
    hidden = e_inner.shape[1]
    heads = part // HEAD_SIZE
    home = links.home.astype(jnp.int32)[None]

    chip = links.chip.astype(jnp.int32)[None]
    deep = model // links.dp

    d_query = links.turn(d_query)
    d_key = links.turn(d_key)
    d_halves = jnp.concatenate([d_query_bias, d_value_bias, d_inner_bias])
    lengths_far = links.swap_core(lengths)
    corrupted_far = links.swap_core(corrupted)

    x_low, e_q, q_keys, e_weights, weight_x, e_mixed, share = encoder_attend(
        lengths, passages, e_query, e_key, e_value, e_project, e_query_bias, e_value_bias
    )
    kept = x_low.shape[0]
    share_far = links.swap_tensor(share)
    d_value = links.turn(d_value)
    d_project = links.turn(d_project)
    d_halves = links.turn(d_halves)
    e_unit1, e_scale1, e_first, e_first_low, e_act, e_slope, share = encoder_feed(
        x_low, share, share_far, e_project_bias, e_first_gain, e_first_shift, e_inner, e_inner_bias,
        e_outer, (d_query, d_key),
    )
    inner_held, outer_held = Held(d_inner), Held(d_outer)
    e_unit2, e_scale2, encoded = encoder_end(
        e_first, share, links.swap_tensor(share), e_outer_bias, e_second_gain, e_second_shift,
        (d_value, d_project, d_halves, corrupted_far, inner_held, outer_held),
    )
    d_query_bias, d_value_bias, d_inner_bias = d_halves[:part], d_halves[part : 2 * part], d_halves[2 * part :]
    left_forward = jnp.concatenate([x_low, e_first_low, weight_x], axis=0).T
    left_forward = lax.all_gather(left_forward, "dp")
    right_forward = lax.all_gather(jnp.concatenate([e_act, e_mixed, e_q], axis=1), "dp")

    encoded_far = links.swap_core(encoded)
    d_inner = links.turn(inner_held.held)
    d_outer = links.turn(outer_held.held)
    d_in, d_low, query, key, value, mixed, lse, share = decoder_attend(
        home, lengths, lengths_far, corrupted, corrupted_far, encoded, encoded_far, d_query, d_key,
        d_value, d_query_bias, d_value_bias, d_project, (),
    )
    cotangent_far = links.swap_core(cotangent)
    unit1, scale1, first_low = decoder_norm(
        d_in, share, links.swap_core(share), d_project_bias, d_first_gain, d_first_shift, ()
    )
    act, slope = decoder_hidden(first_low, d_inner, d_inner_bias, ())
    share = dot(act, d_outer, (1, 1)).astype(LOW)

    decoded, second_grad, fed_low, second_sums = decoder_norm_back(
        home, lengths, lengths_far, unit1, share, links.swap_core(share), d_first_gain, d_first_shift, d_outer_bias,
        d_second_gain, d_second_shift, cotangent, cotangent_far, (),
    )
    outer_grad = weight_grads("outer_grad", fed_low, act, None)
    pre_grad, inner_bias_grad, share = decoder_feed_back(fed_low, d_outer, slope, d_inner, (outer_grad,))
    share_far = links.swap_core(share)
    feed_grads = weight_grads("inner_grad", first_low, pre_grad, outer_grad)
    first_grad, attended_low, first_sums = decoder_first_back(
        second_grad, share, share_far, unit1, scale1, d_first_gain, (feed_grads,)
    )
    feed_grads = links.scatter_groups(feed_grads)
    attend_grads, share, attend_sums = decoder_attend_back(
        home, lengths, lengths_far, attended_low, d_project, lse, query, key, value, d_query, d_key, d_value,
        (left_forward, right_forward),
    )
    share_far = links.swap_core(share)
    decoded, attend_held = Held(decoded), Held(attend_grads)
    corrupted_low, totals = decoder_end(
        home, lengths, lengths_far, first_grad, share, share_far, kept, (attend_held,)
    )
    totals = links.turn(totals)
    across = list(range(links.bits))
    pairs = attend_weight_grads(d_low, attend_held.held, attended_low, mixed, ())
    pairs = [
        Halving(links, pairs[0], across + [-1]),
        Halving(links, pairs[1], across[1:2] + across[:1] + across[2:] + [-1]),
    ]
    corrupted_low = Held(corrupted_low)

    e_second_grad, e_fed_low, e_pre_grad, e_second_sums, e_inner_bias_grad, share = encoder_feed_back(
        totals, e_unit2, e_scale2, e_second_gain, e_outer, e_slope, e_inner, (*pairs,)
    )
    share_far = links.swap_tensor(share)
    for pair in pairs:
        pair.step()
    pre_all = links.gather_rows(e_pre_grad)
    (
        e_first_grad, e_attended_low, e_first_sums, e_mixed_grad, score_x, e_q_grad, e_query_sum, e_value_sum, coefs,
        carried, q_back,
    ) = encoder_attend_back(
        lengths, e_second_grad, share, share_far, e_unit1, e_scale1, e_first_gain, e_project, e_query,
        e_key, e_value, e_value_bias, passages, e_weights, q_keys, (corrupted_low,),
    )
    vectors = pack_vectors([
        (e_query_sum, e_value_sum, e_inner_bias_grad, e_first_sums, e_second_sums),
        (attend_sums[:, :part], attend_sums[:, part:], inner_bias_grad, first_sums, second_sums),
    ], ())
    vectors = Total(links, vectors)
    coefs = coefs.astype(LOW)
    coefs_far = links.swap_tensor(coefs)
    carried_far = links.swap_tensor(carried)
    back_far = links.swap_tensor(q_back)
    for pair in pairs:
        pair.step()
    passages_grad = passages_back(
        chip, lengths, coefs, coefs_far, carried, carried_far, q_back, back_far, e_first_grad,
        (*pairs, vectors, decoded),
    )
    decoded = links.turn(decoded.held)
    corrupted_grad = links.turn(corrupted_low.held).astype(F32)
    pairs = [pair.finish() for pair in pairs]
    feed_grads = links.last_halving(feed_grads)
    d_grads = [pairs[0][:, :part], pairs[0][:, part:], pairs[1][:, :part], pairs[1][:, part:]]
    d_grads += [feed_grads[:, :hidden], feed_grads[:, hidden:]]
    vectors = vectors.finish()

    def cut_vectors(rows):
        return [rows[0, :part], rows[0, part:], rows[1:3].reshape(-1)] + [rows[i] for i in range(3, 9)]

    e_vectors = cut_vectors((vectors + links.swap_core(vectors))[:9])
    d_vectors = (vectors + links.swap_tensor(vectors))[9:18]
    d_vectors = cut_vectors(jnp.concatenate([links.of_chip(d_vectors[:3]), d_vectors[3:]], axis=0))

    left_back = jnp.concatenate([e_fed_low, e_attended_low, score_x], axis=0).T.reshape(links.dp, deep, -1)
    lanes = left_back.shape[2]
    right_back = jnp.concatenate([e_q_grad, e_mixed_grad], axis=1)
    both = lax.all_to_all(jnp.concatenate([left_back, links.copies(right_back, lanes)], axis=1), "dp", 0, 0, tiled=True)
    left_back, right_back = both[:, :deep], links.rows_of(both[:, deep:], kept)
    left_forward = lax.dynamic_slice_in_dim(left_forward, lax.axis_index("dp") * deep, deep, 1)

    def product(left, right):
        return lax.dot_general(left, right, (((0, 2), (0, 1)), ((), ())), preferred_element_type=F32)

    e_outer_grad = product(left_back[:, :, :kept], right_forward[:, :, :hidden])
    e_inner_grad = product(left_forward[:, :, kept : 2 * kept], pre_all)
    e_project_grad = product(left_back[:, :, kept : 2 * kept], right_forward[:, :, hidden : hidden + part])
    e_query_grad = product(left_forward[:, :, :kept], right_back[:, :, :part])
    head_of = jnp.arange(part, dtype=jnp.int32) // HEAD_SIZE

    def by_head(values):
        mine = jnp.arange(heads, dtype=jnp.int32)[None, :, None, None] == head_of[None, None, None, :]
        return jnp.where(mine, values[:, None], jnp.zeros((), LOW)).reshape(links.dp, heads * kept, part)

    e_key_grad = product(left_back[:, :, 2 * kept :], by_head(right_forward[:, :, hidden + part :])) * 0.125
    e_value_grad = product(left_forward[:, :, 2 * kept :], by_head(right_back[:, :, part:]))

    def ordered(matrices, small):
        query_g, key_g, value_g, project_g, inner_g, outer_g = matrices
        query_b, value_b, inner_b, project_b, gain1, shift1, outer_b, gain2, shift2 = small
        return (
            query_g, key_g, value_g, project_g, query_b, value_b, project_b, gain1, shift1,
            inner_g, inner_b, outer_g, outer_b, gain2, shift2,
        )

    return (
        (decoded, passages_grad, corrupted_grad)
        + ordered((e_query_grad, e_key_grad, e_value_grad, e_project_grad, e_inner_grad, e_outer_grad), e_vectors)
        + ordered(d_grads, d_vectors)
    )


def solution(mesh):
    rows = P("dp", None)
    columns, half, whole = P(None, "tensor"), P("tensor"), P()
    block_in = (columns,) * 4 + (half, half, whole, whole, whole, columns, half, columns, whole, whole, whole)
    split = P("dp", "tensor")
    block_out = (split,) * 4 + (half, half, whole, whole, whole, split, half, split, whole, whole, whole)
    return jax.shard_map(
        functools.partial(local, mesh),
        mesh=mesh,
        in_specs=(rows,) * 4 + block_in * 2,
        out_specs=(rows,) * 3 + block_out * 2,
        check_vma=False,
    )
```

```python
import functools

import jax
import jax.numpy as jnp
from jax import lax
from jax.experimental import pallas as pl
from jax.experimental.pallas import tpu as pltpu
from jax.sharding import PartitionSpec as P

HEAD_SIZE = 64
EPSILON = 1e-06
NEGATIVE = -1e30
TILE = 128
CHUNK = 256
STEP = 256
WIDE = 768
AXES = ("dp", "tensor")
VMEM_LIMIT = 56 * 1024 * 1024
F32 = jnp.float32
LOW = jnp.bfloat16


def dot(left, right, contract):
    return lax.dot_general(left, right, ((contract[0:1], contract[1:2]), ((), ())), preferred_element_type=F32)


def call(kernel, name, outs, scalars, arrays, after=(), scratch=(), steps=None, axes=None):
    outs = [jax.ShapeDtypeStruct(shape, kind) for shape, kind in outs]
    count, real = len(scalars) + len(arrays), len(outs)
    passed = [entry for entry in after if hasattr(entry, "held")]
    after = [entry for entry in after if not hasattr(entry, "held")]
    views = [entry.held for entry in passed]
    skip = count + len(views) + len(after)

    def body(*refs):
        kernel(*refs[:count], *refs[skip : skip + real], *refs[skip + real + len(views) :])

    def spec(array):
        if steps is None:
            return pl.BlockSpec(memory_space=pltpu.VMEM)
        axis = axes(array.shape)
        block = [size // steps if d == axis else size for d, size in enumerate(array.shape)]
        return pl.BlockSpec(block, lambda i: tuple(i if d == axis else 0 for d in range(len(block))))

    anywhere = pl.BlockSpec(memory_space=pl.ANY)
    results = pl.pallas_call(
        body,
        out_shape=outs + [jax.ShapeDtypeStruct(view.shape, view.dtype) for view in views],
        grid=() if steps is None else (steps,),
        in_specs=[pl.BlockSpec(memory_space=pltpu.SMEM)] * len(scalars)
        + [spec(array) for array in arrays]
        + [anywhere] * (len(views) + len(after)),
        out_specs=[spec(out) for out in outs] + [anywhere] * len(views),
        scratch_shapes=list(scratch),
        input_output_aliases={count + i: real + i for i in range(len(views))},
        compiler_params=pltpu.CompilerParams(vmem_limit_bytes=VMEM_LIMIT),
        cost_estimate=pl.CostEstimate(flops=0, bytes_accessed=0, transcendentals=0),
        name=name,
    )(*scalars, *arrays, *views, *after)
    for entry, view in zip(passed, results[real:]):
        entry.held = view
    return results[:real]


def copied(arrays, after):
    def kernel(*refs):
        for source, target in zip(refs[: len(arrays)], refs[len(arrays) :]):
            target[...] = source[...]

    return call(kernel, "copied", [(array.shape, array.dtype) for array in arrays], [], arrays, after, steps=4, axes=lambda shape: 0)


def by_rows(rows):
    return lambda shape: 0 if shape[0] == rows else None


def first_step():
    return pl.program_id(0) == 0


def last_step():
    return pl.program_id(0) == pl.num_programs(0) - 1


def over_rows(rows, chunk, body):
    def step(i, carry):
        body(pl.ds(pl.multiple_of(i * chunk, chunk), chunk), i * chunk)
        return carry

    lax.fori_loop(0, rows // chunk, step, 0)


def ends_of(home, own, far):
    ends, end = [], 0
    for p in range(own.shape[1]):
        end = end + (own[0, p] if far is None else jnp.where(home[0] == 1, own[0, p], far[0, p]))
        ends.append(end)
    return ends


def segment_of(place, ends):
    return sum((place >= end).astype(jnp.int32) for end in ends)


def start_of(place, ends):
    start = jnp.zeros_like(place)
    for end in ends:
        start = jnp.where(place >= end, end, start)
    return start


def finish_of(place, ends, rows):
    finish = jnp.full_like(place, rows)
    for end in ends[::-1]:
        finish = jnp.where(place < end, end, finish)
    return finish


def iota(shape, axis):
    return lax.broadcasted_iota(jnp.int32, shape, axis)


def split_low(values):
    first = values.astype(LOW)
    rest = values - first.astype(F32)
    second = rest.astype(LOW)
    third = (rest - second.astype(F32)).astype(LOW)
    return [first, second, third]


def gelu_and_slope(pre):
    phi_sum = 0.5 + 0.5 * lax.erf(pre * 0.7071067811865476)
    density = jnp.exp(-0.5 * pre * pre) * 0.3989422804014327
    return pre * phi_sum, phi_sum + pre * density


def norm(summed):
    center = jnp.mean(summed, axis=-1, keepdims=True)
    offset = summed - center
    scale = lax.rsqrt(jnp.mean(offset * offset, axis=-1, keepdims=True) + EPSILON)
    return offset * scale, scale


def norm_back(grad, unit, scale, gain):
    scaled = grad * gain
    return scale * (
        scaled - jnp.mean(scaled, axis=-1, keepdims=True) - unit * jnp.mean(scaled * unit, axis=-1, keepdims=True)
    )


def column_sum(values):
    return jnp.sum(values, axis=0)


def turned(pieces):
    return jnp.transpose(jnp.concatenate([piece.astype(F32) for piece in pieces], axis=0)).astype(LOW)


def eights(values):
    return jnp.sum(values.reshape(values.shape[0] // 8, 8, values.shape[1]), axis=0)


def encoder_attend(lengths, passages, query, key, value, project, query_bias, value_bias):
    rows, model = passages.shape
    part = query.shape[1]
    heads = part // HEAD_SIZE
    kept = -(-(lengths.shape[1] + 1) // 16) * 16

    def kernel(own, x_ref, q_w, k_w, v_w, p_w, q_b, v_b, xs_ref, q_ref, qk_ref, w_ref, wx_ref, o_ref, share_ref):
        ends = ends_of(None, own, None)
        firsts = [0] + ends
        row, place = iota((kept, rows), 0), iota((kept, rows), 1)
        first = jnp.zeros((kept, rows), jnp.int32)
        for p, at in enumerate(firsts):
            first = jnp.where(row == p, jnp.minimum(at, rows - 1), first)
        xs = dot((place == first).astype(LOW), x_ref[...], (1, 0)).astype(LOW)
        xs_ref[...] = xs
        same = row == segment_of(place, ends)
        queries = (dot(xs, q_w[...], (1, 0)) + q_b[...]).astype(LOW)
        q_ref[...] = queries
        head_of = iota((kept, part), 1) // HEAD_SIZE
        spread = jnp.concatenate(
            [jnp.where(head_of == h, queries, jnp.zeros_like(queries)) for h in range(heads)], axis=0
        )
        q_keys = dot(spread, k_w[...], (1, 1)).astype(LOW)
        qk_ref[...] = q_keys
        score = dot(q_keys, x_ref[...], (1, 1)) * 0.125
        score = jnp.where(same[None], score.reshape(heads, kept, rows), NEGATIVE)
        expo = jnp.exp(score - jnp.max(score, axis=2, keepdims=True))
        weights = (expo / jnp.sum(expo, axis=2, keepdims=True)).reshape(heads * kept, rows)
        w_ref[...] = weights
        low = weights.astype(LOW)
        weight_x = dot(low, x_ref[...], (1, 0)).astype(LOW)
        wx_ref[...] = weight_x
        mixed = dot(weight_x, v_w[...], (1, 0)) + jnp.sum(low.astype(F32), axis=1, keepdims=True) * v_b[...]
        mixed = sum(
            jnp.where(head_of == h, mixed[h * kept : (h + 1) * kept], 0.0) for h in range(heads)
        ).astype(LOW)
        o_ref[...] = mixed
        share_ref[...] = dot(mixed, p_w[...], (1, 1)).astype(LOW)

    return call(
        kernel,
        "encoder_attend",
        [
            ((kept, model), LOW), ((kept, part), LOW), ((heads * kept, model), LOW), ((heads * kept, rows), F32),
            ((heads * kept, model), LOW), ((kept, part), LOW), ((kept, model), LOW),
        ],
        [lengths],
        [passages, query, key, value, project, query_bias, value_bias],
    )


def encoder_feed(xs, share, far, project_bias, gain, shift, inner, inner_bias, outer, weight_x, after):
    kept, model = xs.shape
    hidden = inner.shape[1]

    count = 2 * kept + weight_x.shape[0]

    def kernel(
        xs_ref, s_ref, f_ref, pb, g1, b1, in_w, in_b, out_w, wx_ref,
        unit_ref, scale_ref, y_ref, left_ref, act_ref, slope_ref, share_ref,
    ):
        attended = s_ref[...].astype(F32) + f_ref[...].astype(F32)
        unit, scale = norm(xs_ref[...].astype(F32) + attended + pb[...])
        unit_ref[...] = unit
        scale_ref[...] = scale
        first = unit * g1[...] + b1[...]
        y_ref[...] = first
        first_low = first.astype(LOW)
        left_ref[...] = turned([xs_ref[...], first_low, wx_ref[...]])
        act, slope = gelu_and_slope(dot(first_low, in_w[...], (1, 0)) + in_b[...])
        act_ref[...] = act.astype(LOW)
        slope_ref[...] = slope
        share_ref[...] = dot(act.astype(LOW), out_w[...], (1, 1)).astype(LOW)

    return call(
        kernel,
        "encoder_feed",
        [
            ((kept, model), F32), ((kept, 1), F32), ((kept, model), F32), ((model, count), LOW), ((kept, hidden), LOW),
            ((kept, hidden), F32), ((kept, model), LOW),
        ],
        [],
        [xs, share, far, project_bias, gain, shift, inner, inner_bias, outer, weight_x],
        after,
    )


def encoder_end(first, share, far, outer_bias, gain, shift, after):
    kept, model = first.shape

    def kernel(y_ref, s_ref, f_ref, ob, g2, b2, unit_ref, scale_ref, out_ref):
        fed = s_ref[...].astype(F32) + f_ref[...].astype(F32)
        unit, scale = norm(y_ref[...] + fed + ob[...])
        unit_ref[...] = unit
        scale_ref[...] = scale
        out_ref[...] = unit * g2[...] + b2[...]

    return call(
        kernel,
        "encoder_end",
        [((kept, model), F32), ((kept, 1), F32), ((kept, model), F32)],
        [],
        [first, share, far, outer_bias, gain, shift],
        after,
    )


def encoder_feed_back(totals, unit, scale, gain, outer, slope, inner, after):
    kept, model = totals.shape
    hidden = inner.shape[1]

    def kernel(t_ref, u_ref, r_ref, g2, out_w, slope_ref, in_w, grad_ref, low_ref, pre_ref, sums_ref, bias_ref, share_ref):
        totals, unit = t_ref[...], u_ref[...]
        grad = norm_back(totals, unit, r_ref[...], g2[...])
        grad_ref[...] = grad
        sums_ref[0:1, :] = jnp.sum(grad, axis=0, keepdims=True)
        sums_ref[1:2, :] = jnp.sum(totals * unit, axis=0, keepdims=True)
        sums_ref[2:3, :] = jnp.sum(totals, axis=0, keepdims=True)
        low = grad.astype(LOW)
        low_ref[...] = low
        pre = (dot(low, out_w[...], (1, 0)) * slope_ref[...]).astype(LOW)
        pre_ref[...] = pre
        bias_ref[...] = jnp.sum(pre.astype(F32), axis=0, keepdims=True)
        share_ref[...] = dot(pre, in_w[...], (1, 1)).astype(LOW)

    return call(
        kernel,
        "encoder_feed_back",
        [
            ((kept, model), F32), ((kept, model), LOW), ((kept, hidden), LOW), ((3, model), F32), ((1, hidden), F32),
            ((kept, model), LOW),
        ],
        [],
        [totals, unit, scale, gain, outer, slope, inner],
        after,
    )


def encoder_attend_back(lengths, second, share, far, unit, scale, gain, project, query, key, value, value_bias, passages, weights, q_keys, fed_low, pre_grad, after):
    kept, model = second.shape
    rows = passages.shape[0]
    part = query.shape[1]
    heads = part // HEAD_SIZE
    hidden = pre_grad.shape[1]

    def kernel(
        own, s_grad, s_ref, f_ref, u_ref, r_ref, g1, p_w, q_w, k_w, v_w, v_b, x_ref, w_ref, qk_ref, fed_ref, pre_ref,
        grad_ref, sums_ref, right_ref, left_ref, dq_sum, dv_sum, coef_ref, carried_ref,
    ):
        unit = u_ref[...]
        first_grad = s_grad[...] + (s_ref[...].astype(F32) + f_ref[...].astype(F32))
        grad = norm_back(first_grad, unit, r_ref[...], g1[...])
        grad_ref[...] = grad
        sums_ref[0:1, :] = jnp.sum(grad, axis=0, keepdims=True)
        sums_ref[1:2, :] = jnp.sum(first_grad * unit, axis=0, keepdims=True)
        sums_ref[2:3, :] = jnp.sum(first_grad, axis=0, keepdims=True)
        low = grad.astype(LOW)
        mixed_grad = dot(low, p_w[...], (1, 0)).astype(LOW)
        right_ref[:, part : 2 * part] = mixed_grad
        right_ref[:, 2 * part :] = pre_ref[...]
        head_of = iota((kept, part), 1) // HEAD_SIZE
        spread = jnp.concatenate(
            [jnp.where(head_of == h, mixed_grad, jnp.zeros_like(mixed_grad)) for h in range(heads)], axis=0
        )
        g_values = dot(spread, v_w[...], (1, 1)).astype(LOW)
        weights = w_ref[...]
        weights_low = weights.astype(LOW)
        weight_grad = dot(g_values, x_ref[...], (1, 1)) + jnp.sum(spread.astype(F32) * v_b[...], axis=1, keepdims=True)
        middle = jnp.sum(weights * weight_grad, axis=1, keepdims=True)
        score_grad = (weights * (weight_grad - middle)).astype(LOW)
        score_x = dot(score_grad, x_ref[...], (1, 0)).astype(LOW)
        left_ref[...] = turned([fed_ref[...], low, score_x])
        q_grad = dot(score_x, k_w[...], (1, 0)) * 0.125
        q_grad = sum(jnp.where(head_of == h, q_grad[h * kept : (h + 1) * kept], 0.0) for h in range(heads)).astype(LOW)
        right_ref[:, 0:part] = q_grad
        dq_sum[...] = jnp.sum(q_grad.astype(F32), axis=0, keepdims=True)
        weight_sum = jnp.sum(weights_low.astype(F32), axis=1, keepdims=True)
        dv_sum[...] = jnp.sum(spread.astype(F32) * weight_sum, axis=0, keepdims=True)
        carried_ref[2 * heads * kept :, :] = dot(q_grad, q_w[...], (1, 1)).astype(LOW)
        ends = ends_of(None, own, None)
        same = iota((kept, rows), 0) == segment_of(iota((kept, rows), 1), ends)
        for kind, values in enumerate((score_grad, weights_low)):
            for h in range(heads):
                coefs = jnp.where(same, values[h * kept : (h + 1) * kept].astype(F32), 0.0)
                coef_ref[kind * heads + h : kind * heads + h + 1, :] = jnp.sum(coefs, axis=0, keepdims=True)
        carried_ref[0 : heads * kept, :] = qk_ref[...] * jnp.asarray(0.125, LOW)
        carried_ref[heads * kept : 2 * heads * kept, :] = g_values

    return call(
        kernel,
        "encoder_attend_back",
        [
            ((kept, model), F32), ((3, model), F32), ((kept, 2 * part + hidden), LOW), ((model, (heads + 2) * kept), LOW),
            ((1, part), F32), ((1, part), F32), ((2 * heads, rows), F32), ((2 * heads * kept + kept, model), LOW),
        ],
        [lengths],
        [
            second, share, far, unit, scale, gain, project, query, key, value, value_bias, passages,
            weights, q_keys, fed_low, pre_grad,
        ],
        after,
    )


def passages_back(chip, lengths, coefs, coefs_far, carried, carried_far, picked_grad, after):
    kinds, rows = coefs.shape
    model = carried.shape[1]
    kept = picked_grad.shape[0]
    count = kinds * kept

    def kernel(chip_ref, own, c_ref, cf_ref, v_ref, vf_ref, g_ref, out_ref):
        low_chip = chip_ref[0] == 0
        ends = ends_of(None, own, None)
        row, place = iota((kept, rows), 0), iota((kept, rows), 1)
        same = row == segment_of(place, ends)

        def spread(values):
            return jnp.concatenate(
                [jnp.where(same, values[i : i + 1, :], 0.0).astype(LOW) for i in range(kinds)], axis=0
            )

        mine, other = c_ref[...].astype(F32), cf_ref[...].astype(F32)
        first = spread(jnp.where(low_chip, mine, other))
        second = spread(jnp.where(low_chip, other, mine))
        mine, other = v_ref[0:count, :].astype(F32), vf_ref[0:count, :].astype(F32)
        first = dot(first, jnp.where(low_chip, mine, other).astype(LOW), (0, 0))
        second = dot(second, jnp.where(low_chip, other, mine).astype(LOW), (0, 0))
        leads = (same & (place == start_of(place, ends))).astype(F32).astype(LOW)
        picked = g_ref[...] + (v_ref[count:, :].astype(F32) + vf_ref[count:, :].astype(F32))
        pieces = jnp.concatenate(split_low(picked), axis=0)
        out_ref[...] = (first + second) + dot(jnp.concatenate([leads] * 3, axis=0), pieces, (0, 0))

    return call(
        kernel,
        "passages_back",
        [((rows, model), F32)],
        [chip, lengths],
        [coefs, coefs_far, carried, carried_far, picked_grad],
        after,
    )[0]


def window_sizes(tiles):
    sizes = [2, 3, 4, 6, tiles]
    return sorted({min(s, tiles) for s in sizes})


def for_window(first, last, tiles, body):
    need = last - first
    below = 0
    for size in window_sizes(tiles):
        @pl.when((need > below) & (need <= size))
        def _(size=size):
            body(size, jnp.minimum(first, tiles - size))
        below = size


def tile_window(j, ends, rows):
    low = start_of(j * TILE, ends)
    high = finish_of(j * TILE + TILE - 1, ends, rows)
    return low // TILE, (high + TILE - 1) // TILE


def decoder_attend(home, own, far, corrupt, corrupt_far, encoded, encoded_far, query, key, value, query_bias, value_bias, project, after):
    rows, model = corrupt.shape
    part = query.shape[1]
    kept = encoded.shape[0]
    heads = part // HEAD_SIZE
    tiles = rows // TILE

    def kernel(
        home_ref, own_ref, far_ref, c_ref, cf_ref, e_ref, ef_ref, q_w, k_w, v_w, q_b, v_b, p_w,
        in_ref, low_ref, q_ref, k_ref, v_ref, o_ref, lse_ref, share_ref, table_ref,
    ):
        ends = ends_of(home_ref, own_ref, far_ref)
        at_home = home_ref[0] == 1
        table_ref[...] = jnp.concatenate(split_low(jnp.where(at_home, e_ref[...], ef_ref[...])), axis=0)

        def fill(here, begin):
            place = begin + iota((TILE, 3 * kept), 0)
            lane = iota((TILE, 3 * kept), 1)
            lane = jnp.where(lane >= 2 * kept, lane - 2 * kept, jnp.where(lane >= kept, lane - kept, lane))
            member = (segment_of(place, ends) == lane).astype(F32).astype(LOW)
            corrupt = jnp.where(at_home, c_ref[here, :].astype(F32), cf_ref[here, :].astype(F32))
            d_in = corrupt + dot(member, table_ref[...], (1, 0))
            in_ref[here, :] = d_in
            low_ref[here, :] = d_in.astype(LOW)

        over_rows(rows, TILE, fill)
        q_ref[...] = (dot(low_ref[...], q_w[...], (1, 0)) + q_b[...]).astype(LOW)
        k_ref[...] = dot(low_ref[...], k_w[...], (1, 0)).astype(LOW)
        v_ref[...] = (dot(low_ref[...], v_w[...], (1, 0)) + v_b[...]).astype(LOW)
        first_head = iota((1, TILE), 1) < HEAD_SIZE
        lane = iota((TILE, TILE), 1)

        def step(j, carry):
            def body(size, begin):
                span = size * TILE
                here = pl.ds(pl.multiple_of(j * TILE, TILE), TILE)
                keys = pl.ds(pl.multiple_of(begin * TILE, TILE), span)
                row = j * TILE + iota((TILE, 1), 0)
                row = jnp.concatenate([row, row], axis=0)
                place = begin * TILE + iota((2 * TILE, span), 1)
                inside = (place >= start_of(row, ends)) & (place < finish_of(row, ends, rows))
                logs = jnp.zeros((TILE, TILE), F32)
                for pair in range(part // TILE):
                    cols = pl.ds(pair * TILE, TILE)
                    queries = q_ref[here, cols] * jnp.asarray(0.125, LOW)
                    none = jnp.zeros_like(queries)
                    queries = jnp.concatenate(
                        [jnp.where(first_head, queries, none), jnp.where(first_head, none, queries)], axis=0
                    )
                    score = jnp.where(inside, dot(queries, k_ref[keys, cols], (1, 1)), NEGATIVE)
                    top = jnp.max(score, axis=1, keepdims=True)
                    expo = jnp.exp(score - top)
                    total = jnp.sum(expo, axis=1, keepdims=True)
                    mixed = dot(expo.astype(LOW), v_ref[keys, cols], (1, 0)) * (1.0 / total)
                    log = top + jnp.log(total)
                    logs = jnp.where(lane == 2 * pair, log[0:TILE], logs)
                    logs = jnp.where(lane == 2 * pair + 1, log[TILE:], logs)
                    o_ref[here, cols] = jnp.where(first_head, mixed[0:TILE], mixed[TILE:]).astype(LOW)
                lse_ref[:, here] = jnp.transpose(logs)[0:8, :]

            first, last = tile_window(j, ends, rows)
            for_window(first, last, tiles, body)
            return carry

        lax.fori_loop(0, tiles, step, 0)
        share_ref[...] = dot(o_ref[...], p_w[...], (1, 1)).astype(LOW)

    return call(
        kernel,
        "decoder_attend",
        [
            ((rows, model), F32), ((rows, model), LOW), ((rows, part), LOW), ((rows, part), LOW), ((rows, part), LOW),
            ((rows, part), LOW), ((8, rows), F32), ((rows, model), LOW),
        ],
        [home, own, far],
        [
            corrupt, corrupt_far, encoded, encoded_far, query, key, value, query_bias, value_bias, project,
        ],
        after,
        [pltpu.VMEM((3 * kept, model), LOW)],
    )


def decoder_norm(d_in, share, far, project_bias, gain, shift, after):
    rows, model = d_in.shape

    def kernel(x_ref, s_ref, f_ref, pb, g1, b1, unit_ref, scale_ref, low_ref):
        def part(here, begin):
            attended = s_ref[here, :].astype(F32) + f_ref[here, :].astype(F32)
            unit, scale = norm(x_ref[here, :] + attended + pb[...])
            unit_ref[here, :] = unit
            scale_ref[here, :] = scale
            low_ref[here, :] = (unit * g1[...] + b1[...]).astype(LOW)

        over_rows(unit_ref.shape[0], CHUNK, part)

    return call(
        kernel,
        "decoder_norm",
        [((rows, model), F32), ((rows, 1), F32), ((rows, model), LOW)],
        [],
        [d_in, share, far, project_bias, gain, shift],
        after,
        steps=rows // STEP,
        axes=by_rows(rows),
    )


def decoder_hidden(first_low, inner, inner_bias, after):
    rows, model = first_low.shape
    hidden = inner.shape[1]
    block = 256

    def kernel(low_ref, in_w, in_b, act_ref, slope_ref, pre_ref):
        pre_ref[...] = dot(low_ref[...], in_w[...], (1, 0))

        def activate(here, begin):
            act, slope = gelu_and_slope(pre_ref[here, :] + in_b[...])
            act_ref[here, :] = act.astype(LOW)
            slope_ref[here, :] = slope.astype(LOW)

        over_rows(rows, 64, activate)

    return call(
        kernel,
        "decoder_hidden",
        [((rows, hidden), LOW), ((rows, hidden), LOW)],
        [],
        [first_low, inner, inner_bias[None]],
        after,
        [pltpu.VMEM((rows, block), F32)],
        steps=hidden // block,
        axes=lambda shape: 1 if shape[-1] == hidden else None,
    )


def weight_grads(name, left, right, base):
    rows, model = left.shape
    width = right.shape[1]
    block = WIDE
    steps = width // block
    first = steps if base is None else 0

    def kernel(l_ref, r_ref, *refs):
        refs[-1][...] = dot(l_ref[...], r_ref[...], (0, 0)).astype(LOW)

    return pl.pallas_call(
        kernel,
        out_shape=jax.ShapeDtypeStruct((model, 2 * width), LOW),
        grid=(steps,),
        in_specs=[pl.BlockSpec((rows, model), lambda i: (0, 0)), pl.BlockSpec((rows, block), lambda i: (0, i))]
        + [pl.BlockSpec(memory_space=pl.ANY)] * (base is not None),
        out_specs=pl.BlockSpec((model, block), lambda i: (0, i + first)),
        input_output_aliases={} if base is None else {2: 0},
        compiler_params=pltpu.CompilerParams(vmem_limit_bytes=VMEM_LIMIT),
        cost_estimate=pl.CostEstimate(flops=0, bytes_accessed=0, transcendentals=0),
        name=name,
    )(left, right, *([] if base is None else [base]))


def decoder_norm_back(home, own, far_lengths, unit1, share, far, first_gain, first_shift, outer_bias, gain, shift, cot, cot_far, after):
    rows, model = unit1.shape
    steps = rows // STEP

    def kernel(
        home_ref, own_ref, farl_ref, u_ref, s_ref, f_ref, g1, b1, ob, g2, b2, c_ref, cf_ref,
        out_ref, grad_ref, low_ref, sums_ref, acc_ref,
    ):
        ends = ends_of(home_ref, own_ref, farl_ref)
        at_home = home_ref[0] == 1
        height = u_ref.shape[0]

        @pl.when(first_step())
        def _():
            acc_ref[...] = jnp.zeros_like(acc_ref)

        def part(here, begin):
            fed = s_ref[here, :].astype(F32) + f_ref[here, :].astype(F32)
            first = u_ref[here, :] * g1[...] + b1[...]
            unit, scale = norm(first + fed + ob[...])
            valid = (pl.program_id(0) * height + begin + iota((CHUNK, 1), 0) < ends[-1]).astype(F32)
            out_ref[here, :] = ((unit * g2[...] + b2[...]) * valid).astype(LOW)
            cot = jnp.where(at_home, c_ref[here, :].astype(F32), cf_ref[here, :].astype(F32)) * valid
            grad = norm_back(cot, unit, scale, g2[...])
            grad_ref[here, :] = grad
            low_ref[here, :] = grad.astype(LOW)
            acc_ref[0:8, :] += eights(grad)
            acc_ref[8:16, :] += eights(cot * unit)
            acc_ref[16:24, :] += eights(cot)

        over_rows(height, CHUNK, part)

        @pl.when(last_step())
        def _():
            for i in range(3):
                sums_ref[i : i + 1, :] = jnp.sum(acc_ref[8 * i : 8 * i + 8, :], axis=0, keepdims=True)

    return call(
        kernel,
        "decoder_norm_back",
        [((rows, model), LOW), ((rows, model), F32), ((rows, model), LOW), ((3, model), F32)],
        [home, own, far_lengths],
        [
            unit1, share, far, first_gain, first_shift, outer_bias, gain, shift, cot,
            cot_far,
        ],
        after,
        [pltpu.VMEM((24, model), F32)],
        steps=steps,
        axes=by_rows(rows),
    )


def decoder_feed_back(fed_low, outer, slope, after):
    rows, model = fed_low.shape
    hidden = outer.shape[1]
    block = 256

    def kernel(low_ref, out_w, slope_ref, pre_ref, bias_ref, wide_ref, bias_acc):
        wide_ref[...] = dot(low_ref[...], out_w[...], (1, 0))
        bias_acc[...] = jnp.zeros_like(bias_acc)

        def slopes(here, begin):
            pre = (wide_ref[here, :] * slope_ref[here, :].astype(F32)).astype(LOW)
            pre_ref[here, :] = pre
            bias_acc[...] += eights(pre.astype(F32))

        over_rows(rows, 128, slopes)
        bias_ref[...] = jnp.sum(bias_acc[...], axis=0, keepdims=True)

    return call(
        kernel,
        "decoder_feed_back",
        [((rows, hidden), LOW), ((1, hidden), F32)],
        [],
        [fed_low, outer, slope],
        after,
        [pltpu.VMEM((rows, block), F32), pltpu.VMEM((8, block), F32)],
        steps=hidden // block,
        axes=lambda shape: 1 if shape[-1] == hidden else None,
    )


def decoder_first_back(second, share, far, unit, scale, gain, after):
    rows, model = second.shape

    def kernel(s_grad, s_ref, f_ref, u_ref, r_ref, g1, grad_ref, low_ref, sums_ref, acc_ref):
        @pl.when(first_step())
        def _():
            acc_ref[...] = jnp.zeros_like(acc_ref)

        def part(here, begin):
            unit = u_ref[here, :]
            first_grad = s_grad[here, :] + (s_ref[here, :].astype(F32) + f_ref[here, :].astype(F32))
            grad = norm_back(first_grad, unit, r_ref[here, :], g1[...])
            grad_ref[here, :] = grad
            low_ref[here, :] = grad.astype(LOW)
            acc_ref[0:8, :] += eights(grad)
            acc_ref[8:16, :] += eights(first_grad * unit)
            acc_ref[16:24, :] += eights(first_grad)

        over_rows(u_ref.shape[0], CHUNK, part)

        @pl.when(last_step())
        def _():
            for i in range(3):
                sums_ref[i : i + 1, :] = jnp.sum(acc_ref[8 * i : 8 * i + 8, :], axis=0, keepdims=True)

    return call(
        kernel,
        "decoder_first_back",
        [((rows, model), F32), ((rows, model), LOW), ((3, model), F32)],
        [],
        [second, share, far, unit, scale, gain],
        after,
        [pltpu.VMEM((24, model), F32)],
        steps=rows // STEP,
        axes=by_rows(rows),
    )


def decoder_attend_back(home, own, far_lengths, low, project, lse, query, key, value, query_w, key_w, value_w, after):
    rows, model = low.shape
    part = query.shape[1]
    tiles = rows // TILE

    def kernel(
        home_ref, own_ref, farl_ref, low_ref, p_w, lse_ref, q_ref, k_ref, v_ref, q_w, k_w, v_w,
        all_ref, share_ref, sums_ref, g_ref, kt_ref, dk_sum, dv_sum, acc_ref,
    ):
        ends = ends_of(home_ref, own_ref, farl_ref)
        g_ref[...] = dot(low_ref[...], p_w[...], (1, 0)).astype(LOW)
        first_head = iota((1, TILE), 1) < HEAD_SIZE
        dk_sum[...] = jnp.zeros_like(dk_sum)
        dv_sum[...] = jnp.zeros_like(dv_sum)
        acc_ref[...] = jnp.zeros_like(acc_ref)

        def turn(here, begin):
            for pair in range(part // TILE):
                cols = pl.ds(pair * TILE, TILE)
                kt_ref[cols, here] = jnp.transpose(k_ref[here, cols].astype(F32)).astype(LOW)

        over_rows(rows, TILE, turn)

        def step(j, carry):
            def body(size, begin):
                span = size * TILE
                here = pl.ds(pl.multiple_of(j * TILE, TILE), TILE)
                keys = pl.ds(pl.multiple_of(begin * TILE, TILE), span)
                column = j * TILE + iota((1, TILE), 1)
                column = jnp.concatenate([column, column], axis=1)
                place = begin * TILE + iota((span, 2 * TILE), 0)
                inside = (place >= start_of(column, ends)) & (place < finish_of(column, ends, rows))
                for pair in range(part // TILE):
                    cols = pl.ds(pair * TILE, TILE)
                    queries = q_ref[here, cols] * jnp.asarray(0.125, LOW)
                    grads = g_ref[here, cols]
                    none = jnp.zeros_like(queries)
                    queries = jnp.concatenate(
                        [jnp.where(first_head, queries, none), jnp.where(first_head, none, queries)], axis=0
                    )
                    grads = jnp.concatenate(
                        [jnp.where(first_head, grads, none), jnp.where(first_head, none, grads)], axis=0
                    )
                    log = jnp.concatenate(
                        [lse_ref[2 * pair : 2 * pair + 1, here], lse_ref[2 * pair + 1 : 2 * pair + 2, here]], axis=1
                    )
                    score = dot(k_ref[keys, cols], queries, (1, 1))
                    weight = jnp.exp(jnp.where(inside, score, NEGATIVE) - log)
                    weight_grad = dot(v_ref[keys, cols], grads, (1, 1))
                    middle = jnp.sum(weight * weight_grad, axis=0, keepdims=True)
                    score_grad = (weight * (weight_grad - middle)).astype(LOW)
                    q_grad = dot(kt_ref[cols, keys], score_grad, (1, 0)) * 0.125
                    q_grad = jnp.concatenate([q_grad[0:HEAD_SIZE, 0:TILE], q_grad[HEAD_SIZE:, TILE:]], axis=0)
                    all_ref[here, cols] = jnp.transpose(q_grad).astype(LOW)
                    dk_sum[keys, cols] += dot(score_grad, queries, (1, 0))
                    dv_sum[keys, cols] += dot(weight.astype(LOW), grads, (1, 0))

            first, last = tile_window(j, ends, rows)
            for_window(first, last, tiles, body)
            return carry

        lax.fori_loop(0, tiles, step, 0)

        def close(here, begin):
            all_ref[here, part : 2 * part] = dk_sum[here, :].astype(LOW)
            value_grad = dv_sum[here, :].astype(LOW)
            all_ref[here, 2 * part :] = value_grad
            acc_ref[:, 0:part] += eights(all_ref[here, 0:part].astype(F32))
            acc_ref[:, part:] += eights(value_grad.astype(F32))

        over_rows(rows, TILE, close)
        sums_ref[...] = jnp.sum(acc_ref[...], axis=0, keepdims=True)
        share = dot(all_ref[:, 0:part], q_w[...], (1, 1)) + dot(all_ref[:, part : 2 * part], k_w[...], (1, 1))
        share_ref[...] = (share + dot(all_ref[:, 2 * part :], v_w[...], (1, 1))).astype(LOW)

    return call(
        kernel,
        "decoder_attend_back",
        [((rows, 3 * part), LOW), ((rows, model), LOW), ((1, 2 * part), F32)],
        [home, own, far_lengths],
        [low, project, lse, query, key, value, query_w, key_w, value_w],
        after,
        [
            pltpu.VMEM((rows, part), LOW), pltpu.VMEM((part, rows), LOW), pltpu.VMEM((rows, part), F32),
            pltpu.VMEM((rows, part), F32), pltpu.VMEM((8, 2 * part), F32),
        ],
    )


def attend_weight_grads(d_low, grads, attended_low, mixed, after):
    rows, model = d_low.shape
    part = mixed.shape[1]

    def kernel(x_ref, g_ref, a_ref, o_ref, first_ref, last_ref):
        first_ref[...] = dot(x_ref[...], g_ref[:, 0 : 2 * part], (0, 0)).astype(LOW)
        last_ref[:, 0:part] = dot(x_ref[...], g_ref[:, 2 * part :], (0, 0)).astype(LOW)
        last_ref[:, part:] = dot(a_ref[...], o_ref[...], (0, 0)).astype(LOW)

    return call(
        kernel, "attend_weight_grads", [((model, 2 * part), LOW)] * 2, [], [d_low, grads, attended_low, mixed], after
    )


def pack_vectors(blocks, after):
    model = blocks[0][-1].shape[1]
    part = model // 2
    height = -(-9 * len(blocks) // 8) * 8

    def kernel(*refs):
        out = refs[-1]
        out[...] = jnp.zeros_like(out)
        for i in range(len(blocks)):
            query, value, inner, first, second = refs[5 * i : 5 * i + 5]
            row = 9 * i
            out[row : row + 1, 0:part] = query[...]
            out[row : row + 1, part:] = value[...]
            out[row + 1 : row + 2, :] = inner[:, 0:model]
            out[row + 2 : row + 3, :] = inner[:, model:]
            out[row + 3 : row + 6, :] = first[...]
            out[row + 6 : row + 9, :] = second[...]

    arrays = [array for block in blocks for array in block]
    return call(kernel, "pack_vectors", [((height, model), F32)], [], arrays, after)[0]


def decoder_end(home, own, far_lengths, grad, share, far, kept, after):
    rows, model = grad.shape
    chunk = 256

    def kernel(home_ref, own_ref, farl_ref, g_ref, s_ref, f_ref, low_ref, total_ref):
        ends = ends_of(home_ref, own_ref, farl_ref)

        @pl.when(first_step())
        def _():
            total_ref[...] = jnp.zeros_like(total_ref)

        d_in = g_ref[...] + (s_ref[...].astype(F32) + f_ref[...].astype(F32))
        low_ref[...] = d_in.astype(LOW)
        member = iota((kept, chunk), 0) == segment_of(pl.program_id(0) * chunk + iota((kept, chunk), 1), ends)
        member = member.astype(F32).astype(LOW)
        total_ref[...] += sum(dot(member, piece, (1, 0)) for piece in split_low(d_in))

    return call(
        kernel,
        "decoder_end",
        [((rows, model), LOW), ((kept, model), F32)],
        [home, own, far_lengths],
        [grad, share, far],
        after,
        steps=rows // chunk,
        axes=by_rows(rows),
    )


class Links:
    def __init__(self, mesh):
        self.dp = mesh.shape["dp"]
        self.parts = mesh.shape["tensor"]
        self.bits = (self.dp // 2).bit_length() - 1
        self.core = lax.axis_index("dp") & 1
        self.group = lax.axis_index("dp") >> 1
        self.chip = lax.axis_index("tensor")
        self.home = self.core == self.chip

    def move(self, value, target):
        pairs = []
        for i in range(self.dp):
            for t in range(self.parts):
                place = target(i, t)
                if place is not None:
                    pairs.append((i * self.parts + t, place[0] * self.parts + place[1]))
        return lax.ppermute(value, AXES, pairs)

    def swap_core(self, value):
        return self.move(value, lambda i, t: (i ^ 1, t))

    def swap_tensor(self, value):
        return self.move(value, lambda i, t: (i, t ^ 1))

    def swap_group(self, value, bit):
        return self.move(value, lambda i, t: (i ^ (2 << bit), t))

    def turn(self, value):
        moved = self.move(value, lambda i, t: None if (i & 1) == t else (i ^ 1, t ^ 1))
        return jnp.where(self.home, value, moved)

    def of_chip(self, value):
        return jnp.where(self.home, value, self.swap_core(value))

    def pick(self, value, axis, bit):
        return lax.dynamic_slice_in_dim(value, bit, 1, axis)

    def last_halving(self, value):
        view = value.reshape(2, -1, value.shape[1])
        sent = self.swap_tensor(self.pick(view, 0, 1 - self.chip).astype(LOW))
        return self.turn((self.pick(view, 0, self.chip).astype(F32) + sent.astype(F32))[0].astype(LOW)).astype(F32)

    def copies(self, value, lanes):
        rows = value.shape[0]
        value = value.reshape(rows, -1, lanes).transpose(1, 0, 2).reshape(-1, lanes)
        return jnp.broadcast_to(value[None], (self.dp,) + value.shape)

    def rows_of(self, value, rows):
        lanes = value.shape[2]
        return value.reshape(self.dp, -1, rows, lanes).transpose(0, 2, 1, 3).reshape(self.dp, rows, -1)

    def scatter_groups(self, value):
        cores = [[2 * g + c for g in range(self.dp // 2)] for c in range(2)]
        return lax.psum_scatter(value, "dp", scatter_dimension=0, axis_index_groups=cores, tiled=True)


class Held:
    def __init__(self, view):
        self.held = view


class Total:
    def __init__(self, links, value):
        self.links, self.held, self.done = links, value, 0

    def step(self):
        self.held = self.held + self.links.swap_group(self.held, self.done)
        self.done += 1

    def finish(self):
        while self.done < self.links.bits:
            self.step()
        return self.held


class Halving:
    def __init__(self, links, grad, order):
        self.links, self.order = links, list(order)
        self.width = grad.shape[1]
        self.parts = [(grad.reshape((2,) * links.bits + (-1, self.width)), {})]

    @property
    def held(self):
        return self.parts[-1][0]

    @held.setter
    def held(self, value):
        self.parts[-1] = (value, self.parts[-1][1])

    def cut(self, axis=None, bit=None):
        total = 0
        for view, own in self.parts:
            at = own if axis is None else {**own, axis: bit}
            starts = [at.get(d, 0) if view.shape[d] > 1 else 0 for d in range(view.ndim)]
            sizes = [1 if d in at else view.shape[d] for d in range(view.ndim)]
            total = total + lax.dynamic_slice(view, starts, sizes).astype(F32)
        return total

    def step(self):
        links, step = self.links, self.order.pop(0)
        axis, mine = links.bits - 1 - step, (links.group >> step) & 1
        sent = links.swap_group(self.cut(axis, 1 - mine).astype(LOW), step)
        self.parts = [(view, {**own, axis: mine}) for view, own in self.parts] + [(sent, {})]

    def left(self):
        while self.order:
            self.step()
        return self.cut().reshape(-1, self.width)


def local(mesh, passages, corrupted, lengths, cotangent, *weights):
    (
        e_query, e_key, e_value, e_project, e_query_bias, e_value_bias, e_project_bias, e_first_gain, e_first_shift,
        e_inner, e_inner_bias, e_outer, e_outer_bias, e_second_gain, e_second_shift,
    ) = weights[:15]
    (
        d_query, d_key, d_value, d_project, d_query_bias, d_value_bias, d_project_bias, d_first_gain, d_first_shift,
        d_inner, d_inner_bias, d_outer, d_outer_bias, d_second_gain, d_second_shift,
    ) = weights[15:]
    links = Links(mesh)
    rows, model = passages.shape
    part = e_query.shape[1]
    hidden = e_inner.shape[1]
    heads = part // HEAD_SIZE
    home = links.home.astype(jnp.int32)[None]

    chip = links.chip.astype(jnp.int32)[None]
    deep = model // links.dp

    d_query = links.turn(d_query)
    d_key = links.turn(d_key)
    d_halves = jnp.concatenate([d_query_bias, d_value_bias, d_inner_bias])
    lengths_far = links.swap_core(lengths)
    corrupted_far = links.swap_core(corrupted)

    x_low, e_q, q_keys, e_weights, weight_x, e_mixed, share = encoder_attend(
        lengths, passages, e_query, e_key, e_value, e_project, e_query_bias, e_value_bias
    )
    kept = x_low.shape[0]
    share_far = links.swap_tensor(share)
    d_value = links.turn(d_value)
    d_project = links.turn(d_project)
    d_halves = links.turn(d_halves)
    e_unit1, e_scale1, e_first, left_forward, e_act, e_slope, share = encoder_feed(
        x_low, share, share_far, e_project_bias, e_first_gain, e_first_shift, e_inner, e_inner_bias,
        e_outer, weight_x, (d_query, d_key, d_value, d_project, d_halves, lengths_far),
    )
    inner_held, outer_held = [Held(weight) for weight in copied([d_inner, d_outer], (share_far,))]
    e_unit2, e_scale2, encoded = encoder_end(
        e_first, share, links.swap_tensor(share), e_outer_bias, e_second_gain, e_second_shift,
        (corrupted_far, inner_held, outer_held),
    )
    d_query_bias, d_value_bias, d_inner_bias = d_halves[:part], d_halves[part : 2 * part], d_halves[2 * part :]
    left_forward = lax.all_gather(left_forward, "dp")
    right_forward = lax.all_gather(jnp.concatenate([e_act, e_mixed, e_q], axis=1), "dp")

    encoded_far = links.swap_core(encoded)
    d_inner = links.turn(inner_held.held)
    d_outer = links.turn(outer_held.held)
    d_in, d_low, query, key, value, mixed, lse, share = decoder_attend(
        home, lengths, lengths_far, corrupted, corrupted_far, encoded, encoded_far, d_query, d_key,
        d_value, d_query_bias, d_value_bias, d_project, (),
    )
    cotangent_far = links.swap_core(cotangent)
    unit1, scale1, first_low = decoder_norm(
        d_in, share, links.swap_core(share), d_project_bias, d_first_gain, d_first_shift, ()
    )
    act, slope = decoder_hidden(first_low, d_inner, d_inner_bias, ())
    share = dot(act, d_outer, (1, 1)).astype(LOW)

    decoded, second_grad, fed_low, second_sums = decoder_norm_back(
        home, lengths, lengths_far, unit1, share, links.swap_core(share), d_first_gain, d_first_shift, d_outer_bias,
        d_second_gain, d_second_shift, cotangent, cotangent_far, (),
    )
    decoded = links.turn(decoded)
    outer_grad = weight_grads("outer_grad", fed_low, act, None)
    pre_grad, inner_bias_grad = decoder_feed_back(fed_low, d_outer, slope, (outer_grad,))
    share = dot(pre_grad, d_inner, (1, 1)).astype(LOW)
    share_far = links.swap_core(share)
    feed_grads = weight_grads("inner_grad", first_low, pre_grad, outer_grad)
    first_grad, attended_low, first_sums = decoder_first_back(
        second_grad, share, share_far, unit1, scale1, d_first_gain, (feed_grads,)
    )
    feed_grads = links.scatter_groups(feed_grads)
    attend_grads, share, attend_sums = decoder_attend_back(
        home, lengths, lengths_far, attended_low, d_project, lse, query, key, value, d_query, d_key, d_value,
        (),
    )
    share_far = links.swap_core(share)
    attend_held = Held(attend_grads)
    corrupted_low, totals = decoder_end(
        home, lengths, lengths_far, first_grad, share, share_far, kept, (attend_held, decoded)
    )
    totals = links.turn(totals)
    attend_grads = attend_weight_grads(d_low, attend_held.held, attended_low, mixed, ())
    across = list(range(links.bits))
    pairs = [
        Halving(links, attend_grads[0], across),
        Halving(links, attend_grads[1], across[1:2] + across[:1] + across[2:]),
    ]
    corrupted_low = Held(corrupted_low)

    e_second_grad, e_fed_low, e_pre_grad, e_second_sums, e_inner_bias_grad, share = encoder_feed_back(
        totals, e_unit2, e_scale2, e_second_gain, e_outer, e_slope, e_inner, (*pairs,)
    )
    share_far = links.swap_tensor(share)
    for pair in pairs:
        pair.step()
    (
        e_first_grad, e_first_sums, right_back, left_back, e_query_sum, e_value_sum, coefs, carried,
    ) = encoder_attend_back(
        lengths, e_second_grad, share, share_far, e_unit1, e_scale1, e_first_gain, e_project, e_query,
        e_key, e_value, e_value_bias, passages, e_weights, q_keys, e_fed_low, e_pre_grad, (left_forward, right_forward),
    )
    vectors = pack_vectors([
        (e_query_sum, e_value_sum, e_inner_bias_grad, e_first_sums, e_second_sums),
        (attend_sums[:, :part], attend_sums[:, part:], inner_bias_grad, first_sums, second_sums),
    ], (*pairs,))
    mine = jnp.arange(vectors.shape[0])[:, None] < 9
    vectors = Total(links, vectors + jnp.where(mine, links.swap_core(vectors), links.swap_tensor(vectors)))
    for pair in pairs:
        pair.step()
    coefs = coefs.astype(LOW)
    coefs_far = links.swap_tensor(coefs)
    carried_far = links.swap_tensor(carried)
    left_back = left_back.reshape(links.dp, deep, -1)
    both = jnp.concatenate([left_back, links.copies(right_back, left_back.shape[2])], axis=1)
    both = lax.all_to_all(both, "dp", 0, 0, tiled=True)
    vectors.step()
    passages_grad = passages_back(
        chip, lengths, coefs, coefs_far, carried, carried_far, e_first_grad, (vectors, corrupted_low, *pairs),
    )
    corrupted_grad = links.turn(corrupted_low.held).astype(F32)
    d_grads = links.last_halving(jnp.concatenate([feed_grads.astype(F32)] + [pair.left() for pair in pairs], axis=1))
    edges = [0, hidden, 2 * hidden, 2 * hidden + part, 2 * hidden + 2 * part, 2 * hidden + 3 * part, d_grads.shape[1]]
    d_grads = [d_grads[:, low:high] for low, high in zip(edges, edges[1:])]
    d_grads = d_grads[2:] + d_grads[:2]
    vectors = vectors.finish()

    def cut_vectors(rows):
        return [rows[0, :part], rows[0, part:], rows[1:3].reshape(-1)] + [rows[i] for i in range(3, 9)]

    e_vectors = cut_vectors(vectors[:9])
    d_vectors = vectors[9:18]
    d_vectors = cut_vectors(jnp.concatenate([links.of_chip(d_vectors[:3]), d_vectors[3:]], axis=0))

    left_back, right_back = both[:, :deep], links.rows_of(both[:, deep:], kept)
    left_forward = lax.dynamic_slice_in_dim(left_forward, lax.axis_index("dp") * deep, deep, 1)

    def product(left, right):
        return lax.dot_general(left, right, (((0, 2), (0, 1)), ((), ())), preferred_element_type=F32)

    e_outer_grad = product(left_back[:, :, :kept], right_forward[:, :, :hidden])
    e_inner_grad = product(left_forward[:, :, kept : 2 * kept], right_back[:, :, 2 * part :])
    e_project_grad = product(left_back[:, :, kept : 2 * kept], right_forward[:, :, hidden : hidden + part])
    e_query_grad = product(left_forward[:, :, :kept], right_back[:, :, :part])
    head_of = jnp.arange(part, dtype=jnp.int32) // HEAD_SIZE

    def by_head(values):
        mine = jnp.arange(heads, dtype=jnp.int32)[None, :, None, None] == head_of[None, None, None, :]
        return jnp.where(mine, values[:, None], jnp.zeros((), LOW)).reshape(links.dp, heads * kept, part)

    e_key_grad = product(left_back[:, :, 2 * kept :], by_head(right_forward[:, :, hidden + part :])) * 0.125
    e_value_grad = product(left_forward[:, :, 2 * kept :], by_head(right_back[:, :, part : 2 * part]))

    def ordered(matrices, small):
        query_g, key_g, value_g, project_g, inner_g, outer_g = matrices
        query_b, value_b, inner_b, project_b, gain1, shift1, outer_b, gain2, shift2 = small
        return (
            query_g, key_g, value_g, project_g, query_b, value_b, project_b, gain1, shift1,
            inner_g, inner_b, outer_g, outer_b, gain2, shift2,
        )

    return (
        (decoded, passages_grad, corrupted_grad)
        + ordered((e_query_grad, e_key_grad, e_value_grad, e_project_grad, e_inner_grad, e_outer_grad), e_vectors)
        + ordered(d_grads, d_vectors)
    )


def solution(mesh):
    rows = P("dp", None)
    columns, half, whole = P(None, "tensor"), P("tensor"), P()
    block_in = (columns,) * 4 + (half, half, whole, whole, whole, columns, half, columns, whole, whole, whole)
    split = P("dp", "tensor")
    block_out = (split,) * 4 + (half, half, whole, whole, whole, split, half, split, whole, whole, whole)
    return jax.shard_map(
        functools.partial(local, mesh),
        mesh=mesh,
        in_specs=(rows,) * 4 + block_in * 2,
        out_specs=(rows,) * 3 + block_out * 2,
        check_vma=False,
    )
```

```python
import functools

import jax
import jax.numpy as jnp
from jax import lax
from jax.experimental import pallas as pl
from jax.experimental.pallas import tpu as pltpu
from jax.sharding import PartitionSpec as P

HEAD_SIZE = 64
EPSILON = 1e-06
NEGATIVE = -1e30
TILE = 128
CHUNK = 256
STEP = 256
WIDE = 768
AXES = ("dp", "tensor")
VMEM_LIMIT = 56 * 1024 * 1024
F32 = jnp.float32
LOW = jnp.bfloat16


def dot(left, right, contract):
    return lax.dot_general(left, right, ((contract[0:1], contract[1:2]), ((), ())), preferred_element_type=F32)


def call(kernel, name, outs, scalars, arrays, after=(), scratch=(), steps=None, axes=None):
    outs = [jax.ShapeDtypeStruct(shape, kind) for shape, kind in outs]
    count, real = len(scalars) + len(arrays), len(outs)
    passed = [entry for entry in after if hasattr(entry, "held")]
    after = [entry for entry in after if not hasattr(entry, "held")]
    views = [entry.held for entry in passed]
    skip = count + len(views) + len(after)

    def body(*refs):
        kernel(*refs[:count], *refs[skip : skip + real], *refs[skip + real + len(views) :])

    def spec(array):
        if steps is None:
            return pl.BlockSpec(memory_space=pltpu.VMEM)
        axis = axes(array.shape)
        block = [size // steps if d == axis else size for d, size in enumerate(array.shape)]
        return pl.BlockSpec(block, lambda i: tuple(i if d == axis else 0 for d in range(len(block))))

    anywhere = pl.BlockSpec(memory_space=pl.ANY)
    results = pl.pallas_call(
        body,
        out_shape=outs + [jax.ShapeDtypeStruct(view.shape, view.dtype) for view in views],
        grid=() if steps is None else (steps,),
        in_specs=[pl.BlockSpec(memory_space=pltpu.SMEM)] * len(scalars)
        + [spec(array) for array in arrays]
        + [anywhere] * (len(views) + len(after)),
        out_specs=[spec(out) for out in outs] + [anywhere] * len(views),
        scratch_shapes=list(scratch),
        input_output_aliases={count + i: real + i for i in range(len(views))},
        compiler_params=pltpu.CompilerParams(vmem_limit_bytes=VMEM_LIMIT),
        cost_estimate=pl.CostEstimate(flops=0, bytes_accessed=0, transcendentals=0),
        name=name,
    )(*scalars, *arrays, *views, *after)
    for entry, view in zip(passed, results[real:]):
        entry.held = view
    return results[:real]


def copied(arrays, after):
    def kernel(*refs):
        for source, target in zip(refs[: len(arrays)], refs[len(arrays) :]):
            target[...] = source[...]

    return call(kernel, "copied", [(array.shape, array.dtype) for array in arrays], [], arrays, after, steps=4, axes=lambda shape: 0)


def by_rows(rows):
    return lambda shape: 0 if shape[0] == rows else None


def first_step():
    return pl.program_id(0) == 0


def last_step():
    return pl.program_id(0) == pl.num_programs(0) - 1


def over_rows(rows, chunk, body):
    def step(i, carry):
        body(pl.ds(pl.multiple_of(i * chunk, chunk), chunk), i * chunk)
        return carry

    lax.fori_loop(0, rows // chunk, step, 0)


def ends_of(home, own, far):
    ends, end = [], 0
    for p in range(own.shape[1]):
        end = end + (own[0, p] if far is None else jnp.where(home[0] == 1, own[0, p], far[0, p]))
        ends.append(end)
    return ends


def segment_of(place, ends):
    return sum((place >= end).astype(jnp.int32) for end in ends)


def start_of(place, ends):
    start = jnp.zeros_like(place)
    for end in ends:
        start = jnp.where(place >= end, end, start)
    return start


def finish_of(place, ends, rows):
    finish = jnp.full_like(place, rows)
    for end in ends[::-1]:
        finish = jnp.where(place < end, end, finish)
    return finish


def iota(shape, axis):
    return lax.broadcasted_iota(jnp.int32, shape, axis)


def split_low(values):
    first = values.astype(LOW)
    rest = values - first.astype(F32)
    second = rest.astype(LOW)
    third = (rest - second.astype(F32)).astype(LOW)
    return [first, second, third]


def gelu_and_slope(pre):
    phi_sum = 0.5 + 0.5 * lax.erf(pre * 0.7071067811865476)
    density = jnp.exp(-0.5 * pre * pre) * 0.3989422804014327
    return pre * phi_sum, phi_sum + pre * density


def norm(summed):
    center = jnp.mean(summed, axis=-1, keepdims=True)
    offset = summed - center
    scale = lax.rsqrt(jnp.mean(offset * offset, axis=-1, keepdims=True) + EPSILON)
    return offset * scale, scale


def norm_back(grad, unit, scale, gain):
    scaled = grad * gain
    return scale * (
        scaled - jnp.mean(scaled, axis=-1, keepdims=True) - unit * jnp.mean(scaled * unit, axis=-1, keepdims=True)
    )


def column_sum(values):
    return jnp.sum(values, axis=0)


def turned(pieces):
    return jnp.transpose(jnp.concatenate([piece.astype(F32) for piece in pieces], axis=0)).astype(LOW)


def eights(values):
    return jnp.sum(values.reshape(values.shape[0] // 8, 8, values.shape[1]), axis=0)


def encoder_attend(lengths, passages, query, key, value, project, query_bias, value_bias):
    rows, model = passages.shape
    part = query.shape[1]
    heads = part // HEAD_SIZE
    kept = -(-(lengths.shape[1] + 1) // 16) * 16

    def kernel(own, x_ref, q_w, k_w, v_w, p_w, q_b, v_b, xs_ref, q_ref, qk_ref, w_ref, wx_ref, o_ref, share_ref):
        ends = ends_of(None, own, None)
        firsts = [0] + ends
        row, place = iota((kept, rows), 0), iota((kept, rows), 1)
        first = jnp.zeros((kept, rows), jnp.int32)
        for p, at in enumerate(firsts):
            first = jnp.where(row == p, jnp.minimum(at, rows - 1), first)
        xs = dot((place == first).astype(LOW), x_ref[...], (1, 0)).astype(LOW)
        xs_ref[...] = xs
        same = row == segment_of(place, ends)
        queries = (dot(xs, q_w[...], (1, 0)) + q_b[...]).astype(LOW)
        q_ref[...] = queries
        head_of = iota((kept, part), 1) // HEAD_SIZE
        spread = jnp.concatenate(
            [jnp.where(head_of == h, queries, jnp.zeros_like(queries)) for h in range(heads)], axis=0
        )
        q_keys = dot(spread, k_w[...], (1, 1)).astype(LOW)
        qk_ref[...] = q_keys
        score = dot(q_keys, x_ref[...], (1, 1)) * 0.125
        score = jnp.where(same[None], score.reshape(heads, kept, rows), NEGATIVE)
        expo = jnp.exp(score - jnp.max(score, axis=2, keepdims=True))
        weights = (expo / jnp.sum(expo, axis=2, keepdims=True)).reshape(heads * kept, rows)
        w_ref[...] = weights
        low = weights.astype(LOW)
        weight_x = dot(low, x_ref[...], (1, 0)).astype(LOW)
        wx_ref[...] = weight_x
        mixed = dot(weight_x, v_w[...], (1, 0)) + jnp.sum(low.astype(F32), axis=1, keepdims=True) * v_b[...]
        mixed = sum(
            jnp.where(head_of == h, mixed[h * kept : (h + 1) * kept], 0.0) for h in range(heads)
        ).astype(LOW)
        o_ref[...] = mixed
        share_ref[...] = dot(mixed, p_w[...], (1, 1)).astype(LOW)

    return call(
        kernel,
        "encoder_attend",
        [
            ((kept, model), LOW), ((kept, part), LOW), ((heads * kept, model), LOW), ((heads * kept, rows), F32),
            ((heads * kept, model), LOW), ((kept, part), LOW), ((kept, model), LOW),
        ],
        [lengths],
        [passages, query, key, value, project, query_bias, value_bias],
    )


def encoder_feed(xs, share, far, project_bias, gain, shift, inner, inner_bias, outer, weight_x, after):
    kept, model = xs.shape
    hidden = inner.shape[1]

    count = 2 * kept + weight_x.shape[0]

    def kernel(
        xs_ref, s_ref, f_ref, pb, g1, b1, in_w, in_b, out_w, wx_ref,
        unit_ref, scale_ref, y_ref, left_ref, act_ref, slope_ref, share_ref,
    ):
        attended = s_ref[...].astype(F32) + f_ref[...].astype(F32)
        unit, scale = norm(xs_ref[...].astype(F32) + attended + pb[...])
        unit_ref[...] = unit
        scale_ref[...] = scale
        first = unit * g1[...] + b1[...]
        y_ref[...] = first
        first_low = first.astype(LOW)
        left_ref[...] = turned([xs_ref[...], first_low, wx_ref[...]])
        act, slope = gelu_and_slope(dot(first_low, in_w[...], (1, 0)) + in_b[...])
        act_ref[...] = act.astype(LOW)
        slope_ref[...] = slope
        share_ref[...] = dot(act.astype(LOW), out_w[...], (1, 1)).astype(LOW)

    return call(
        kernel,
        "encoder_feed",
        [
            ((kept, model), F32), ((kept, 1), F32), ((kept, model), F32), ((model, count), LOW), ((kept, hidden), LOW),
            ((kept, hidden), F32), ((kept, model), LOW),
        ],
        [],
        [xs, share, far, project_bias, gain, shift, inner, inner_bias, outer, weight_x],
        after,
    )


def encoder_end(first, share, far, outer_bias, gain, shift, after):
    kept, model = first.shape

    def kernel(y_ref, s_ref, f_ref, ob, g2, b2, unit_ref, scale_ref, out_ref):
        fed = s_ref[...].astype(F32) + f_ref[...].astype(F32)
        unit, scale = norm(y_ref[...] + fed + ob[...])
        unit_ref[...] = unit
        scale_ref[...] = scale
        out_ref[...] = unit * g2[...] + b2[...]

    return call(
        kernel,
        "encoder_end",
        [((kept, model), F32), ((kept, 1), F32), ((kept, model), F32)],
        [],
        [first, share, far, outer_bias, gain, shift],
        after,
    )


def encoder_feed_back(totals, unit, scale, gain, outer, slope, inner, after):
    kept, model = totals.shape
    hidden = inner.shape[1]

    def kernel(t_ref, u_ref, r_ref, g2, out_w, slope_ref, in_w, grad_ref, low_ref, pre_ref, sums_ref, bias_ref, share_ref):
        totals, unit = t_ref[...], u_ref[...]
        grad = norm_back(totals, unit, r_ref[...], g2[...])
        grad_ref[...] = grad
        sums_ref[0:1, :] = jnp.sum(grad, axis=0, keepdims=True)
        sums_ref[1:2, :] = jnp.sum(totals * unit, axis=0, keepdims=True)
        sums_ref[2:3, :] = jnp.sum(totals, axis=0, keepdims=True)
        low = grad.astype(LOW)
        low_ref[...] = low
        pre = (dot(low, out_w[...], (1, 0)) * slope_ref[...]).astype(LOW)
        pre_ref[...] = pre
        bias_ref[...] = jnp.sum(pre.astype(F32), axis=0, keepdims=True)
        share_ref[...] = dot(pre, in_w[...], (1, 1)).astype(LOW)

    return call(
        kernel,
        "encoder_feed_back",
        [
            ((kept, model), F32), ((kept, model), LOW), ((kept, hidden), LOW), ((3, model), F32), ((1, hidden), F32),
            ((kept, model), LOW),
        ],
        [],
        [totals, unit, scale, gain, outer, slope, inner],
        after,
    )


def encoder_attend_back(lengths, second, share, far, unit, scale, gain, project, query, key, value, value_bias, passages, weights, q_keys, fed_low, pre_grad, after):
    kept, model = second.shape
    rows = passages.shape[0]
    part = query.shape[1]
    heads = part // HEAD_SIZE
    hidden = pre_grad.shape[1]

    def kernel(
        own, s_grad, s_ref, f_ref, u_ref, r_ref, g1, p_w, q_w, k_w, v_w, v_b, x_ref, w_ref, qk_ref, fed_ref, pre_ref,
        grad_ref, sums_ref, right_ref, left_ref, dq_sum, dv_sum, coef_ref, carried_ref,
    ):
        unit = u_ref[...]
        first_grad = s_grad[...] + (s_ref[...].astype(F32) + f_ref[...].astype(F32))
        grad = norm_back(first_grad, unit, r_ref[...], g1[...])
        grad_ref[...] = grad
        sums_ref[0:1, :] = jnp.sum(grad, axis=0, keepdims=True)
        sums_ref[1:2, :] = jnp.sum(first_grad * unit, axis=0, keepdims=True)
        sums_ref[2:3, :] = jnp.sum(first_grad, axis=0, keepdims=True)
        low = grad.astype(LOW)
        mixed_grad = dot(low, p_w[...], (1, 0)).astype(LOW)
        right_ref[:, part : 2 * part] = mixed_grad
        right_ref[:, 2 * part :] = pre_ref[...]
        head_of = iota((kept, part), 1) // HEAD_SIZE
        spread = jnp.concatenate(
            [jnp.where(head_of == h, mixed_grad, jnp.zeros_like(mixed_grad)) for h in range(heads)], axis=0
        )
        g_values = dot(spread, v_w[...], (1, 1)).astype(LOW)
        weights = w_ref[...]
        weights_low = weights.astype(LOW)
        weight_grad = dot(g_values, x_ref[...], (1, 1)) + jnp.sum(spread.astype(F32) * v_b[...], axis=1, keepdims=True)
        middle = jnp.sum(weights * weight_grad, axis=1, keepdims=True)
        score_grad = (weights * (weight_grad - middle)).astype(LOW)
        score_x = dot(score_grad, x_ref[...], (1, 0)).astype(LOW)
        left_ref[...] = turned([fed_ref[...], low, score_x])
        q_grad = dot(score_x, k_w[...], (1, 0)) * 0.125
        q_grad = sum(jnp.where(head_of == h, q_grad[h * kept : (h + 1) * kept], 0.0) for h in range(heads)).astype(LOW)
        right_ref[:, 0:part] = q_grad
        dq_sum[...] = jnp.sum(q_grad.astype(F32), axis=0, keepdims=True)
        weight_sum = jnp.sum(weights_low.astype(F32), axis=1, keepdims=True)
        dv_sum[...] = jnp.sum(spread.astype(F32) * weight_sum, axis=0, keepdims=True)
        carried_ref[2 * heads * kept :, :] = dot(q_grad, q_w[...], (1, 1)).astype(LOW)
        ends = ends_of(None, own, None)
        same = iota((kept, rows), 0) == segment_of(iota((kept, rows), 1), ends)
        for kind, values in enumerate((score_grad, weights_low)):
            for h in range(heads):
                coefs = jnp.where(same, values[h * kept : (h + 1) * kept].astype(F32), 0.0)
                coef_ref[kind * heads + h : kind * heads + h + 1, :] = jnp.sum(coefs, axis=0, keepdims=True)
        carried_ref[0 : heads * kept, :] = qk_ref[...] * jnp.asarray(0.125, LOW)
        carried_ref[heads * kept : 2 * heads * kept, :] = g_values

    return call(
        kernel,
        "encoder_attend_back",
        [
            ((kept, model), F32), ((3, model), F32), ((kept, 2 * part + hidden), LOW), ((model, (heads + 2) * kept), LOW),
            ((1, part), F32), ((1, part), F32), ((2 * heads, rows), F32), ((2 * heads * kept + kept, model), LOW),
        ],
        [lengths],
        [
            second, share, far, unit, scale, gain, project, query, key, value, value_bias, passages,
            weights, q_keys, fed_low, pre_grad,
        ],
        after,
    )


def passages_back(chip, lengths, coefs, coefs_far, carried, carried_far, picked_grad, after):
    kinds, rows = coefs.shape
    model = carried.shape[1]
    kept = picked_grad.shape[0]
    count = kinds * kept

    def kernel(chip_ref, own, c_ref, cf_ref, v_ref, vf_ref, g_ref, out_ref):
        low_chip = chip_ref[0] == 0
        ends = ends_of(None, own, None)
        row, place = iota((kept, rows), 0), iota((kept, rows), 1)
        same = row == segment_of(place, ends)

        def spread(values):
            return jnp.concatenate(
                [jnp.where(same, values[i : i + 1, :], 0.0).astype(LOW) for i in range(kinds)], axis=0
            )

        mine, other = c_ref[...].astype(F32), cf_ref[...].astype(F32)
        first = spread(jnp.where(low_chip, mine, other))
        second = spread(jnp.where(low_chip, other, mine))
        mine, other = v_ref[0:count, :].astype(F32), vf_ref[0:count, :].astype(F32)
        first = dot(first, jnp.where(low_chip, mine, other).astype(LOW), (0, 0))
        second = dot(second, jnp.where(low_chip, other, mine).astype(LOW), (0, 0))
        leads = (same & (place == start_of(place, ends))).astype(F32).astype(LOW)
        picked = g_ref[...] + (v_ref[count:, :].astype(F32) + vf_ref[count:, :].astype(F32))
        pieces = jnp.concatenate(split_low(picked), axis=0)
        out_ref[...] = (first + second) + dot(jnp.concatenate([leads] * 3, axis=0), pieces, (0, 0))

    return call(
        kernel,
        "passages_back",
        [((rows, model), F32)],
        [chip, lengths],
        [coefs, coefs_far, carried, carried_far, picked_grad],
        after,
    )[0]


def window_sizes(tiles):
    sizes = [2, 3, 4, 6, tiles]
    return sorted({min(s, tiles) for s in sizes})


def for_window(first, last, tiles, body):
    need = last - first
    below = 0
    for size in window_sizes(tiles):
        @pl.when((need > below) & (need <= size))
        def _(size=size):
            body(size, jnp.minimum(first, tiles - size))
        below = size


def tile_window(j, ends, rows):
    low = start_of(j * TILE, ends)
    high = finish_of(j * TILE + TILE - 1, ends, rows)
    return low // TILE, (high + TILE - 1) // TILE


def decoder_attend(home, own, far, corrupt, corrupt_far, encoded, encoded_far, query, key, value, query_bias, value_bias, project, after):
    rows, model = corrupt.shape
    part = query.shape[1]
    kept = encoded.shape[0]
    heads = part // HEAD_SIZE
    tiles = rows // TILE

    def kernel(
        home_ref, own_ref, far_ref, c_ref, cf_ref, e_ref, ef_ref, q_w, k_w, v_w, q_b, v_b, p_w,
        in_ref, low_ref, q_ref, k_ref, v_ref, o_ref, lse_ref, share_ref, table_ref,
    ):
        ends = ends_of(home_ref, own_ref, far_ref)
        at_home = home_ref[0] == 1
        table_ref[...] = jnp.concatenate(split_low(jnp.where(at_home, e_ref[...], ef_ref[...])), axis=0)

        def fill(here, begin):
            place = begin + iota((TILE, 3 * kept), 0)
            lane = iota((TILE, 3 * kept), 1)
            lane = jnp.where(lane >= 2 * kept, lane - 2 * kept, jnp.where(lane >= kept, lane - kept, lane))
            member = (segment_of(place, ends) == lane).astype(F32).astype(LOW)
            corrupt = jnp.where(at_home, c_ref[here, :].astype(F32), cf_ref[here, :].astype(F32))
            d_in = corrupt + dot(member, table_ref[...], (1, 0))
            in_ref[here, :] = d_in
            low_ref[here, :] = d_in.astype(LOW)

        over_rows(rows, TILE, fill)
        q_ref[...] = (dot(low_ref[...], q_w[...], (1, 0)) + q_b[...]).astype(LOW)
        k_ref[...] = dot(low_ref[...], k_w[...], (1, 0)).astype(LOW)
        v_ref[...] = (dot(low_ref[...], v_w[...], (1, 0)) + v_b[...]).astype(LOW)
        first_head = iota((1, TILE), 1) < HEAD_SIZE
        lane = iota((TILE, TILE), 1)

        def step(j, carry):
            def body(size, begin):
                span = size * TILE
                here = pl.ds(pl.multiple_of(j * TILE, TILE), TILE)
                keys = pl.ds(pl.multiple_of(begin * TILE, TILE), span)
                row = j * TILE + iota((TILE, 1), 0)
                row = jnp.concatenate([row, row], axis=0)
                place = begin * TILE + iota((2 * TILE, span), 1)
                inside = (place >= start_of(row, ends)) & (place < finish_of(row, ends, rows))
                logs = jnp.zeros((TILE, TILE), F32)
                for pair in range(part // TILE):
                    cols = pl.ds(pair * TILE, TILE)
                    queries = q_ref[here, cols] * jnp.asarray(0.125, LOW)
                    none = jnp.zeros_like(queries)
                    queries = jnp.concatenate(
                        [jnp.where(first_head, queries, none), jnp.where(first_head, none, queries)], axis=0
                    )
                    score = jnp.where(inside, dot(queries, k_ref[keys, cols], (1, 1)), NEGATIVE)
                    top = jnp.max(score, axis=1, keepdims=True)
                    expo = jnp.exp(score - top)
                    total = jnp.sum(expo, axis=1, keepdims=True)
                    mixed = dot(expo.astype(LOW), v_ref[keys, cols], (1, 0)) * (1.0 / total)
                    log = top + jnp.log(total)
                    logs = jnp.where(lane == 2 * pair, log[0:TILE], logs)
                    logs = jnp.where(lane == 2 * pair + 1, log[TILE:], logs)
                    o_ref[here, cols] = jnp.where(first_head, mixed[0:TILE], mixed[TILE:]).astype(LOW)
                lse_ref[:, here] = jnp.transpose(logs)[0:8, :]

            first, last = tile_window(j, ends, rows)
            for_window(first, last, tiles, body)
            return carry

        lax.fori_loop(0, tiles, step, 0)
        share_ref[...] = dot(o_ref[...], p_w[...], (1, 1)).astype(LOW)

    return call(
        kernel,
        "decoder_attend",
        [
            ((rows, model), F32), ((rows, model), LOW), ((rows, part), LOW), ((rows, part), LOW), ((rows, part), LOW),
            ((rows, part), LOW), ((8, rows), F32), ((rows, model), LOW),
        ],
        [home, own, far],
        [
            corrupt, corrupt_far, encoded, encoded_far, query, key, value, query_bias, value_bias, project,
        ],
        after,
        [pltpu.VMEM((3 * kept, model), LOW)],
    )


def decoder_norm(d_in, share, far, project_bias, gain, shift, after):
    rows, model = d_in.shape

    def kernel(x_ref, s_ref, f_ref, pb, g1, b1, unit_ref, scale_ref, low_ref):
        def part(here, begin):
            attended = s_ref[here, :].astype(F32) + f_ref[here, :].astype(F32)
            unit, scale = norm(x_ref[here, :] + attended + pb[...])
            unit_ref[here, :] = unit
            scale_ref[here, :] = scale
            low_ref[here, :] = (unit * g1[...] + b1[...]).astype(LOW)

        over_rows(unit_ref.shape[0], CHUNK, part)

    return call(
        kernel,
        "decoder_norm",
        [((rows, model), F32), ((rows, 1), F32), ((rows, model), LOW)],
        [],
        [d_in, share, far, project_bias, gain, shift],
        after,
        steps=rows // STEP,
        axes=by_rows(rows),
    )


def decoder_hidden(first_low, inner, inner_bias, after):
    rows, model = first_low.shape
    hidden = inner.shape[1]
    block = 256

    def kernel(low_ref, in_w, in_b, act_ref, slope_ref, pre_ref):
        pre_ref[...] = dot(low_ref[...], in_w[...], (1, 0))

        def activate(here, begin):
            act, slope = gelu_and_slope(pre_ref[here, :] + in_b[...])
            act_ref[here, :] = act.astype(LOW)
            slope_ref[here, :] = slope.astype(LOW)

        over_rows(rows, 64, activate)

    return call(
        kernel,
        "decoder_hidden",
        [((rows, hidden), LOW), ((rows, hidden), LOW)],
        [],
        [first_low, inner, inner_bias[None]],
        after,
        [pltpu.VMEM((rows, block), F32)],
        steps=hidden // block,
        axes=lambda shape: 1 if shape[-1] == hidden else None,
    )


def weight_grads(name, left, right, base, after=()):
    rows, model = left.shape
    width = right.shape[1]
    block = WIDE
    steps = width // block
    first = steps if base is None else 0

    def kernel(l_ref, r_ref, *refs):
        refs[-1][...] = dot(l_ref[...], r_ref[...], (0, 0)).astype(LOW)

    return pl.pallas_call(
        kernel,
        out_shape=jax.ShapeDtypeStruct((model, 2 * width), LOW),
        grid=(steps,),
        in_specs=[pl.BlockSpec((rows, model), lambda i: (0, 0)), pl.BlockSpec((rows, block), lambda i: (0, i))]
        + [pl.BlockSpec(memory_space=pl.ANY)] * ((base is not None) + len(after)),
        out_specs=pl.BlockSpec((model, block), lambda i: (0, i + first)),
        input_output_aliases={} if base is None else {2: 0},
        compiler_params=pltpu.CompilerParams(vmem_limit_bytes=VMEM_LIMIT),
        cost_estimate=pl.CostEstimate(flops=0, bytes_accessed=0, transcendentals=0),
        name=name,
    )(left, right, *([] if base is None else [base]), *after)


def decoder_norm_back(home, own, far_lengths, unit1, share, far, first_gain, first_shift, outer_bias, gain, shift, cot, cot_far, after):
    rows, model = unit1.shape
    steps = rows // STEP

    def kernel(
        home_ref, own_ref, farl_ref, u_ref, s_ref, f_ref, g1, b1, ob, g2, b2, c_ref, cf_ref,
        out_ref, grad_ref, low_ref, sums_ref, acc_ref,
    ):
        ends = ends_of(home_ref, own_ref, farl_ref)
        at_home = home_ref[0] == 1
        height = u_ref.shape[0]

        @pl.when(first_step())
        def _():
            acc_ref[...] = jnp.zeros_like(acc_ref)

        def part(here, begin):
            fed = s_ref[here, :].astype(F32) + f_ref[here, :].astype(F32)
            first = u_ref[here, :] * g1[...] + b1[...]
            unit, scale = norm(first + fed + ob[...])
            valid = (pl.program_id(0) * height + begin + iota((CHUNK, 1), 0) < ends[-1]).astype(F32)
            out_ref[here, :] = ((unit * g2[...] + b2[...]) * valid).astype(LOW)
            cot = jnp.where(at_home, c_ref[here, :].astype(F32), cf_ref[here, :].astype(F32)) * valid
            grad = norm_back(cot, unit, scale, g2[...])
            grad_ref[here, :] = grad
            low_ref[here, :] = grad.astype(LOW)
            acc_ref[0:8, :] += eights(grad)
            acc_ref[8:16, :] += eights(cot * unit)
            acc_ref[16:24, :] += eights(cot)

        over_rows(height, CHUNK, part)

        @pl.when(last_step())
        def _():
            for i in range(3):
                sums_ref[i : i + 1, :] = jnp.sum(acc_ref[8 * i : 8 * i + 8, :], axis=0, keepdims=True)

    return call(
        kernel,
        "decoder_norm_back",
        [((rows, model), LOW), ((rows, model), F32), ((rows, model), LOW), ((3, model), F32)],
        [home, own, far_lengths],
        [
            unit1, share, far, first_gain, first_shift, outer_bias, gain, shift, cot,
            cot_far,
        ],
        after,
        [pltpu.VMEM((24, model), F32)],
        steps=steps,
        axes=by_rows(rows),
    )


def decoder_feed_back(fed_low, outer, slope, after):
    rows, model = fed_low.shape
    hidden = outer.shape[1]
    block = 256

    def kernel(low_ref, out_w, slope_ref, pre_ref, bias_ref, wide_ref, bias_acc):
        wide_ref[...] = dot(low_ref[...], out_w[...], (1, 0))
        bias_acc[...] = jnp.zeros_like(bias_acc)

        def slopes(here, begin):
            pre = (wide_ref[here, :] * slope_ref[here, :].astype(F32)).astype(LOW)
            pre_ref[here, :] = pre
            bias_acc[...] += eights(pre.astype(F32))

        over_rows(rows, 128, slopes)
        bias_ref[...] = jnp.sum(bias_acc[...], axis=0, keepdims=True)

    return call(
        kernel,
        "decoder_feed_back",
        [((rows, hidden), LOW), ((1, hidden), F32)],
        [],
        [fed_low, outer, slope],
        after,
        [pltpu.VMEM((rows, block), F32), pltpu.VMEM((8, block), F32)],
        steps=hidden // block,
        axes=lambda shape: 1 if shape[-1] == hidden else None,
    )


def decoder_first_back(second, share, far, unit, scale, gain, after):
    rows, model = second.shape

    def kernel(s_grad, s_ref, f_ref, u_ref, r_ref, g1, grad_ref, low_ref, sums_ref, acc_ref):
        @pl.when(first_step())
        def _():
            acc_ref[...] = jnp.zeros_like(acc_ref)

        def part(here, begin):
            unit = u_ref[here, :]
            first_grad = s_grad[here, :] + (s_ref[here, :].astype(F32) + f_ref[here, :].astype(F32))
            grad = norm_back(first_grad, unit, r_ref[here, :], g1[...])
            grad_ref[here, :] = grad
            low_ref[here, :] = grad.astype(LOW)
            acc_ref[0:8, :] += eights(grad)
            acc_ref[8:16, :] += eights(first_grad * unit)
            acc_ref[16:24, :] += eights(first_grad)

        over_rows(u_ref.shape[0], CHUNK, part)

        @pl.when(last_step())
        def _():
            for i in range(3):
                sums_ref[i : i + 1, :] = jnp.sum(acc_ref[8 * i : 8 * i + 8, :], axis=0, keepdims=True)

    return call(
        kernel,
        "decoder_first_back",
        [((rows, model), F32), ((rows, model), LOW), ((3, model), F32)],
        [],
        [second, share, far, unit, scale, gain],
        after,
        [pltpu.VMEM((24, model), F32)],
        steps=rows // STEP,
        axes=by_rows(rows),
    )


def decoder_attend_back(home, own, far_lengths, low, project, lse, query, key, value, query_w, key_w, value_w, after):
    rows, model = low.shape
    part = query.shape[1]
    tiles = rows // TILE

    def kernel(
        home_ref, own_ref, farl_ref, low_ref, p_w, lse_ref, q_ref, k_ref, v_ref, q_w, k_w, v_w,
        all_ref, share_ref, sums_ref, g_ref, kt_ref, dk_sum, dv_sum, acc_ref,
    ):
        ends = ends_of(home_ref, own_ref, farl_ref)
        g_ref[...] = dot(low_ref[...], p_w[...], (1, 0)).astype(LOW)
        first_head = iota((1, TILE), 1) < HEAD_SIZE
        dk_sum[...] = jnp.zeros_like(dk_sum)
        dv_sum[...] = jnp.zeros_like(dv_sum)
        acc_ref[...] = jnp.zeros_like(acc_ref)

        def turn(here, begin):
            for pair in range(part // TILE):
                cols = pl.ds(pair * TILE, TILE)
                kt_ref[cols, here] = jnp.transpose(k_ref[here, cols].astype(F32)).astype(LOW)

        over_rows(rows, TILE, turn)

        def step(j, carry):
            def body(size, begin):
                span = size * TILE
                here = pl.ds(pl.multiple_of(j * TILE, TILE), TILE)
                keys = pl.ds(pl.multiple_of(begin * TILE, TILE), span)
                column = j * TILE + iota((1, TILE), 1)
                column = jnp.concatenate([column, column], axis=1)
                place = begin * TILE + iota((span, 2 * TILE), 0)
                inside = (place >= start_of(column, ends)) & (place < finish_of(column, ends, rows))
                for pair in range(part // TILE):
                    cols = pl.ds(pair * TILE, TILE)
                    queries = q_ref[here, cols] * jnp.asarray(0.125, LOW)
                    grads = g_ref[here, cols]
                    none = jnp.zeros_like(queries)
                    queries = jnp.concatenate(
                        [jnp.where(first_head, queries, none), jnp.where(first_head, none, queries)], axis=0
                    )
                    grads = jnp.concatenate(
                        [jnp.where(first_head, grads, none), jnp.where(first_head, none, grads)], axis=0
                    )
                    log = jnp.concatenate(
                        [lse_ref[2 * pair : 2 * pair + 1, here], lse_ref[2 * pair + 1 : 2 * pair + 2, here]], axis=1
                    )
                    score = dot(k_ref[keys, cols], queries, (1, 1))
                    weight = jnp.exp(jnp.where(inside, score, NEGATIVE) - log)
                    weight_grad = dot(v_ref[keys, cols], grads, (1, 1))
                    middle = jnp.sum(weight * weight_grad, axis=0, keepdims=True)
                    score_grad = (weight * (weight_grad - middle)).astype(LOW)
                    q_grad = dot(kt_ref[cols, keys], score_grad, (1, 0)) * 0.125
                    q_grad = jnp.concatenate([q_grad[0:HEAD_SIZE, 0:TILE], q_grad[HEAD_SIZE:, TILE:]], axis=0)
                    all_ref[here, cols] = jnp.transpose(q_grad).astype(LOW)
                    dk_sum[keys, cols] += dot(score_grad, queries, (1, 0))
                    dv_sum[keys, cols] += dot(weight.astype(LOW), grads, (1, 0))

            first, last = tile_window(j, ends, rows)
            for_window(first, last, tiles, body)
            return carry

        lax.fori_loop(0, tiles, step, 0)

        def close(here, begin):
            all_ref[here, part : 2 * part] = dk_sum[here, :].astype(LOW)
            value_grad = dv_sum[here, :].astype(LOW)
            all_ref[here, 2 * part :] = value_grad
            acc_ref[:, 0:part] += eights(all_ref[here, 0:part].astype(F32))
            acc_ref[:, part:] += eights(value_grad.astype(F32))

        over_rows(rows, TILE, close)
        sums_ref[...] = jnp.sum(acc_ref[...], axis=0, keepdims=True)
        share = dot(all_ref[:, 0:part], q_w[...], (1, 1)) + dot(all_ref[:, part : 2 * part], k_w[...], (1, 1))
        share_ref[...] = (share + dot(all_ref[:, 2 * part :], v_w[...], (1, 1))).astype(LOW)

    return call(
        kernel,
        "decoder_attend_back",
        [((rows, 3 * part), LOW), ((rows, model), LOW), ((1, 2 * part), F32)],
        [home, own, far_lengths],
        [low, project, lse, query, key, value, query_w, key_w, value_w],
        after,
        [
            pltpu.VMEM((rows, part), LOW), pltpu.VMEM((part, rows), LOW), pltpu.VMEM((rows, part), F32),
            pltpu.VMEM((rows, part), F32), pltpu.VMEM((8, 2 * part), F32),
        ],
    )


def attend_weight_grads(d_low, grads, attended_low, mixed, after):
    rows, model = d_low.shape
    part = mixed.shape[1]

    def kernel(x_ref, g_ref, a_ref, o_ref, first_ref, last_ref):
        first_ref[...] = dot(x_ref[...], g_ref[:, 0 : 2 * part], (0, 0)).astype(LOW)
        last_ref[:, 0:part] = dot(x_ref[...], g_ref[:, 2 * part :], (0, 0)).astype(LOW)
        last_ref[:, part:] = dot(a_ref[...], o_ref[...], (0, 0)).astype(LOW)

    return call(
        kernel, "attend_weight_grads", [((model, 2 * part), LOW)] * 2, [], [d_low, grads, attended_low, mixed], after
    )


def pack_vectors(blocks, after):
    model = blocks[0][-1].shape[1]
    part = model // 2
    height = -(-9 * len(blocks) // 8) * 8

    def kernel(*refs):
        out = refs[-1]
        out[...] = jnp.zeros_like(out)
        for i in range(len(blocks)):
            query, value, inner, first, second = refs[5 * i : 5 * i + 5]
            row = 9 * i
            out[row : row + 1, 0:part] = query[...]
            out[row : row + 1, part:] = value[...]
            out[row + 1 : row + 2, :] = inner[:, 0:model]
            out[row + 2 : row + 3, :] = inner[:, model:]
            out[row + 3 : row + 6, :] = first[...]
            out[row + 6 : row + 9, :] = second[...]

    arrays = [array for block in blocks for array in block]
    return call(kernel, "pack_vectors", [((height, model), F32)], [], arrays, after)[0]


def decoder_end(home, own, far_lengths, grad, share, far, kept, after):
    rows, model = grad.shape
    chunk = 256

    def kernel(home_ref, own_ref, farl_ref, g_ref, s_ref, f_ref, low_ref, total_ref):
        ends = ends_of(home_ref, own_ref, farl_ref)

        @pl.when(first_step())
        def _():
            total_ref[...] = jnp.zeros_like(total_ref)

        d_in = g_ref[...] + (s_ref[...].astype(F32) + f_ref[...].astype(F32))
        low_ref[...] = d_in.astype(LOW)
        member = iota((kept, chunk), 0) == segment_of(pl.program_id(0) * chunk + iota((kept, chunk), 1), ends)
        member = member.astype(F32).astype(LOW)
        total_ref[...] += sum(dot(member, piece, (1, 0)) for piece in split_low(d_in))

    return call(
        kernel,
        "decoder_end",
        [((rows, model), LOW), ((kept, model), F32)],
        [home, own, far_lengths],
        [grad, share, far],
        after,
        steps=rows // chunk,
        axes=by_rows(rows),
    )


class Links:
    def __init__(self, mesh):
        self.dp = mesh.shape["dp"]
        self.parts = mesh.shape["tensor"]
        self.bits = (self.dp // 2).bit_length() - 1
        self.core = lax.axis_index("dp") & 1
        self.group = lax.axis_index("dp") >> 1
        self.chip = lax.axis_index("tensor")
        self.home = self.core == self.chip

    def move(self, value, target):
        pairs = []
        for i in range(self.dp):
            for t in range(self.parts):
                place = target(i, t)
                if place is not None:
                    pairs.append((i * self.parts + t, place[0] * self.parts + place[1]))
        return lax.ppermute(value, AXES, pairs)

    def swap_core(self, value):
        return self.move(value, lambda i, t: (i ^ 1, t))

    def swap_tensor(self, value):
        return self.move(value, lambda i, t: (i, t ^ 1))

    def swap_group(self, value, bit):
        return self.move(value, lambda i, t: (i ^ (2 << bit), t))

    def turn(self, value):
        moved = self.move(value, lambda i, t: None if (i & 1) == t else (i ^ 1, t ^ 1))
        return jnp.where(self.home, value, moved)

    def of_chip(self, value):
        return jnp.where(self.home, value, self.swap_core(value))

    def pick(self, value, axis, bit):
        return lax.dynamic_slice_in_dim(value, bit, 1, axis)

    def last_halving(self, value):
        view = value.reshape(2, -1, value.shape[1])
        sent = self.swap_tensor(self.pick(view, 0, 1 - self.chip).astype(LOW))
        return (self.pick(view, 0, self.chip).astype(F32) + sent.astype(F32))[0]

    def copies(self, value, lanes):
        rows = value.shape[0]
        value = value.reshape(rows, -1, lanes).transpose(1, 0, 2).reshape(-1, lanes)
        return jnp.broadcast_to(value[None], (self.dp,) + value.shape)

    def rows_of(self, value, rows):
        lanes = value.shape[2]
        return value.reshape(self.dp, -1, rows, lanes).transpose(0, 2, 1, 3).reshape(self.dp, rows, -1)

    def scatter_groups(self, value):
        cores = [[2 * g + c for g in range(self.dp // 2)] for c in range(2)]
        return lax.psum_scatter(value, "dp", scatter_dimension=0, axis_index_groups=cores, tiled=True)


class Held:
    def __init__(self, view):
        self.held = view


class Total:
    def __init__(self, links, value):
        self.links, self.held, self.done = links, value, 0

    def step(self):
        self.held = self.held + self.links.swap_group(self.held, self.done)
        self.done += 1

    def finish(self):
        while self.done < self.links.bits:
            self.step()
        return self.held


class Halving:
    def __init__(self, links, grad, order):
        self.links, self.order = links, list(order)
        self.width = grad.shape[1]
        self.parts = [(grad.reshape((2,) * links.bits + (2, -1, self.width)), {})]

    @property
    def held(self):
        return self.parts[-1][0]

    @held.setter
    def held(self, value):
        self.parts[-1] = (value, self.parts[-1][1])

    def cut(self, axis=None, bit=None):
        total = 0
        for view, own in self.parts:
            at = own if axis is None else {**own, axis: bit}
            starts = [at.get(d, 0) if view.shape[d] > 1 else 0 for d in range(view.ndim)]
            sizes = [1 if d in at else view.shape[d] for d in range(view.ndim)]
            total = total + lax.dynamic_slice(view, starts, sizes).astype(F32)
        return total

    def step(self):
        links, step = self.links, self.order.pop(0)
        if step < 0:
            axis, mine, swap = links.bits, links.chip, links.swap_tensor
        else:
            axis, mine = links.bits - 1 - step, (links.group >> step) & 1
            swap = lambda value: links.swap_group(value, step)
        sent = swap(self.cut(axis, 1 - mine).astype(LOW))
        self.parts = [(view, {**own, axis: mine}) for view, own in self.parts] + [(sent, {})]

    def left(self):
        while self.order:
            self.step()
        return self.cut().reshape(-1, self.width)


def local(mesh, passages, corrupted, lengths, cotangent, *weights):
    (
        e_query, e_key, e_value, e_project, e_query_bias, e_value_bias, e_project_bias, e_first_gain, e_first_shift,
        e_inner, e_inner_bias, e_outer, e_outer_bias, e_second_gain, e_second_shift,
    ) = weights[:15]
    (
        d_query, d_key, d_value, d_project, d_query_bias, d_value_bias, d_project_bias, d_first_gain, d_first_shift,
        d_inner, d_inner_bias, d_outer, d_outer_bias, d_second_gain, d_second_shift,
    ) = weights[15:]
    links = Links(mesh)
    rows, model = passages.shape
    part = e_query.shape[1]
    hidden = e_inner.shape[1]
    heads = part // HEAD_SIZE
    home = links.home.astype(jnp.int32)[None]

    chip = links.chip.astype(jnp.int32)[None]
    deep = model // links.dp

    d_query = links.turn(d_query)
    d_key = links.turn(d_key)
    d_halves = jnp.concatenate([d_query_bias, d_value_bias, d_inner_bias])
    lengths_far = links.swap_core(lengths)
    corrupted_far = links.swap_core(corrupted)

    x_low, e_q, q_keys, e_weights, weight_x, e_mixed, share = encoder_attend(
        lengths, passages, e_query, e_key, e_value, e_project, e_query_bias, e_value_bias
    )
    kept = x_low.shape[0]
    inner_held, outer_held = [Held(weight) for weight in copied([d_inner, d_outer], (share,))]
    share_far = links.swap_tensor(share)
    d_value = links.turn(d_value)
    d_project = links.turn(d_project)
    d_halves = links.turn(d_halves)
    e_unit1, e_scale1, e_first, left_forward, e_act, e_slope, share = encoder_feed(
        x_low, share, share_far, e_project_bias, e_first_gain, e_first_shift, e_inner, e_inner_bias,
        e_outer, weight_x, (d_query, d_key, d_value, d_project, d_halves, lengths_far),
    )
    e_unit2, e_scale2, encoded = encoder_end(
        e_first, share, links.swap_tensor(share), e_outer_bias, e_second_gain, e_second_shift,
        (corrupted_far, inner_held, outer_held),
    )
    d_query_bias, d_value_bias, d_inner_bias = d_halves[:part], d_halves[part : 2 * part], d_halves[2 * part :]
    left_forward = lax.all_gather(left_forward, "dp")
    right_forward = lax.all_gather(jnp.concatenate([e_act, e_mixed, e_q], axis=1), "dp")

    encoded_far = links.swap_core(encoded)
    d_inner = links.turn(inner_held.held)
    d_outer = links.turn(outer_held.held)
    d_in, d_low, query, key, value, mixed, lse, share = decoder_attend(
        home, lengths, lengths_far, corrupted, corrupted_far, encoded, encoded_far, d_query, d_key,
        d_value, d_query_bias, d_value_bias, d_project, (),
    )
    cotangent_far = links.swap_core(cotangent)
    unit1, scale1, first_low = decoder_norm(
        d_in, share, links.swap_core(share), d_project_bias, d_first_gain, d_first_shift, ()
    )
    act, slope = decoder_hidden(first_low, d_inner, d_inner_bias, ())
    share = dot(act, d_outer, (1, 1)).astype(LOW)

    decoded, second_grad, fed_low, second_sums = decoder_norm_back(
        home, lengths, lengths_far, unit1, share, links.swap_core(share), d_first_gain, d_first_shift, d_outer_bias,
        d_second_gain, d_second_shift, cotangent, cotangent_far, (),
    )
    decoded = links.turn(decoded)
    outer_grad = weight_grads("outer_grad", fed_low, act, None)
    pre_grad, inner_bias_grad = decoder_feed_back(fed_low, d_outer, slope, (outer_grad,))
    share = dot(pre_grad, d_inner, (1, 1)).astype(LOW)
    share_far = links.swap_core(share)
    feed_grads = weight_grads("inner_grad", first_low, pre_grad, outer_grad)
    first_grad, attended_low, first_sums = decoder_first_back(
        second_grad, share, share_far, unit1, scale1, d_first_gain, (feed_grads,)
    )
    feed_grads = links.scatter_groups(feed_grads)
    attend_grads, share, attend_sums = decoder_attend_back(
        home, lengths, lengths_far, attended_low, d_project, lse, query, key, value, d_query, d_key, d_value,
        (),
    )
    share_far = links.swap_core(share)
    attend_held = Held(attend_grads)
    corrupted_low, totals = decoder_end(
        home, lengths, lengths_far, first_grad, share, share_far, kept, (attend_held, decoded)
    )
    totals = links.turn(totals)
    attend_grads = attend_weight_grads(d_low, attend_held.held, attended_low, mixed, ())
    across = list(range(links.bits))
    pairs = [
        Halving(links, attend_grads[0], [-1] + across),
        Halving(links, attend_grads[1], [-1] + across[1:2] + across[:1] + across[2:]),
    ]
    corrupted_low = Held(corrupted_low)

    e_second_grad, e_fed_low, e_pre_grad, e_second_sums, e_inner_bias_grad, share = encoder_feed_back(
        totals, e_unit2, e_scale2, e_second_gain, e_outer, e_slope, e_inner, (*pairs,)
    )
    share_far = links.swap_tensor(share)
    (
        e_first_grad, e_first_sums, right_back, left_back, e_query_sum, e_value_sum, coefs, carried,
    ) = encoder_attend_back(
        lengths, e_second_grad, share, share_far, e_unit1, e_scale1, e_first_gain, e_project, e_query,
        e_key, e_value, e_value_bias, passages, e_weights, q_keys, e_fed_low, e_pre_grad, (left_forward, right_forward, *pairs),
    )
    vectors = pack_vectors([
        (e_query_sum, e_value_sum, e_inner_bias_grad, e_first_sums, e_second_sums),
        (attend_sums[:, :part], attend_sums[:, part:], inner_bias_grad, first_sums, second_sums),
    ], ())
    mine = jnp.arange(vectors.shape[0])[:, None] < 9
    vectors = Total(links, vectors + jnp.where(mine, links.swap_core(vectors), links.swap_tensor(vectors)))
    for pair in pairs:
        pair.step()
    coefs = coefs.astype(LOW)
    coefs_far = links.swap_tensor(coefs)
    carried_far = links.swap_tensor(carried)
    left_back = left_back.reshape(links.dp, deep, -1)
    both = jnp.concatenate([left_back, links.copies(right_back, left_back.shape[2])], axis=1)
    both = lax.all_to_all(both, "dp", 0, 0, tiled=True)
    passages_grad = passages_back(
        chip, lengths, coefs, coefs_far, carried, carried_far, e_first_grad, (corrupted_low, vectors),
    )
    corrupted_grad = links.turn(corrupted_low.held).astype(F32)
    d_grads = jnp.concatenate([links.last_halving(feed_grads)] + [pair.left() for pair in pairs], axis=1)
    d_grads = links.turn(d_grads.astype(LOW)).astype(F32)
    edges = [0, hidden, 2 * hidden, 2 * hidden + part, 2 * hidden + 2 * part, 2 * hidden + 3 * part, d_grads.shape[1]]
    d_grads = [d_grads[:, low:high] for low, high in zip(edges, edges[1:])]
    d_grads = d_grads[2:] + d_grads[:2]
    vectors = vectors.finish()

    def cut_vectors(rows):
        return [rows[0, :part], rows[0, part:], rows[1:3].reshape(-1)] + [rows[i] for i in range(3, 9)]

    e_vectors = cut_vectors(vectors[:9])
    d_vectors = vectors[9:18]
    d_vectors = cut_vectors(jnp.concatenate([links.of_chip(d_vectors[:3]), d_vectors[3:]], axis=0))

    left_back, right_back = both[:, :deep], links.rows_of(both[:, deep:], kept)
    left_forward = lax.dynamic_slice_in_dim(left_forward, lax.axis_index("dp") * deep, deep, 1)

    def product(left, right):
        return lax.dot_general(left, right, (((0, 2), (0, 1)), ((), ())), preferred_element_type=F32)

    e_outer_grad = product(left_back[:, :, :kept], right_forward[:, :, :hidden])
    e_inner_grad = product(left_forward[:, :, kept : 2 * kept], right_back[:, :, 2 * part :])
    e_project_grad = product(left_back[:, :, kept : 2 * kept], right_forward[:, :, hidden : hidden + part])
    e_query_grad = product(left_forward[:, :, :kept], right_back[:, :, :part])
    head_of = jnp.arange(part, dtype=jnp.int32) // HEAD_SIZE

    def by_head(values):
        mine = jnp.arange(heads, dtype=jnp.int32)[None, :, None, None] == head_of[None, None, None, :]
        return jnp.where(mine, values[:, None], jnp.zeros((), LOW)).reshape(links.dp, heads * kept, part)

    e_key_grad = product(left_back[:, :, 2 * kept :], by_head(right_forward[:, :, hidden + part :])) * 0.125
    e_value_grad = product(left_forward[:, :, 2 * kept :], by_head(right_back[:, :, part : 2 * part]))

    def ordered(matrices, small):
        query_g, key_g, value_g, project_g, inner_g, outer_g = matrices
        query_b, value_b, inner_b, project_b, gain1, shift1, outer_b, gain2, shift2 = small
        return (
            query_g, key_g, value_g, project_g, query_b, value_b, project_b, gain1, shift1,
            inner_g, inner_b, outer_g, outer_b, gain2, shift2,
        )

    return (
        (decoded, passages_grad, corrupted_grad)
        + ordered((e_query_grad, e_key_grad, e_value_grad, e_project_grad, e_inner_grad, e_outer_grad), e_vectors)
        + ordered(d_grads, d_vectors)
    )


def solution(mesh):
    rows = P("dp", None)
    columns, half, whole = P(None, "tensor"), P("tensor"), P()
    block_in = (columns,) * 4 + (half, half, whole, whole, whole, columns, half, columns, whole, whole, whole)
    split = P("dp", "tensor")
    block_out = (split,) * 4 + (half, half, whole, whole, whole, split, half, split, whole, whole, whole)
    return jax.shard_map(
        functools.partial(local, mesh),
        mesh=mesh,
        in_specs=(rows,) * 4 + block_in * 2,
        out_specs=(rows,) * 3 + block_out * 2,
        check_vma=False,
    )
```

```python
import functools

import jax
import jax.numpy as jnp
from jax import lax
from jax.experimental import pallas as pl
from jax.experimental.pallas import tpu as pltpu
from jax.sharding import PartitionSpec as P

HEAD_SIZE = 64
EPSILON = 1e-06
NEGATIVE = -1e30
TILE = 128
CHUNK = 256
STEP = 256
WIDE = 768
AXES = ("dp", "tensor")
VMEM_LIMIT = 56 * 1024 * 1024
F32 = jnp.float32
LOW = jnp.bfloat16


def dot(left, right, contract):
    return lax.dot_general(left, right, ((contract[0:1], contract[1:2]), ((), ())), preferred_element_type=F32)


def call(kernel, name, outs, scalars, arrays, after=(), scratch=(), steps=None, axes=None):
    outs = [jax.ShapeDtypeStruct(shape, kind) for shape, kind in outs]
    count, real = len(scalars) + len(arrays), len(outs)
    passed = [entry for entry in after if hasattr(entry, "held")]
    after = [entry for entry in after if not hasattr(entry, "held")]
    views = [entry.held for entry in passed]
    skip = count + len(views) + len(after)

    def body(*refs):
        kernel(*refs[:count], *refs[skip : skip + real], *refs[skip + real + len(views) :])

    def spec(array):
        if steps is None:
            return pl.BlockSpec(memory_space=pltpu.VMEM)
        axis = axes(array.shape)
        block = [size // steps if d == axis else size for d, size in enumerate(array.shape)]
        return pl.BlockSpec(block, lambda i: tuple(i if d == axis else 0 for d in range(len(block))))

    anywhere = pl.BlockSpec(memory_space=pl.ANY)
    results = pl.pallas_call(
        body,
        out_shape=outs + [jax.ShapeDtypeStruct(view.shape, view.dtype) for view in views],
        grid=() if steps is None else (steps,),
        in_specs=[pl.BlockSpec(memory_space=pltpu.SMEM)] * len(scalars)
        + [spec(array) for array in arrays]
        + [anywhere] * (len(views) + len(after)),
        out_specs=[spec(out) for out in outs] + [anywhere] * len(views),
        scratch_shapes=list(scratch),
        input_output_aliases={count + i: real + i for i in range(len(views))},
        compiler_params=pltpu.CompilerParams(vmem_limit_bytes=VMEM_LIMIT),
        cost_estimate=pl.CostEstimate(flops=0, bytes_accessed=0, transcendentals=0),
        name=name,
    )(*scalars, *arrays, *views, *after)
    for entry, view in zip(passed, results[real:]):
        entry.held = view
    return results[:real]


def copied(arrays, after):
    def kernel(*refs):
        for source, target in zip(refs[: len(arrays)], refs[len(arrays) :]):
            target[...] = source[...]

    return call(kernel, "copied", [(array.shape, array.dtype) for array in arrays], [], arrays, after, steps=4, axes=lambda shape: 0)


def by_rows(rows):
    return lambda shape: 0 if shape[0] == rows else None


def first_step():
    return pl.program_id(0) == 0


def last_step():
    return pl.program_id(0) == pl.num_programs(0) - 1


def over_rows(rows, chunk, body):
    def step(i, carry):
        body(pl.ds(pl.multiple_of(i * chunk, chunk), chunk), i * chunk)
        return carry

    lax.fori_loop(0, rows // chunk, step, 0)


def ends_of(home, own, far):
    ends, end = [], 0
    for p in range(own.shape[1]):
        end = end + (own[0, p] if far is None else jnp.where(home[0] == 1, own[0, p], far[0, p]))
        ends.append(end)
    return ends


def segment_of(place, ends):
    return sum((place >= end).astype(jnp.int32) for end in ends)


def start_of(place, ends):
    start = jnp.zeros_like(place)
    for end in ends:
        start = jnp.where(place >= end, end, start)
    return start


def finish_of(place, ends, rows):
    finish = jnp.full_like(place, rows)
    for end in ends[::-1]:
        finish = jnp.where(place < end, end, finish)
    return finish


def iota(shape, axis):
    return lax.broadcasted_iota(jnp.int32, shape, axis)


def split_low(values):
    first = values.astype(LOW)
    rest = values - first.astype(F32)
    second = rest.astype(LOW)
    third = (rest - second.astype(F32)).astype(LOW)
    return [first, second, third]


def gelu_and_slope(pre):
    phi_sum = 0.5 + 0.5 * lax.erf(pre * 0.7071067811865476)
    density = jnp.exp(-0.5 * pre * pre) * 0.3989422804014327
    return pre * phi_sum, phi_sum + pre * density


def norm(summed):
    center = jnp.mean(summed, axis=-1, keepdims=True)
    offset = summed - center
    scale = lax.rsqrt(jnp.mean(offset * offset, axis=-1, keepdims=True) + EPSILON)
    return offset * scale, scale


def norm_back(grad, unit, scale, gain):
    scaled = grad * gain
    return scale * (
        scaled - jnp.mean(scaled, axis=-1, keepdims=True) - unit * jnp.mean(scaled * unit, axis=-1, keepdims=True)
    )


def column_sum(values):
    return jnp.sum(values, axis=0)


def turned(pieces):
    return jnp.transpose(jnp.concatenate([piece.astype(F32) for piece in pieces], axis=0)).astype(LOW)


def eights(values):
    return jnp.sum(values.reshape(values.shape[0] // 8, 8, values.shape[1]), axis=0)


def encoder_attend(lengths, passages, query, key, value, project, query_bias, value_bias):
    rows, model = passages.shape
    part = query.shape[1]
    heads = part // HEAD_SIZE
    kept = -(-(lengths.shape[1] + 1) // 16) * 16

    def kernel(own, x_ref, q_w, k_w, v_w, p_w, q_b, v_b, xs_ref, q_ref, qk_ref, w_ref, wx_ref, o_ref, share_ref):
        ends = ends_of(None, own, None)
        firsts = [0] + ends
        row, place = iota((kept, rows), 0), iota((kept, rows), 1)
        first = jnp.zeros((kept, rows), jnp.int32)
        for p, at in enumerate(firsts):
            first = jnp.where(row == p, jnp.minimum(at, rows - 1), first)
        xs = dot((place == first).astype(LOW), x_ref[...], (1, 0)).astype(LOW)
        xs_ref[...] = xs
        same = row == segment_of(place, ends)
        queries = (dot(xs, q_w[...], (1, 0)) + q_b[...]).astype(LOW)
        q_ref[...] = queries
        head_of = iota((kept, part), 1) // HEAD_SIZE
        spread = jnp.concatenate(
            [jnp.where(head_of == h, queries, jnp.zeros_like(queries)) for h in range(heads)], axis=0
        )
        q_keys = dot(spread, k_w[...], (1, 1)).astype(LOW)
        qk_ref[...] = q_keys
        score = dot(q_keys, x_ref[...], (1, 1)) * 0.125
        score = jnp.where(same[None], score.reshape(heads, kept, rows), NEGATIVE)
        expo = jnp.exp(score - jnp.max(score, axis=2, keepdims=True))
        weights = (expo / jnp.sum(expo, axis=2, keepdims=True)).reshape(heads * kept, rows)
        w_ref[...] = weights
        low = weights.astype(LOW)
        weight_x = dot(low, x_ref[...], (1, 0)).astype(LOW)
        wx_ref[...] = weight_x
        mixed = dot(weight_x, v_w[...], (1, 0)) + jnp.sum(low.astype(F32), axis=1, keepdims=True) * v_b[...]
        mixed = sum(
            jnp.where(head_of == h, mixed[h * kept : (h + 1) * kept], 0.0) for h in range(heads)
        ).astype(LOW)
        o_ref[...] = mixed
        share_ref[...] = dot(mixed, p_w[...], (1, 1)).astype(LOW)

    return call(
        kernel,
        "encoder_attend",
        [
            ((kept, model), LOW), ((kept, part), LOW), ((heads * kept, model), LOW), ((heads * kept, rows), F32),
            ((heads * kept, model), LOW), ((kept, part), LOW), ((kept, model), LOW),
        ],
        [lengths],
        [passages, query, key, value, project, query_bias, value_bias],
    )


def encoder_feed(xs, share, far, project_bias, gain, shift, inner, inner_bias, outer, weight_x, after):
    kept, model = xs.shape
    hidden = inner.shape[1]

    count = 2 * kept + weight_x.shape[0]

    def kernel(
        xs_ref, s_ref, f_ref, pb, g1, b1, in_w, in_b, out_w, wx_ref,
        unit_ref, scale_ref, y_ref, left_ref, act_ref, slope_ref, share_ref,
    ):
        attended = s_ref[...].astype(F32) + f_ref[...].astype(F32)
        unit, scale = norm(xs_ref[...].astype(F32) + attended + pb[...])
        unit_ref[...] = unit
        scale_ref[...] = scale
        first = unit * g1[...] + b1[...]
        y_ref[...] = first
        first_low = first.astype(LOW)
        left_ref[...] = turned([xs_ref[...], first_low, wx_ref[...]])
        act, slope = gelu_and_slope(dot(first_low, in_w[...], (1, 0)) + in_b[...])
        act_ref[...] = act.astype(LOW)
        slope_ref[...] = slope
        share_ref[...] = dot(act.astype(LOW), out_w[...], (1, 1)).astype(LOW)

    return call(
        kernel,
        "encoder_feed",
        [
            ((kept, model), F32), ((kept, 1), F32), ((kept, model), F32), ((model, count), LOW), ((kept, hidden), LOW),
            ((kept, hidden), F32), ((kept, model), LOW),
        ],
        [],
        [xs, share, far, project_bias, gain, shift, inner, inner_bias, outer, weight_x],
        after,
    )


def encoder_end(first, share, far, outer_bias, gain, shift, after):
    kept, model = first.shape

    def kernel(y_ref, s_ref, f_ref, ob, g2, b2, unit_ref, scale_ref, out_ref):
        fed = s_ref[...].astype(F32) + f_ref[...].astype(F32)
        unit, scale = norm(y_ref[...] + fed + ob[...])
        unit_ref[...] = unit
        scale_ref[...] = scale
        out_ref[...] = unit * g2[...] + b2[...]

    return call(
        kernel,
        "encoder_end",
        [((kept, model), F32), ((kept, 1), F32), ((kept, model), F32)],
        [],
        [first, share, far, outer_bias, gain, shift],
        after,
    )


def encoder_feed_back(totals, unit, scale, gain, outer, slope, inner, after):
    kept, model = totals.shape
    hidden = inner.shape[1]

    def kernel(t_ref, u_ref, r_ref, g2, out_w, slope_ref, in_w, grad_ref, low_ref, pre_ref, sums_ref, bias_ref, share_ref):
        totals, unit = t_ref[...], u_ref[...]
        grad = norm_back(totals, unit, r_ref[...], g2[...])
        grad_ref[...] = grad
        sums_ref[0:1, :] = jnp.sum(grad, axis=0, keepdims=True)
        sums_ref[1:2, :] = jnp.sum(totals * unit, axis=0, keepdims=True)
        sums_ref[2:3, :] = jnp.sum(totals, axis=0, keepdims=True)
        low = grad.astype(LOW)
        low_ref[...] = low
        pre = (dot(low, out_w[...], (1, 0)) * slope_ref[...]).astype(LOW)
        pre_ref[...] = pre
        bias_ref[...] = jnp.sum(pre.astype(F32), axis=0, keepdims=True)
        share_ref[...] = dot(pre, in_w[...], (1, 1)).astype(LOW)

    return call(
        kernel,
        "encoder_feed_back",
        [
            ((kept, model), F32), ((kept, model), LOW), ((kept, hidden), LOW), ((3, model), F32), ((1, hidden), F32),
            ((kept, model), LOW),
        ],
        [],
        [totals, unit, scale, gain, outer, slope, inner],
        after,
    )


def encoder_attend_back(lengths, second, share, far, unit, scale, gain, project, query, key, value, value_bias, passages, weights, q_keys, fed_low, pre_grad, after):
    kept, model = second.shape
    rows = passages.shape[0]
    part = query.shape[1]
    heads = part // HEAD_SIZE
    hidden = pre_grad.shape[1]

    def kernel(
        own, s_grad, s_ref, f_ref, u_ref, r_ref, g1, p_w, q_w, k_w, v_w, v_b, x_ref, w_ref, qk_ref, fed_ref, pre_ref,
        grad_ref, sums_ref, right_ref, left_ref, dq_sum, dv_sum, coef_ref, carried_ref,
    ):
        unit = u_ref[...]
        first_grad = s_grad[...] + (s_ref[...].astype(F32) + f_ref[...].astype(F32))
        grad = norm_back(first_grad, unit, r_ref[...], g1[...])
        grad_ref[...] = grad
        sums_ref[0:1, :] = jnp.sum(grad, axis=0, keepdims=True)
        sums_ref[1:2, :] = jnp.sum(first_grad * unit, axis=0, keepdims=True)
        sums_ref[2:3, :] = jnp.sum(first_grad, axis=0, keepdims=True)
        low = grad.astype(LOW)
        mixed_grad = dot(low, p_w[...], (1, 0)).astype(LOW)
        right_ref[:, part : 2 * part] = mixed_grad
        right_ref[:, 2 * part :] = pre_ref[...]
        head_of = iota((kept, part), 1) // HEAD_SIZE
        spread = jnp.concatenate(
            [jnp.where(head_of == h, mixed_grad, jnp.zeros_like(mixed_grad)) for h in range(heads)], axis=0
        )
        g_values = dot(spread, v_w[...], (1, 1)).astype(LOW)
        weights = w_ref[...]
        weights_low = weights.astype(LOW)
        weight_grad = dot(g_values, x_ref[...], (1, 1)) + jnp.sum(spread.astype(F32) * v_b[...], axis=1, keepdims=True)
        middle = jnp.sum(weights * weight_grad, axis=1, keepdims=True)
        score_grad = (weights * (weight_grad - middle)).astype(LOW)
        score_x = dot(score_grad, x_ref[...], (1, 0)).astype(LOW)
        left_ref[...] = turned([fed_ref[...], low, score_x])
        q_grad = dot(score_x, k_w[...], (1, 0)) * 0.125
        q_grad = sum(jnp.where(head_of == h, q_grad[h * kept : (h + 1) * kept], 0.0) for h in range(heads)).astype(LOW)
        right_ref[:, 0:part] = q_grad
        dq_sum[...] = jnp.sum(q_grad.astype(F32), axis=0, keepdims=True)
        weight_sum = jnp.sum(weights_low.astype(F32), axis=1, keepdims=True)
        dv_sum[...] = jnp.sum(spread.astype(F32) * weight_sum, axis=0, keepdims=True)
        carried_ref[2 * heads * kept :, :] = dot(q_grad, q_w[...], (1, 1)).astype(LOW)
        ends = ends_of(None, own, None)
        same = iota((kept, rows), 0) == segment_of(iota((kept, rows), 1), ends)
        for kind, values in enumerate((score_grad, weights_low)):
            for h in range(heads):
                coefs = jnp.where(same, values[h * kept : (h + 1) * kept].astype(F32), 0.0)
                coef_ref[kind * heads + h : kind * heads + h + 1, :] = jnp.sum(coefs, axis=0, keepdims=True)
        carried_ref[0 : heads * kept, :] = qk_ref[...] * jnp.asarray(0.125, LOW)
        carried_ref[heads * kept : 2 * heads * kept, :] = g_values

    return call(
        kernel,
        "encoder_attend_back",
        [
            ((kept, model), F32), ((3, model), F32), ((kept, 2 * part + hidden), LOW), ((model, (heads + 2) * kept), LOW),
            ((1, part), F32), ((1, part), F32), ((2 * heads, rows), F32), ((2 * heads * kept + kept, model), LOW),
        ],
        [lengths],
        [
            second, share, far, unit, scale, gain, project, query, key, value, value_bias, passages,
            weights, q_keys, fed_low, pre_grad,
        ],
        after,
    )


def passages_back(chip, lengths, coefs, coefs_far, carried, carried_far, picked_grad, after):
    kinds, rows = coefs.shape
    model = carried.shape[1]
    kept = picked_grad.shape[0]
    count = kinds * kept

    def kernel(chip_ref, own, c_ref, cf_ref, v_ref, vf_ref, g_ref, out_ref):
        low_chip = chip_ref[0] == 0
        ends = ends_of(None, own, None)
        row, place = iota((kept, rows), 0), iota((kept, rows), 1)
        same = row == segment_of(place, ends)

        def spread(values):
            return jnp.concatenate(
                [jnp.where(same, values[i : i + 1, :], 0.0).astype(LOW) for i in range(kinds)], axis=0
            )

        mine, other = c_ref[...].astype(F32), cf_ref[...].astype(F32)
        first = spread(jnp.where(low_chip, mine, other))
        second = spread(jnp.where(low_chip, other, mine))
        mine, other = v_ref[0:count, :].astype(F32), vf_ref[0:count, :].astype(F32)
        first = dot(first, jnp.where(low_chip, mine, other).astype(LOW), (0, 0))
        second = dot(second, jnp.where(low_chip, other, mine).astype(LOW), (0, 0))
        leads = (same & (place == start_of(place, ends))).astype(F32).astype(LOW)
        picked = g_ref[...] + (v_ref[count:, :].astype(F32) + vf_ref[count:, :].astype(F32))
        pieces = jnp.concatenate(split_low(picked), axis=0)
        out_ref[...] = (first + second) + dot(jnp.concatenate([leads] * 3, axis=0), pieces, (0, 0))

    return call(
        kernel,
        "passages_back",
        [((rows, model), F32)],
        [chip, lengths],
        [coefs, coefs_far, carried, carried_far, picked_grad],
        after,
    )[0]


def window_sizes(tiles):
    sizes = [2, 3, 4, 6, tiles]
    return sorted({min(s, tiles) for s in sizes})


def for_window(first, last, tiles, body):
    need = last - first
    below = 0
    for size in window_sizes(tiles):
        @pl.when((need > below) & (need <= size))
        def _(size=size):
            body(size, jnp.minimum(first, tiles - size))
        below = size


def tile_window(j, ends, rows):
    low = start_of(j * TILE, ends)
    high = finish_of(j * TILE + TILE - 1, ends, rows)
    return low // TILE, (high + TILE - 1) // TILE


def decoder_attend(home, own, far, corrupt, corrupt_far, encoded, encoded_far, query, key, value, query_bias, value_bias, project, after):
    rows, model = corrupt.shape
    part = query.shape[1]
    kept = encoded.shape[0]
    heads = part // HEAD_SIZE
    tiles = rows // TILE

    def kernel(
        home_ref, own_ref, far_ref, c_ref, cf_ref, e_ref, ef_ref, q_w, k_w, v_w, q_b, v_b, p_w,
        in_ref, low_ref, q_ref, k_ref, v_ref, o_ref, lse_ref, share_ref, table_ref,
    ):
        ends = ends_of(home_ref, own_ref, far_ref)
        at_home = home_ref[0] == 1
        table_ref[...] = jnp.concatenate(split_low(jnp.where(at_home, e_ref[...], ef_ref[...])), axis=0)

        def fill(here, begin):
            place = begin + iota((TILE, 3 * kept), 0)
            lane = iota((TILE, 3 * kept), 1)
            lane = jnp.where(lane >= 2 * kept, lane - 2 * kept, jnp.where(lane >= kept, lane - kept, lane))
            member = (segment_of(place, ends) == lane).astype(F32).astype(LOW)
            corrupt = jnp.where(at_home, c_ref[here, :].astype(F32), cf_ref[here, :].astype(F32))
            d_in = corrupt + dot(member, table_ref[...], (1, 0))
            in_ref[here, :] = d_in
            low_ref[here, :] = d_in.astype(LOW)

        over_rows(rows, TILE, fill)
        q_ref[...] = (dot(low_ref[...], q_w[...], (1, 0)) + q_b[...]).astype(LOW)
        k_ref[...] = dot(low_ref[...], k_w[...], (1, 0)).astype(LOW)
        v_ref[...] = (dot(low_ref[...], v_w[...], (1, 0)) + v_b[...]).astype(LOW)
        first_head = iota((1, TILE), 1) < HEAD_SIZE
        lane = iota((TILE, TILE), 1)

        def step(j, carry):
            def body(size, begin):
                span = size * TILE
                here = pl.ds(pl.multiple_of(j * TILE, TILE), TILE)
                keys = pl.ds(pl.multiple_of(begin * TILE, TILE), span)
                row = j * TILE + iota((TILE, 1), 0)
                row = jnp.concatenate([row, row], axis=0)
                place = begin * TILE + iota((2 * TILE, span), 1)
                inside = (place >= start_of(row, ends)) & (place < finish_of(row, ends, rows))
                logs = jnp.zeros((TILE, TILE), F32)
                for pair in range(part // TILE):
                    cols = pl.ds(pair * TILE, TILE)
                    queries = q_ref[here, cols] * jnp.asarray(0.125, LOW)
                    none = jnp.zeros_like(queries)
                    queries = jnp.concatenate(
                        [jnp.where(first_head, queries, none), jnp.where(first_head, none, queries)], axis=0
                    )
                    score = jnp.where(inside, dot(queries, k_ref[keys, cols], (1, 1)), NEGATIVE)
                    top = jnp.max(score, axis=1, keepdims=True)
                    expo = jnp.exp(score - top)
                    total = jnp.sum(expo, axis=1, keepdims=True)
                    mixed = dot(expo.astype(LOW), v_ref[keys, cols], (1, 0)) * (1.0 / total)
                    log = top + jnp.log(total)
                    logs = jnp.where(lane == 2 * pair, log[0:TILE], logs)
                    logs = jnp.where(lane == 2 * pair + 1, log[TILE:], logs)
                    o_ref[here, cols] = jnp.where(first_head, mixed[0:TILE], mixed[TILE:]).astype(LOW)
                lse_ref[:, here] = jnp.transpose(logs)[0:8, :]

            first, last = tile_window(j, ends, rows)
            for_window(first, last, tiles, body)
            return carry

        lax.fori_loop(0, tiles, step, 0)
        share_ref[...] = dot(o_ref[...], p_w[...], (1, 1)).astype(LOW)

    return call(
        kernel,
        "decoder_attend",
        [
            ((rows, model), F32), ((rows, model), LOW), ((rows, part), LOW), ((rows, part), LOW), ((rows, part), LOW),
            ((rows, part), LOW), ((8, rows), F32), ((rows, model), LOW),
        ],
        [home, own, far],
        [
            corrupt, corrupt_far, encoded, encoded_far, query, key, value, query_bias, value_bias, project,
        ],
        after,
        [pltpu.VMEM((3 * kept, model), LOW)],
    )


def decoder_norm(d_in, share, far, project_bias, gain, shift, after):
    rows, model = d_in.shape

    def kernel(x_ref, s_ref, f_ref, pb, g1, b1, unit_ref, scale_ref, low_ref):
        def part(here, begin):
            attended = s_ref[here, :].astype(F32) + f_ref[here, :].astype(F32)
            unit, scale = norm(x_ref[here, :] + attended + pb[...])
            unit_ref[here, :] = unit
            scale_ref[here, :] = scale
            low_ref[here, :] = (unit * g1[...] + b1[...]).astype(LOW)

        over_rows(unit_ref.shape[0], CHUNK, part)

    return call(
        kernel,
        "decoder_norm",
        [((rows, model), F32), ((rows, 1), F32), ((rows, model), LOW)],
        [],
        [d_in, share, far, project_bias, gain, shift],
        after,
        steps=rows // STEP,
        axes=by_rows(rows),
    )


def decoder_hidden(first_low, inner, inner_bias, after):
    rows, model = first_low.shape
    hidden = inner.shape[1]
    block = 256

    def kernel(low_ref, in_w, in_b, act_ref, slope_ref, pre_ref):
        pre_ref[...] = dot(low_ref[...], in_w[...], (1, 0))

        def activate(here, begin):
            act, slope = gelu_and_slope(pre_ref[here, :] + in_b[...])
            act_ref[here, :] = act.astype(LOW)
            slope_ref[here, :] = slope.astype(LOW)

        over_rows(rows, 128, activate)

    return call(
        kernel,
        "decoder_hidden",
        [((rows, hidden), LOW), ((rows, hidden), LOW)],
        [],
        [first_low, inner, inner_bias[None]],
        after,
        [pltpu.VMEM((rows, block), F32)],
        steps=hidden // block,
        axes=lambda shape: 1 if shape[-1] == hidden else None,
    )


def weight_grads(name, left, right, base, after=()):
    rows, model = left.shape
    width = right.shape[1]
    block = WIDE
    steps = width // block
    first = steps if base is None else 0

    def kernel(l_ref, r_ref, *refs):
        refs[-1][...] = dot(l_ref[...], r_ref[...], (0, 0)).astype(LOW)

    return pl.pallas_call(
        kernel,
        out_shape=jax.ShapeDtypeStruct((model, 2 * width), LOW),
        grid=(steps,),
        in_specs=[pl.BlockSpec((rows, model), lambda i: (0, 0)), pl.BlockSpec((rows, block), lambda i: (0, i))]
        + [pl.BlockSpec(memory_space=pl.ANY)] * ((base is not None) + len(after)),
        out_specs=pl.BlockSpec((model, block), lambda i: (0, i + first)),
        input_output_aliases={} if base is None else {2: 0},
        compiler_params=pltpu.CompilerParams(vmem_limit_bytes=VMEM_LIMIT),
        cost_estimate=pl.CostEstimate(flops=0, bytes_accessed=0, transcendentals=0),
        name=name,
    )(left, right, *([] if base is None else [base]), *after)


def decoder_norm_back(home, own, far_lengths, unit1, share, far, first_gain, first_shift, outer_bias, gain, shift, cot, cot_far, after):
    rows, model = unit1.shape
    steps = rows // STEP

    def kernel(
        home_ref, own_ref, farl_ref, u_ref, s_ref, f_ref, g1, b1, ob, g2, b2, c_ref, cf_ref,
        out_ref, grad_ref, low_ref, sums_ref, acc_ref,
    ):
        ends = ends_of(home_ref, own_ref, farl_ref)
        at_home = home_ref[0] == 1
        height = u_ref.shape[0]

        @pl.when(first_step())
        def _():
            acc_ref[...] = jnp.zeros_like(acc_ref)

        def part(here, begin):
            fed = s_ref[here, :].astype(F32) + f_ref[here, :].astype(F32)
            first = u_ref[here, :] * g1[...] + b1[...]
            unit, scale = norm(first + fed + ob[...])
            valid = (pl.program_id(0) * height + begin + iota((CHUNK, 1), 0) < ends[-1]).astype(F32)
            out_ref[here, :] = ((unit * g2[...] + b2[...]) * valid).astype(LOW)
            cot = jnp.where(at_home, c_ref[here, :].astype(F32), cf_ref[here, :].astype(F32)) * valid
            grad = norm_back(cot, unit, scale, g2[...])
            grad_ref[here, :] = grad
            low_ref[here, :] = grad.astype(LOW)
            acc_ref[0:8, :] += eights(grad)
            acc_ref[8:16, :] += eights(cot * unit)
            acc_ref[16:24, :] += eights(cot)

        over_rows(height, CHUNK, part)

        @pl.when(last_step())
        def _():
            for i in range(3):
                sums_ref[i : i + 1, :] = jnp.sum(acc_ref[8 * i : 8 * i + 8, :], axis=0, keepdims=True)

    return call(
        kernel,
        "decoder_norm_back",
        [((rows, model), LOW), ((rows, model), F32), ((rows, model), LOW), ((3, model), F32)],
        [home, own, far_lengths],
        [
            unit1, share, far, first_gain, first_shift, outer_bias, gain, shift, cot,
            cot_far,
        ],
        after,
        [pltpu.VMEM((24, model), F32)],
        steps=steps,
        axes=by_rows(rows),
    )


def decoder_feed_back(fed_low, outer, slope, after):
    rows, model = fed_low.shape
    hidden = outer.shape[1]
    block = 256

    def kernel(low_ref, out_w, slope_ref, pre_ref, bias_ref, wide_ref, bias_acc):
        wide_ref[...] = dot(low_ref[...], out_w[...], (1, 0))
        bias_acc[...] = jnp.zeros_like(bias_acc)

        def slopes(here, begin):
            pre = (wide_ref[here, :] * slope_ref[here, :].astype(F32)).astype(LOW)
            pre_ref[here, :] = pre
            bias_acc[...] += eights(pre.astype(F32))

        over_rows(rows, 128, slopes)
        bias_ref[...] = jnp.sum(bias_acc[...], axis=0, keepdims=True)

    return call(
        kernel,
        "decoder_feed_back",
        [((rows, hidden), LOW), ((1, hidden), F32)],
        [],
        [fed_low, outer, slope],
        after,
        [pltpu.VMEM((rows, block), F32), pltpu.VMEM((8, block), F32)],
        steps=hidden // block,
        axes=lambda shape: 1 if shape[-1] == hidden else None,
    )


def decoder_first_back(second, share, far, unit, scale, gain, after):
    rows, model = second.shape

    def kernel(s_grad, s_ref, f_ref, u_ref, r_ref, g1, grad_ref, low_ref, sums_ref, acc_ref):
        @pl.when(first_step())
        def _():
            acc_ref[...] = jnp.zeros_like(acc_ref)

        def part(here, begin):
            unit = u_ref[here, :]
            first_grad = s_grad[here, :] + (s_ref[here, :].astype(F32) + f_ref[here, :].astype(F32))
            grad = norm_back(first_grad, unit, r_ref[here, :], g1[...])
            grad_ref[here, :] = grad
            low_ref[here, :] = grad.astype(LOW)
            acc_ref[0:8, :] += eights(grad)
            acc_ref[8:16, :] += eights(first_grad * unit)
            acc_ref[16:24, :] += eights(first_grad)

        over_rows(u_ref.shape[0], CHUNK, part)

        @pl.when(last_step())
        def _():
            for i in range(3):
                sums_ref[i : i + 1, :] = jnp.sum(acc_ref[8 * i : 8 * i + 8, :], axis=0, keepdims=True)

    return call(
        kernel,
        "decoder_first_back",
        [((rows, model), F32), ((rows, model), LOW), ((3, model), F32)],
        [],
        [second, share, far, unit, scale, gain],
        after,
        [pltpu.VMEM((24, model), F32)],
        steps=rows // STEP,
        axes=by_rows(rows),
    )


def decoder_attend_back(home, own, far_lengths, low, project, lse, query, key, value, query_w, key_w, value_w, after):
    rows, model = low.shape
    part = query.shape[1]
    tiles = rows // TILE

    def kernel(
        home_ref, own_ref, farl_ref, low_ref, p_w, lse_ref, q_ref, k_ref, v_ref, q_w, k_w, v_w,
        all_ref, share_ref, sums_ref, g_ref, kt_ref, dk_sum, dv_sum, acc_ref,
    ):
        ends = ends_of(home_ref, own_ref, farl_ref)
        g_ref[...] = dot(low_ref[...], p_w[...], (1, 0)).astype(LOW)
        first_head = iota((1, TILE), 1) < HEAD_SIZE
        dk_sum[...] = jnp.zeros_like(dk_sum)
        dv_sum[...] = jnp.zeros_like(dv_sum)
        acc_ref[...] = jnp.zeros_like(acc_ref)

        def turn(here, begin):
            for pair in range(part // TILE):
                cols = pl.ds(pair * TILE, TILE)
                kt_ref[cols, here] = jnp.transpose(k_ref[here, cols].astype(F32)).astype(LOW)

        over_rows(rows, TILE, turn)

        def step(j, carry):
            def body(size, begin):
                span = size * TILE
                here = pl.ds(pl.multiple_of(j * TILE, TILE), TILE)
                keys = pl.ds(pl.multiple_of(begin * TILE, TILE), span)
                column = j * TILE + iota((1, TILE), 1)
                column = jnp.concatenate([column, column], axis=1)
                place = begin * TILE + iota((span, 2 * TILE), 0)
                inside = (place >= start_of(column, ends)) & (place < finish_of(column, ends, rows))
                for pair in range(part // TILE):
                    cols = pl.ds(pair * TILE, TILE)
                    queries = q_ref[here, cols] * jnp.asarray(0.125, LOW)
                    grads = g_ref[here, cols]
                    none = jnp.zeros_like(queries)
                    queries = jnp.concatenate(
                        [jnp.where(first_head, queries, none), jnp.where(first_head, none, queries)], axis=0
                    )
                    grads = jnp.concatenate(
                        [jnp.where(first_head, grads, none), jnp.where(first_head, none, grads)], axis=0
                    )
                    log = jnp.concatenate(
                        [lse_ref[2 * pair : 2 * pair + 1, here], lse_ref[2 * pair + 1 : 2 * pair + 2, here]], axis=1
                    )
                    score = dot(k_ref[keys, cols], queries, (1, 1))
                    weight = jnp.exp(jnp.where(inside, score, NEGATIVE) - log)
                    weight_grad = dot(v_ref[keys, cols], grads, (1, 1))
                    middle = jnp.sum(weight * weight_grad, axis=0, keepdims=True)
                    score_grad = (weight * (weight_grad - middle)).astype(LOW)
                    q_grad = dot(kt_ref[cols, keys], score_grad, (1, 0)) * 0.125
                    q_grad = jnp.concatenate([q_grad[0:HEAD_SIZE, 0:TILE], q_grad[HEAD_SIZE:, TILE:]], axis=0)
                    all_ref[here, cols] = jnp.transpose(q_grad).astype(LOW)
                    dk_sum[keys, cols] += dot(score_grad, queries, (1, 0))
                    dv_sum[keys, cols] += dot(weight.astype(LOW), grads, (1, 0))

            first, last = tile_window(j, ends, rows)
            for_window(first, last, tiles, body)
            return carry

        lax.fori_loop(0, tiles, step, 0)

        def close(here, begin):
            all_ref[here, part : 2 * part] = dk_sum[here, :].astype(LOW)
            value_grad = dv_sum[here, :].astype(LOW)
            all_ref[here, 2 * part :] = value_grad
            acc_ref[:, 0:part] += eights(all_ref[here, 0:part].astype(F32))
            acc_ref[:, part:] += eights(value_grad.astype(F32))

        over_rows(rows, TILE, close)
        sums_ref[...] = jnp.sum(acc_ref[...], axis=0, keepdims=True)
        share = dot(all_ref[:, 0:part], q_w[...], (1, 1)) + dot(all_ref[:, part : 2 * part], k_w[...], (1, 1))
        share_ref[...] = (share + dot(all_ref[:, 2 * part :], v_w[...], (1, 1))).astype(LOW)

    return call(
        kernel,
        "decoder_attend_back",
        [((rows, 3 * part), LOW), ((rows, model), LOW), ((1, 2 * part), F32)],
        [home, own, far_lengths],
        [low, project, lse, query, key, value, query_w, key_w, value_w],
        after,
        [
            pltpu.VMEM((rows, part), LOW), pltpu.VMEM((part, rows), LOW), pltpu.VMEM((rows, part), F32),
            pltpu.VMEM((rows, part), F32), pltpu.VMEM((8, 2 * part), F32),
        ],
    )


def attend_weight_grads(d_low, grads, attended_low, mixed, after):
    rows, model = d_low.shape
    part = mixed.shape[1]

    def kernel(x_ref, g_ref, a_ref, o_ref, first_ref, last_ref):
        first_ref[...] = dot(x_ref[...], g_ref[:, 0 : 2 * part], (0, 0)).astype(LOW)
        last_ref[:, 0:part] = dot(x_ref[...], g_ref[:, 2 * part :], (0, 0)).astype(LOW)
        last_ref[:, part:] = dot(a_ref[...], o_ref[...], (0, 0)).astype(LOW)

    return call(
        kernel, "attend_weight_grads", [((model, 2 * part), LOW)] * 2, [], [d_low, grads, attended_low, mixed], after
    )


def pack_vectors(blocks, after):
    model = blocks[0][-1].shape[1]
    part = model // 2
    height = -(-9 * len(blocks) // 8) * 8

    def kernel(*refs):
        out = refs[-1]
        out[...] = jnp.zeros_like(out)
        for i in range(len(blocks)):
            query, value, inner, first, second = refs[5 * i : 5 * i + 5]
            row = 9 * i
            out[row : row + 1, 0:part] = query[...]
            out[row : row + 1, part:] = value[...]
            out[row + 1 : row + 2, :] = inner[:, 0:model]
            out[row + 2 : row + 3, :] = inner[:, model:]
            out[row + 3 : row + 6, :] = first[...]
            out[row + 6 : row + 9, :] = second[...]

    arrays = [array for block in blocks for array in block]
    return call(kernel, "pack_vectors", [((height, model), F32)], [], arrays, after)[0]


def decoder_end(home, own, far_lengths, grad, share, far, kept, after):
    rows, model = grad.shape
    chunk = 256

    def kernel(home_ref, own_ref, farl_ref, g_ref, s_ref, f_ref, low_ref, total_ref):
        ends = ends_of(home_ref, own_ref, farl_ref)

        @pl.when(first_step())
        def _():
            total_ref[...] = jnp.zeros_like(total_ref)

        d_in = g_ref[...] + (s_ref[...].astype(F32) + f_ref[...].astype(F32))
        low_ref[...] = d_in.astype(LOW)
        member = iota((kept, chunk), 0) == segment_of(pl.program_id(0) * chunk + iota((kept, chunk), 1), ends)
        member = member.astype(F32).astype(LOW)
        total_ref[...] += sum(dot(member, piece, (1, 0)) for piece in split_low(d_in))

    return call(
        kernel,
        "decoder_end",
        [((rows, model), LOW), ((kept, model), F32)],
        [home, own, far_lengths],
        [grad, share, far],
        after,
        steps=rows // chunk,
        axes=by_rows(rows),
    )


class Links:
    def __init__(self, mesh):
        self.dp = mesh.shape["dp"]
        self.parts = mesh.shape["tensor"]
        self.bits = (self.dp // 2).bit_length() - 1
        self.core = lax.axis_index("dp") & 1
        self.group = lax.axis_index("dp") >> 1
        self.chip = lax.axis_index("tensor")
        self.home = self.core == self.chip

    def move(self, value, target):
        pairs = []
        for i in range(self.dp):
            for t in range(self.parts):
                place = target(i, t)
                if place is not None:
                    pairs.append((i * self.parts + t, place[0] * self.parts + place[1]))
        return lax.ppermute(value, AXES, pairs)

    def swap_core(self, value):
        return self.move(value, lambda i, t: (i ^ 1, t))

    def swap_tensor(self, value):
        return self.move(value, lambda i, t: (i, t ^ 1))

    def swap_group(self, value, bit):
        return self.move(value, lambda i, t: (i ^ (2 << bit), t))

    def turn(self, value):
        moved = self.move(value, lambda i, t: None if (i & 1) == t else (i ^ 1, t ^ 1))
        return jnp.where(self.home, value, moved)

    def of_chip(self, value):
        return jnp.where(self.home, value, self.swap_core(value))

    def pick(self, value, axis, bit):
        return lax.dynamic_slice_in_dim(value, bit, 1, axis)

    def last_halving(self, value):
        view = value.reshape(2, -1, value.shape[1])
        sent = self.swap_tensor(self.pick(view, 0, 1 - self.chip).astype(LOW))
        return (self.pick(view, 0, self.chip).astype(F32) + sent.astype(F32))[0]

    def copies(self, value, lanes):
        rows = value.shape[0]
        value = value.reshape(rows, -1, lanes).transpose(1, 0, 2).reshape(-1, lanes)
        return jnp.broadcast_to(value[None], (self.dp,) + value.shape)

    def rows_of(self, value, rows):
        lanes = value.shape[2]
        return value.reshape(self.dp, -1, rows, lanes).transpose(0, 2, 1, 3).reshape(self.dp, rows, -1)

    def scatter_groups(self, value):
        cores = [[2 * g + c for g in range(self.dp // 2)] for c in range(2)]
        return lax.psum_scatter(value, "dp", scatter_dimension=0, axis_index_groups=cores, tiled=True)


class Held:
    def __init__(self, view):
        self.held = view


class Total:
    def __init__(self, links, value):
        self.links, self.held, self.done = links, value, 0

    def step(self):
        self.held = self.held + self.links.swap_group(self.held, self.done)
        self.done += 1

    def finish(self):
        while self.done < self.links.bits:
            self.step()
        return self.held


class Halving:
    def __init__(self, links, grad, order):
        self.links, self.order = links, list(order)
        self.width = grad.shape[1]
        self.parts = [(grad.reshape((2,) * links.bits + (2, -1, self.width)), {})]

    @property
    def held(self):
        return self.parts[-1][0]

    @held.setter
    def held(self, value):
        self.parts[-1] = (value, self.parts[-1][1])

    def cut(self, axis=None, bit=None):
        total = 0
        for view, own in self.parts:
            at = own if axis is None else {**own, axis: bit}
            starts = [at.get(d, 0) if view.shape[d] > 1 else 0 for d in range(view.ndim)]
            sizes = [1 if d in at else view.shape[d] for d in range(view.ndim)]
            total = total + lax.dynamic_slice(view, starts, sizes).astype(F32)
        return total

    def step(self):
        links, step = self.links, self.order.pop(0)
        if step < 0:
            axis, mine, swap = links.bits, links.chip, links.swap_tensor
        else:
            axis, mine = links.bits - 1 - step, (links.group >> step) & 1
            swap = lambda value: links.swap_group(value, step)
        sent = swap(self.cut(axis, 1 - mine).astype(LOW))
        self.parts = [(view, {**own, axis: mine}) for view, own in self.parts] + [(sent, {})]

    def left(self):
        while self.order:
            self.step()
        return self.cut().reshape(-1, self.width)


def local(mesh, passages, corrupted, lengths, cotangent, *weights):
    (
        e_query, e_key, e_value, e_project, e_query_bias, e_value_bias, e_project_bias, e_first_gain, e_first_shift,
        e_inner, e_inner_bias, e_outer, e_outer_bias, e_second_gain, e_second_shift,
    ) = weights[:15]
    (
        d_query, d_key, d_value, d_project, d_query_bias, d_value_bias, d_project_bias, d_first_gain, d_first_shift,
        d_inner, d_inner_bias, d_outer, d_outer_bias, d_second_gain, d_second_shift,
    ) = weights[15:]
    links = Links(mesh)
    rows, model = passages.shape
    part = e_query.shape[1]
    hidden = e_inner.shape[1]
    heads = part // HEAD_SIZE
    home = links.home.astype(jnp.int32)[None]

    chip = links.chip.astype(jnp.int32)[None]
    deep = model // links.dp

    d_query = links.turn(d_query)
    d_key = links.turn(d_key)
    d_halves = jnp.concatenate([d_query_bias, d_value_bias, d_inner_bias])
    lengths_far = links.swap_core(lengths)
    corrupted_far = links.swap_core(corrupted)

    x_low, e_q, q_keys, e_weights, weight_x, e_mixed, share = encoder_attend(
        lengths, passages, e_query, e_key, e_value, e_project, e_query_bias, e_value_bias
    )
    kept = x_low.shape[0]
    inner_held, outer_held = [Held(weight) for weight in copied([d_inner, d_outer], (share,))]
    share_far = links.swap_tensor(share)
    d_value = links.turn(d_value)
    d_project = links.turn(d_project)
    d_halves = links.turn(d_halves)
    e_unit1, e_scale1, e_first, left_forward, e_act, e_slope, share = encoder_feed(
        x_low, share, share_far, e_project_bias, e_first_gain, e_first_shift, e_inner, e_inner_bias,
        e_outer, weight_x, (d_query, d_key, d_value, d_project, d_halves, lengths_far),
    )
    e_unit2, e_scale2, encoded = encoder_end(
        e_first, share, links.swap_tensor(share), e_outer_bias, e_second_gain, e_second_shift,
        (corrupted_far, inner_held, outer_held),
    )
    d_query_bias, d_value_bias, d_inner_bias = d_halves[:part], d_halves[part : 2 * part], d_halves[2 * part :]
    left_forward = lax.all_gather(left_forward, "dp")
    right_forward = lax.all_gather(jnp.concatenate([e_act, e_mixed, e_q], axis=1), "dp")

    encoded_far = links.swap_core(encoded)
    d_inner = links.turn(inner_held.held)
    d_outer = links.turn(outer_held.held)
    d_in, d_low, query, key, value, mixed, lse, share = decoder_attend(
        home, lengths, lengths_far, corrupted, corrupted_far, encoded, encoded_far, d_query, d_key,
        d_value, d_query_bias, d_value_bias, d_project, (),
    )
    cotangent_far = links.swap_core(cotangent)
    unit1, scale1, first_low = decoder_norm(
        d_in, share, links.swap_core(share), d_project_bias, d_first_gain, d_first_shift, ()
    )
    act, slope = decoder_hidden(first_low, d_inner, d_inner_bias, ())
    share = dot(act, d_outer, (1, 1)).astype(LOW)

    decoded, second_grad, fed_low, second_sums = decoder_norm_back(
        home, lengths, lengths_far, unit1, share, links.swap_core(share), d_first_gain, d_first_shift, d_outer_bias,
        d_second_gain, d_second_shift, cotangent, cotangent_far, (),
    )
    decoded = links.turn(decoded)
    outer_grad = weight_grads("outer_grad", fed_low, act, None)
    pre_grad, inner_bias_grad = decoder_feed_back(fed_low, d_outer, slope, (outer_grad,))
    share = dot(pre_grad, d_inner, (1, 1)).astype(LOW)
    share_far = links.swap_core(share)
    feed_grads = weight_grads("inner_grad", first_low, pre_grad, outer_grad)
    first_grad, attended_low, first_sums = decoder_first_back(
        second_grad, share, share_far, unit1, scale1, d_first_gain, (feed_grads,)
    )
    feed_grads = links.scatter_groups(feed_grads)
    attend_grads, share, attend_sums = decoder_attend_back(
        home, lengths, lengths_far, attended_low, d_project, lse, query, key, value, d_query, d_key, d_value,
        (),
    )
    share_far = links.swap_core(share)
    attend_held = Held(attend_grads)
    corrupted_low, totals = decoder_end(
        home, lengths, lengths_far, first_grad, share, share_far, kept, (attend_held, decoded)
    )
    totals = links.turn(totals)
    attend_grads = attend_weight_grads(d_low, attend_held.held, attended_low, mixed, ())
    across = list(range(links.bits))
    pairs = [
        Halving(links, attend_grads[0], [-1] + across),
        Halving(links, attend_grads[1], [-1] + across[1:2] + across[:1] + across[2:]),
    ]
    corrupted_low = Held(corrupted_low)

    e_second_grad, e_fed_low, e_pre_grad, e_second_sums, e_inner_bias_grad, share = encoder_feed_back(
        totals, e_unit2, e_scale2, e_second_gain, e_outer, e_slope, e_inner, (*pairs,)
    )
    share_far = links.swap_tensor(share)
    (
        e_first_grad, e_first_sums, right_back, left_back, e_query_sum, e_value_sum, coefs, carried,
    ) = encoder_attend_back(
        lengths, e_second_grad, share, share_far, e_unit1, e_scale1, e_first_gain, e_project, e_query,
        e_key, e_value, e_value_bias, passages, e_weights, q_keys, e_fed_low, e_pre_grad, (left_forward, right_forward, *pairs),
    )
    vectors = pack_vectors([
        (e_query_sum, e_value_sum, e_inner_bias_grad, e_first_sums, e_second_sums),
        (attend_sums[:, :part], attend_sums[:, part:], inner_bias_grad, first_sums, second_sums),
    ], ())
    mine = jnp.arange(vectors.shape[0])[:, None] < 9
    vectors = Total(links, vectors + jnp.where(mine, links.swap_core(vectors), links.swap_tensor(vectors)))
    for pair in pairs:
        pair.step()
    coefs = coefs.astype(LOW)
    coefs_far = links.swap_tensor(coefs)
    carried_far = links.swap_tensor(carried)
    left_back = left_back.reshape(links.dp, deep, -1)
    both = jnp.concatenate([left_back, links.copies(right_back, left_back.shape[2])], axis=1)
    both = lax.all_to_all(both, "dp", 0, 0, tiled=True)
    passages_grad = passages_back(
        chip, lengths, coefs, coefs_far, carried, carried_far, e_first_grad, (corrupted_low, vectors),
    )
    corrupted_grad = links.turn(corrupted_low.held).astype(F32)
    d_grads = jnp.concatenate([links.last_halving(feed_grads)] + [pair.left() for pair in pairs], axis=1)
    d_grads = links.turn(d_grads.astype(LOW)).astype(F32)
    edges = [0, hidden, 2 * hidden, 2 * hidden + part, 2 * hidden + 2 * part, 2 * hidden + 3 * part, d_grads.shape[1]]
    d_grads = [d_grads[:, low:high] for low, high in zip(edges, edges[1:])]
    d_grads = d_grads[2:] + d_grads[:2]
    vectors = vectors.finish()

    def cut_vectors(rows):
        return [rows[0, :part], rows[0, part:], rows[1:3].reshape(-1)] + [rows[i] for i in range(3, 9)]

    e_vectors = cut_vectors(vectors[:9])
    d_vectors = vectors[9:18]
    d_vectors = cut_vectors(jnp.concatenate([links.of_chip(d_vectors[:3]), d_vectors[3:]], axis=0))

    left_back, right_back = both[:, :deep], links.rows_of(both[:, deep:], kept)
    left_forward = lax.dynamic_slice_in_dim(left_forward, lax.axis_index("dp") * deep, deep, 1)

    def product(left, right):
        return lax.dot_general(left, right, (((0, 2), (0, 1)), ((), ())), preferred_element_type=F32)

    e_outer_grad = product(left_back[:, :, :kept], right_forward[:, :, :hidden])
    e_inner_grad = product(left_forward[:, :, kept : 2 * kept], right_back[:, :, 2 * part :])
    e_project_grad = product(left_back[:, :, kept : 2 * kept], right_forward[:, :, hidden : hidden + part])
    e_query_grad = product(left_forward[:, :, :kept], right_back[:, :, :part])
    head_of = jnp.arange(part, dtype=jnp.int32) // HEAD_SIZE

    def by_head(values):
        mine = jnp.arange(heads, dtype=jnp.int32)[None, :, None, None] == head_of[None, None, None, :]
        return jnp.where(mine, values[:, None], jnp.zeros((), LOW)).reshape(links.dp, heads * kept, part)

    e_key_grad = product(left_back[:, :, 2 * kept :], by_head(right_forward[:, :, hidden + part :])) * 0.125
    e_value_grad = product(left_forward[:, :, 2 * kept :], by_head(right_back[:, :, part : 2 * part]))

    def ordered(matrices, small):
        query_g, key_g, value_g, project_g, inner_g, outer_g = matrices
        query_b, value_b, inner_b, project_b, gain1, shift1, outer_b, gain2, shift2 = small
        return (
            query_g, key_g, value_g, project_g, query_b, value_b, project_b, gain1, shift1,
            inner_g, inner_b, outer_g, outer_b, gain2, shift2,
        )

    return (
        (decoded, passages_grad, corrupted_grad)
        + ordered((e_query_grad, e_key_grad, e_value_grad, e_project_grad, e_inner_grad, e_outer_grad), e_vectors)
        + ordered(d_grads, d_vectors)
    )


def solution(mesh):
    rows = P("dp", None)
    columns, half, whole = P(None, "tensor"), P("tensor"), P()
    block_in = (columns,) * 4 + (half, half, whole, whole, whole, columns, half, columns, whole, whole, whole)
    split = P("dp", "tensor")
    block_out = (split,) * 4 + (half, half, whole, whole, whole, split, half, split, whole, whole, whole)
    return jax.shard_map(
        functools.partial(local, mesh),
        mesh=mesh,
        in_specs=(rows,) * 4 + block_in * 2,
        out_specs=(rows,) * 3 + block_out * 2,
        check_vma=False,
    )
```
